256 devices in a mesh: frames: 32 (over x, z), edges: 8 (over y, core).
Axes of the slice: x: 4, y: 4, z: 8, core: 2. Of those that a mesh axis runs over, the one named last changes fastest.
Arguments:
- fmap: bfloat16 [32, 3072, 128], P('frames'), may hold values from -6 to 6
- context: bfloat16 [32, 3072, 256], P('frames'), may hold values from -6 to 6
- poses: float32 [6, 32], P(None, 'frames'), may hold values from -0.05 to 0.05
- inv_depth: float32 [32, 3072], P('frames'), may hold values from 0.2 to 1
- targets: int32 [256], P(('frames', 'edges')), may hold values from 0 to 31, as said below
- w_corr: bfloat16 [196, 128], replicated, may hold values from -0.4375 to 0.4375
- w_gates: bfloat16 [3, 3, 256, 256], replicated, may hold values from -0.125 to 0.125
- w_cand: bfloat16 [3, 3, 256, 128], replicated, may hold values from -0.125 to 0.125
- w_head: bfloat16 [128, 4], replicated, may hold values from -0.5 to 0.5
Outputs:
- new_poses: float32 [6, 32], P(None, 'frames')
- new_depth: float32 [32, 3072], P('frames')
- hidden: bfloat16 [256, 3072, 128], P(('frames', 'edges'))
The draws below stay inside these ranges and needn't reach their ends.
Inputs may be any that keep to these rules, and one draw needn't show every extreme that they name: `targets`: every edge held by the devices of frames index f has source keyframe f and a target keyframe other than f.
All inputs are finite; a program needn't handle non-finite values.
Results may differ from the reference program's by a relative error of at most 0.0048.
Values may be sent and summed in bfloat16 or wider, within the bound.
A program may use at most 128 MiB of HBM per device.

```python
import math
import jax
import jax.numpy as jnp
from jax import lax

HGT = 48
WID = 64
CH = 128
HID = 128
LEVELS = 4
RADIUS = 3
ITERS = 2
PIX = 3072
CORR = 196
NF = 32
GROUP_EDGES = 8
NE = 256


def draw_targets(key, part):
    offsets = jax.random.randint(key, (NE,), 1, NF)
    edge_rows = jnp.arange(NE)
    owner_frame = edge_rows // GROUP_EDGES
    offsets = jnp.where(edge_rows % GROUP_EDGES == 0, 1, offsets)
    return ((owner_frame + offsets) % NF).astype(jnp.int32)


def levels(own_key, shape, shards, smallest, high):
    def one(position, parts):
        draws = jax.random.uniform(jax.random.fold_in(jax.random.fold_in(own_key, 6), position), (parts,), jnp.float32, smallest / len(shards), high / len(shards))
        return jnp.repeat(jnp.exp(draws), shape[position] // parts).reshape((-1,) + (1,) * (len(shape) - position - 1))

    loudness = one(*shards[0])
    for cut in shards[1:]:
        loudness = loudness * one(*cut)
    return loudness


def normal_values(stream_key, dims, scale, bound, cuts=(), kind=jnp.bfloat16):
    values = scale * jax.random.normal(stream_key, dims, jnp.float32)
    if cuts:
        values = values * levels(stream_key, dims, cuts, -0.22, 0.18)
    return jnp.clip(values, -bound, bound).astype(kind)


def setup_inputs(seed: int = 0) -> dict:
    splits = jax.random.split(jax.random.key(seed), 10)
    fmap = normal_values(splits[0], (NF, PIX, CH), 1.0, 6.0, ((0, 32),))
    context = normal_values(splits[1], (NF, PIX, 2 * HID), 1.0, 6.0, ((0, 32),))
    poses = jnp.clip(jax.random.uniform(splits[2], (6, NF), jnp.float32, -0.05, 0.05) * levels(splits[2], (6, NF), ((1, 32),), -0.4, 0.0), -0.05, 0.05)
    inv_depth = jnp.clip(0.2 + 0.8 * jax.random.uniform(splits[3], (NF, PIX), jnp.float32) ** levels(splits[3], (NF, PIX), ((0, 32),), -0.2, 0.2), 0.2, 1.0)
    targets = draw_targets(jax.random.fold_in(splits[9], 71), 0)
    w_corr = normal_values(splits[5], (CORR, HID), CORR ** -0.5, 0.4375)
    w_gates = normal_values(splits[6], (3, 3, 2 * HID, 2 * HID), (18 * HID) ** -0.5, 0.125)
    w_cand = normal_values(splits[7], (3, 3, 2 * HID, HID), (18 * HID) ** -0.5, 0.125)
    w_head = normal_values(splits[8], (HID, 4), HID ** -0.5, 0.5)
    return dict(fmap=fmap, context=context, poses=poses, inv_depth=inv_depth, targets=targets, w_corr=w_corr, w_gates=w_gates, w_cand=w_cand, w_head=w_head)


focal = 50.0
pose_damping = 0.1
pose_floor = 1.0
depth_damping = 0.1
depth_floor = 1.0
highest = lax.Precision.HIGHEST

def pyramid_lookup(source, target):
    edge_count, hgt, wid, channels = target.shape
    span = 2 * RADIUS + 1
    offsets = jnp.arange(span) - RADIUS
    scale = 1.0 / math.sqrt(channels)
    source_wide = source.astype(jnp.float32)
    level_feat = target.astype(jnp.float32)
    collected = []
    for level_index in range(LEVELS):
        stride = 2 ** level_index
        if level_index > 0:
            shape_now = level_feat.shape
            level_feat = level_feat.reshape(edge_count, shape_now[1] // 2, 2, shape_now[2] // 2, 2, channels).mean(axis=(2, 4))
        coarse = level_feat.astype(jnp.bfloat16).astype(jnp.float32)
        coarse_cols = coarse.shape[2]
        padded = jnp.pad(coarse, ((0, 0), (RADIUS, RADIUS), (0, 0), (0, 0)))
        spread = jnp.repeat(padded, stride, axis=1)
        col_target = jnp.arange(wid)[:, None] // stride + offsets[None, :]
        picker = (col_target[:, None, :] == jnp.arange(coarse_cols)[None, :, None]).astype(jnp.float32)
        for row_shift in range(-RADIUS, RADIUS + 1):
            begin = (RADIUS + row_shift) * stride
            band = lax.slice_in_dim(spread, begin, begin + hgt, axis=1)
            volume = jnp.einsum('hwc,ehvc->ehwv', source_wide, band, precision=highest)
            collected.append(jnp.einsum('ehwv,wvk->ehwk', volume, picker, precision=highest) * scale)
    return jnp.concatenate(collected, axis=3)

def conv_same(inputs, kernel):
    return lax.conv_general_dilated(inputs.astype(jnp.float32), kernel.astype(jnp.float32), (1, 1), 'SAME', dimension_numbers=('NHWC', 'HWIO', 'NHWC'), precision=highest)

def recurrent_update(source, target, ctx, w_corr, w_gates, w_cand, w_head):
    edge_count, hgt, wid, channels = target.shape
    width = w_head.shape[0]
    corr = pyramid_lookup(source, target).astype(jnp.bfloat16)
    encoded = jax.nn.relu(jnp.dot(corr.reshape(-1, corr.shape[3]).astype(jnp.float32), w_corr.astype(jnp.float32), preferred_element_type=jnp.float32))
    net_state = jnp.tanh(ctx[:, :width].astype(jnp.float32)).astype(jnp.bfloat16)
    inject = jax.nn.relu(ctx[:, width:].astype(jnp.float32))
    motion = (encoded.reshape(edge_count, -1, width) + inject[None]).astype(jnp.bfloat16)
    motion_map = motion.reshape(edge_count, hgt, wid, width)
    state_map = jnp.broadcast_to(net_state[None], motion.shape).reshape(edge_count, hgt, wid, width)
    gates = conv_same(jnp.concatenate([state_map, motion_map], axis=3), w_gates)
    update_gate = jax.nn.sigmoid(gates[..., :width])
    reset_gate = jax.nn.sigmoid(gates[..., width:])
    reset_state = (reset_gate * state_map.astype(jnp.float32)).astype(jnp.bfloat16)
    candidate = jnp.tanh(conv_same(jnp.concatenate([reset_state, motion_map], axis=3), w_cand))
    new_state = ((1.0 - update_gate) * state_map.astype(jnp.float32) + update_gate * candidate).astype(jnp.bfloat16)
    heads = jnp.dot(new_state.reshape(-1, width).astype(jnp.float32), w_head.astype(jnp.float32), preferred_element_type=jnp.float32)
    heads = heads.reshape(edge_count, -1, 4).transpose(0, 2, 1)
    return (new_state.reshape(edge_count, -1, width), heads)

def edge_terms(relative, depth_rows, flow, confidence, hgt, wid):
    pixel_ids = jnp.arange(hgt * wid)
    col_pos = (pixel_ids % wid).astype(jnp.float32)
    row_pos = (pixel_ids // wid).astype(jnp.float32)
    center_x = (wid - 1) / 2.0
    center_y = (hgt - 1) / 2.0
    ray_x = (col_pos - center_x) / focal
    ray_y = (row_pos - center_y) / focal
    move_x, move_y, move_z, turn_x, turn_y, turn_z = [relative[index][:, None] for index in range(6)]
    point_x = ray_x + turn_y - turn_z * ray_y + depth_rows * move_x
    point_y = ray_y + turn_z * ray_x - turn_x + depth_rows * move_y
    point_z = 1.0 + turn_x * ray_y - turn_y * ray_x + depth_rows * move_z
    inverse_z = 1.0 / point_z
    slope = focal * inverse_z
    bend_u = -focal * point_x * inverse_z * inverse_z
    bend_v = -focal * point_y * inverse_z * inverse_z
    resid_u = col_pos + flow[:, 0] - (focal * point_x * inverse_z + center_x)
    resid_v = row_pos + flow[:, 1] - (focal * point_y * inverse_z + center_y)
    blank = jnp.zeros_like(slope)
    jac_u = jnp.stack([depth_rows * slope, blank, depth_rows * bend_u, bend_u * ray_y, slope - bend_u * ray_x, -slope * ray_y], axis=1)
    jac_v = jnp.stack([blank, depth_rows * slope, depth_rows * bend_v, bend_v * ray_y - slope, -bend_v * ray_x, slope * ray_x], axis=1)
    depth_u = slope * move_x + bend_u * move_z
    depth_v = slope * move_y + bend_v * move_z
    weight_u = confidence[:, 0]
    weight_v = confidence[:, 1]
    hess = jnp.einsum('ekp,elp->ekl', jac_u * weight_u[:, None], jac_u, precision=highest)
    hess = hess + jnp.einsum('ekp,elp->ekl', jac_v * weight_v[:, None], jac_v, precision=highest)
    grad = lax.optimization_barrier(jnp.sum(jac_u * (weight_u * resid_u)[:, None] + jac_v * (weight_v * resid_v)[:, None], axis=2))
    cross = jac_u * (weight_u * depth_u)[:, None] + jac_v * (weight_v * depth_v)[:, None]
    curve = weight_u * depth_u * depth_u + weight_v * depth_v * depth_v
    depth_grad = weight_u * depth_u * resid_u + weight_v * depth_v * resid_v
    return (hess, grad, cross, curve, depth_grad)

def place_edges(source_ids, target_ids, frames_total):
    frame_ids = jnp.arange(frames_total)
    sign = (target_ids[:, None] == frame_ids[None, :]).astype(jnp.float32) - (source_ids[:, None] == frame_ids[None, :]).astype(jnp.float32)
    eye_six = jnp.eye(6, dtype=jnp.float32)
    return (sign[:, None, :, None] * eye_six[None, :, None, :]).reshape(source_ids.shape[0], 6, frames_total * 6)

def solve_poses(system, rhs):
    sym = 0.5 * (system + system.T)
    damped = sym + jnp.diag(pose_damping * jnp.diagonal(sym) + pose_floor)
    factor = jnp.linalg.cholesky(damped)
    middle = lax.linalg.triangular_solve(factor, rhs[:, None], left_side=True, lower=True)
    return lax.linalg.triangular_solve(factor, middle, left_side=True, lower=True, transpose_a=True)[:, 0]

def reference(fmap, context, poses, inv_depth, targets, w_corr, w_gates, w_cand, w_head):
    frames_total, pixel_count, channels = fmap.shape
    edges_total = targets.shape[0]
    per_frame = edges_total // frames_total
    sources = (jnp.arange(edges_total) // per_frame).astype(jnp.int32)

    def one_edge(pair):
        source_id, target_id = pair
        source = fmap[source_id].reshape(HGT, WID, channels)
        target = fmap[target_id].reshape(1, HGT, WID, channels)
        return recurrent_update(source, target, context[source_id], w_corr, w_gates, w_cand, w_head)
    hidden, heads = lax.map(one_edge, (sources, targets))
    hidden = hidden.reshape(edges_total, pixel_count, -1)
    heads = heads.reshape(edges_total, 4, pixel_count)
    flow = heads[:, 0:2]
    confidence = jax.nn.sigmoid(heads[:, 2:4])
    placement = place_edges(sources, targets, frames_total)
    for step_index in range(ITERS):
        relative = jnp.take(poses, targets, axis=1) - jnp.take(poses, sources, axis=1)
        depth_rows = jnp.take(inv_depth, sources, axis=0)
        hess, grad, cross, curve, depth_grad = edge_terms(relative, depth_rows, flow, confidence, HGT, WID)
        system = jnp.einsum('ekm,ekl,eln->mn', placement, hess, placement, precision=highest)
        rhs = jnp.einsum('ekm,ek->m', placement, grad, precision=highest)
        curve_frame = curve.reshape(frames_total, per_frame, pixel_count).sum(axis=1)
        grad_frame = depth_grad.reshape(frames_total, per_frame, pixel_count).sum(axis=1)
        damped_curve = (1.0 + depth_damping) * curve_frame + depth_floor

        def coupling_of(index):
            rows_place = lax.dynamic_slice_in_dim(placement, index * per_frame, per_frame, 0)
            rows_cross = lax.dynamic_slice_in_dim(cross, index * per_frame, per_frame, 0)
            return jnp.einsum('ekm,ekp->mp', rows_place, rows_cross, precision=highest)

        def frame_schur(index):
            coupling = coupling_of(index)
            scaled = coupling / damped_curve[index][None, :]
            return (jnp.dot(scaled, coupling.T, precision=highest), jnp.dot(scaled, grad_frame[index], precision=highest))
        frame_index = jnp.arange(frames_total).astype(jnp.int32)
        schur_parts, rhs_parts = lax.map(frame_schur, frame_index)
        reduced = system - lax.optimization_barrier(jnp.sum(schur_parts, axis=0))
        reduced_rhs = rhs - lax.optimization_barrier(jnp.sum(rhs_parts, axis=0))
        step = solve_poses(reduced, reduced_rhs)
        along = lax.map(lambda index: jnp.dot(step, coupling_of(index), precision=highest), frame_index)
        poses = poses + step.reshape(frames_total, 6).T
        inv_depth = inv_depth + (grad_frame - along) / damped_curve
    return (poses, inv_depth, hidden)
```

```python
import functools
import math

import jax
import jax.numpy as jnp
from jax import lax
from jax.experimental import pallas as pl
from jax.experimental.pallas import tpu as pltpu
from jax.sharding import PartitionSpec as P

HGT = 48
WID = 64
CH = 128
LEVELS = 4
RADIUS = 3
ITERS = 2
PIX = HGT * WID
NF = 32
EDGES = 8
SLICE = PIX // EDGES
ROWS = SLICE // WID
UNK = 6 * NF

FOCAL = 50.0
POSE_DAMPING = 0.1
POSE_FLOOR = 1.0
DEPTH_DAMPING = 0.1
DEPTH_FLOOR = 1.0
HIGHEST = lax.Precision.HIGHEST
F32 = jnp.float32
BF16 = jnp.bfloat16
MESH = pl.DeviceIdType.MESH


def dot_nt(a, b, precision=None):
    return lax.dot_general(a, b, (((1,), (1,)), ((), ())), precision=precision, preferred_element_type=F32)


def corr_kernel(src_ref, tgt_ref, inj_ref, w_ref, out_ref, p0, p1, p2, p3, t1, f1, t2, f2, t3):
    zero = jnp.zeros((3 * WID, CH), BF16)
    p0[pl.ds(0, 192), :] = zero
    p0[pl.ds(51 * 64, 192), :] = zero
    p1[pl.ds(0, 96), :] = zero[:96]
    p1[pl.ds(27 * 32, 96), :] = zero[:96]
    p2[pl.ds(0, 48), :] = zero[:48]
    p2[pl.ds(15 * 16, 48), :] = zero[:48]
    p3[pl.ds(0, 24), :] = jnp.zeros((24, CH), F32)
    p3[pl.ds(9 * 8, 24), :] = jnp.zeros((24, CH), F32)

    p0[pl.ds(192, PIX), :] = tgt_ref[...]

    def fold_rows(r, carry):
        a = tgt_ref[pl.ds(r * 128, 64), :].astype(F32)
        b = tgt_ref[pl.ds(r * 128 + 64, 64), :].astype(F32)
        t1[pl.ds(r * 64, 64), :] = a + b
        return carry

    lax.fori_loop(0, HGT // 2, fold_rows, 0)
    f1[...] = 0.25 * (t1[pl.ds(0, 768, stride=2), :] + t1[pl.ds(1, 768, stride=2), :])
    p1[pl.ds(96, 768), :] = f1[...].astype(BF16)
    half = f1[...].reshape(12, 2, 32, CH)
    t2[...] = (half[:, 0] + half[:, 1]).reshape(384, CH)
    f2[...] = 0.25 * (t2[pl.ds(0, 192, stride=2), :] + t2[pl.ds(1, 192, stride=2), :])
    p2[pl.ds(48, 192), :] = f2[...].astype(BF16)
    half = f2[...].reshape(6, 2, 16, CH)
    t3[...] = (half[:, 0] + half[:, 1]).reshape(96, CH)
    f3 = 0.25 * (t3[pl.ds(0, 48, stride=2), :] + t3[pl.ds(1, 48, stride=2), :])
    p3[pl.ds(24, 48), :] = f3.astype(BF16).astype(F32)

    lane = lax.broadcasted_iota(jnp.int32, (8, 128), 1)
    sub = lax.broadcasted_iota(jnp.int32, (8, 128), 0)
    col = lane % WID
    scale = 1.0 / math.sqrt(CH)

    def rotate(x, level):
        amount = ((col >> level) + 5) % 8
        for bit in (1, 2, 4):
            x = jnp.where((amount // bit) % 2 == 1, pltpu.roll(x, 8 - bit, 0), x)
        return x

    def pick(vol, groups, level):
        acc = jnp.zeros((8, 128), F32)
        for g in range(groups):
            acc = jnp.where(jnp.abs(8 * g + sub - (col >> level)) <= RADIUS, vol[8 * g : 8 * g + 8], acc)
        return acc

    def block(q, carry):
        src = src_ref[pl.ds(q * 128, 128), :]
        parts = []
        vol = dot_nt(p0[pl.ds(q * 128, 512), :], src)
        rows = [pick(vol[64 * a : 64 * a + 64], 8, 0) for a in range(8)]
        for a in range(7):
            parts.append(rotate(jnp.where(lane < WID, rows[a], rows[a + 1]), 0))
        vol = dot_nt(p1[pl.ds(q * 32, 224), :], src)
        for a in range(7):
            parts.append(rotate(pick(vol[32 * a : 32 * a + 32], 4, 1), 1))
        vol = dot_nt(p2[pl.ds((q // 2) * 16, 112), :], src)
        for a in range(7):
            parts.append(rotate(pick(vol[16 * a : 16 * a + 16], 2, 2), 2))
        vol = dot_nt(p3[pl.ds((q // 4) * 8, 56), :].astype(BF16), src)
        for a in range(7):
            parts.append(rotate(pick(vol[8 * a : 8 * a + 8], 1, 3), 3))
        corr = (jnp.concatenate(parts, axis=0) * scale).astype(BF16)
        enc = lax.dot_general(corr, w_ref[...], (((0,), (0,)), ((), ())), preferred_element_type=F32)
        inj = jnp.maximum(inj_ref[pl.ds(q * 128, 128), :].astype(F32), 0.0)
        out_ref[pl.ds(q * 128, 128), :] = (jnp.maximum(enc, 0.0) + inj).astype(BF16)
        return carry

    lax.fori_loop(0, PIX // 128, block, 0, unroll=2)


def encode(source, target, inject, w_corr):
    w_slots = jnp.pad(w_corr.reshape(28, 7, CH), ((0, 0), (0, 1), (0, 0))).reshape(224, CH)
    vmem = pl.BlockSpec(memory_space=pltpu.VMEM)
    return pl.pallas_call(
        corr_kernel,
        out_shape=jax.ShapeDtypeStruct((PIX, CH), BF16),
        in_specs=[vmem] * 4,
        out_specs=vmem,
        scratch_shapes=[
            pltpu.VMEM((54 * 64, CH), BF16),
            pltpu.VMEM((30 * 32, CH), BF16),
            pltpu.VMEM((18 * 16, CH), BF16),
            pltpu.VMEM((12 * 8, CH), F32),
            pltpu.VMEM((1536, CH), F32),
            pltpu.VMEM((768, CH), F32),
            pltpu.VMEM((384, CH), F32),
            pltpu.VMEM((192, CH), F32),
            pltpu.VMEM((96, CH), F32),
        ],
        compiler_params=pltpu.CompilerParams(vmem_limit_bytes=32 * 1024 * 1024),
        cost_estimate=pl.CostEstimate(flops=1_400_000_000, bytes_accessed=3_500_000, transcendentals=0),
        name="corr_encode",
    )(source, target, inject, w_slots)


def conv_same(inputs, kernel):
    return lax.conv_general_dilated(
        inputs, kernel, (1, 1), "SAME", dimension_numbers=("NHWC", "HWIO", "NHWC"), preferred_element_type=F32
    )


def recurrent_update(motion, ctx, w_gates, w_cand):
    width = CH
    motion_map = motion.reshape(1, HGT, WID, width)
    state_map = jnp.tanh(ctx[:, :width].astype(F32)).astype(BF16).reshape(1, HGT, WID, width)
    gates = conv_same(jnp.concatenate([state_map, motion_map], axis=3), w_gates)
    update_gate = jax.nn.sigmoid(gates[..., :width])
    reset_gate = jax.nn.sigmoid(gates[..., width:])
    state_wide = state_map.astype(F32)
    reset_state = (reset_gate * state_wide).astype(BF16)
    candidate = jnp.tanh(conv_same(jnp.concatenate([reset_state, motion_map], axis=3), w_cand))
    new_state = ((1.0 - update_gate) * state_wide + update_gate * candidate).astype(BF16)
    return new_state.reshape(PIX, width)


def sigmoid(x):
    return 1.0 / (1.0 + jnp.exp(-x))


def edge_terms(rel, depth, flow_u, flow_v, weight_u, weight_v, col, row):
    center_x = (WID - 1) / 2.0
    center_y = (HGT - 1) / 2.0
    ray_x = (col - center_x) / FOCAL
    ray_y = (row - center_y) / FOCAL
    move_x, move_y, move_z, turn_x, turn_y, turn_z = rel
    point_x = ray_x + turn_y - turn_z * ray_y + depth * move_x
    point_y = ray_y + turn_z * ray_x - turn_x + depth * move_y
    point_z = 1.0 + turn_x * ray_y - turn_y * ray_x + depth * move_z
    inverse_z = 1.0 / point_z
    slope = FOCAL * inverse_z
    bend_u = -FOCAL * point_x * inverse_z * inverse_z
    bend_v = -FOCAL * point_y * inverse_z * inverse_z
    resid_u = col + flow_u - (FOCAL * point_x * inverse_z + center_x)
    resid_v = row + flow_v - (FOCAL * point_y * inverse_z + center_y)
    blank = jnp.zeros_like(slope)
    jac_u = [depth * slope, blank, depth * bend_u, bend_u * ray_y, slope - bend_u * ray_x, -slope * ray_y]
    jac_v = [blank, depth * slope, depth * bend_v, bend_v * ray_y - slope, -bend_v * ray_x, slope * ray_x]
    depth_u = slope * move_x + bend_u * move_z
    depth_v = slope * move_y + bend_v * move_z
    scaled_u = [j * weight_u for j in jac_u]
    scaled_v = [j * weight_v for j in jac_v]
    cross = [scaled_u[c] * depth_u + scaled_v[c] * depth_v for c in range(6)]
    curve = weight_u * depth_u * depth_u + weight_v * depth_v * depth_v
    depth_grad = weight_u * depth_u * resid_u + weight_v * depth_v * resid_v
    return jac_u, jac_v, scaled_u, scaled_v, resid_u, resid_v, cross, curve, depth_grad


def panel_step(mat, p, tiles):
    cols = [slice(128 * t, 128 * t + 128) for t in range(tiles)]
    base = pl.multiple_of(p * 8, 8)
    panel = mat[pl.ds(base, 8), 0 : 128 * tiles]
    splat = [[jnp.broadcast_to(panel[i : i + 1, j : j + 1], (8, 128)) for j in range(i + 1)] for i in range(8)]
    low = [[None] * 8 for _ in range(8)]
    inv = [None] * 8
    for j in range(8):
        inv[j] = 1.0 / splat[j][j]
        for i in range(j + 1, 8):
            low[i][j] = splat[i][j] * inv[j]
        for i in range(j + 1, 8):
            for k in range(j + 1, i + 1):
                splat[i][k] = splat[i][k] - low[i][j] * splat[k][j]
    x = [[jnp.broadcast_to(panel[i : i + 1, c], (8, 128)) for c in cols] for i in range(8)]
    for i in range(8):
        for j in range(i):
            x[i] = [x[i][t] - low[i][j] * x[j][t] for t in range(tiles)]
    x = [[v * inv[i] for v in x[i]] for i in range(8)]
    for i in range(7, -1, -1):
        for j in range(i + 1, 8):
            x[i] = [x[i][t] - low[j][i] * x[j][t] for t in range(tiles)]
    lane = lax.broadcasted_iota(jnp.int32, (8, 128), 1)
    sub = lax.broadcasted_iota(jnp.int32, (8, 128), 0)

    def put(start, vals):
        rolled = [pltpu.roll(v, 120, 1) for v in vals]
        for t in range(tiles):
            v = rolled[t] if t == tiles - 1 else jnp.where(lane < 120, rolled[t], rolled[t + 1])
            mat[pl.ds(start, 8), cols[t]] = v

    for r in range(UNK // 8):
        vals = [mat[8 * r : 8 * r + 8, c] for c in cols]
        lead = vals[0]
        for i in range(8):
            factor = jnp.broadcast_to(lead[:, i : i + 1], (8, 128))
            vals = [vals[t] - factor * x[i][t] for t in range(tiles)]
        put(8 * r, vals)
    own = []
    for t in range(tiles):
        v = x[0][t]
        for i in range(1, 8):
            v = jnp.where(sub == i, x[i][t], v)
        own.append(v)
    put(base, own)


def gn_kernel(
    hid_ref, wh_ref, pose_ref, sgn_ref, sgnt_ref, trep_ref, depth_ref,
    pose_out, depth_out,
    heads_s, heads_r, k_s, k_r, f_s, f_r, row_s, row_r, d_s, rep_s, mat,
    h_send, h_recv, k_send, k_recv, f_send, f_recv, r_send, r_recv, d_send, d_recv,
):
    me_f = lax.axis_index("frames")
    me_e = lax.axis_index("edges")

    barrier = pltpu.get_barrier_semaphore()
    for d in range(1, EDGES):
        pl.semaphore_signal(barrier, inc=1, device_id={"edges": lax.rem(me_e + d, EDGES)}, device_id_type=MESH)

    def greet(d, carry):
        pl.semaphore_signal(barrier, inc=1, device_id={"frames": lax.rem(me_f + d, NF)}, device_id_type=MESH)
        return carry

    lax.fori_loop(1, NF, greet, 0)

    heads = dot_nt(wh_ref[...], hid_ref[...])
    for j in range(EDGES):
        heads_s[j] = heads[:, j * SLICE : (j + 1) * SLICE]

    lane256 = lax.broadcasted_iota(jnp.int32, (256, 128), 1)
    frame256 = lax.broadcasted_iota(jnp.int32, (256, 128), 0) // 8
    own = (frame256 == lane256 % NF).astype(F32)
    for k in range(EDGES):
        rep_s[k] = (trep_ref[:, k : k + 1] == lane256 % NF).astype(F32) - own

    pl.semaphore_wait(barrier, EDGES - 1 + NF - 1)

    def exchange(src_of, dst_ref, send_sem, recv_sem):
        copies = []
        for d in range(1, EDGES):
            peer = lax.rem(me_e + d, EDGES)
            copy = pltpu.make_async_remote_copy(
                src_ref=src_of(peer),
                dst_ref=dst_ref.at[me_e],
                send_sem=send_sem.at[d],
                recv_sem=recv_sem.at[d],
                device_id={"edges": peer},
                device_id_type=MESH,
            )
            copy.start()
            copies.append(copy)
        return copies

    copies = exchange(lambda peer: heads_s.at[peer], heads_r, h_send, h_recv)
    heads_r[me_e] = heads_s[me_e]
    for copy in copies:
        copy.wait()

    def component(c):
        return jnp.concatenate([heads_r[k, c : c + 1, :] for k in range(EDGES)], axis=0)

    flow_u, flow_v = component(0), component(1)
    weight_u, weight_v = sigmoid(component(2)), sigmoid(component(3))
    pix = lax.broadcasted_iota(jnp.int32, (8, SLICE), 1)
    col = (pix % WID).astype(F32)
    row = (pix // WID + me_e * ROWS).astype(F32)
    depth = depth_ref[pl.ds(me_e, 1), :]
    sgn = sgn_ref[...]
    poses = pose_ref[...]

    k_lane = lax.broadcasted_iota(jnp.int32, (48, 128), 1)
    k_row = lax.broadcasted_iota(jnp.int32, (48, 128), 0)
    same_edge = (k_lane < 56) & (k_lane % 8 == k_row % 8)
    lane32 = lax.broadcasted_iota(jnp.int32, (NF, 128), 1)
    sub32 = lax.broadcasted_iota(jnp.int32, (NF, 128), 0)
    lane8 = lax.broadcasted_iota(jnp.int32, (8, 128), 1)
    sub8 = lax.broadcasted_iota(jnp.int32, (8, 128), 0)

    def along_edges(vector):
        return jnp.sum(sgn * vector, axis=1, keepdims=True)

    for it in range(ITERS):
        rel = [along_edges(poses[c : c + 1, :]) for c in range(6)]
        jac_u, jac_v, scaled_u, scaled_v, resid_u, resid_v, cross, curve, depth_grad = edge_terms(
            rel, depth, flow_u, flow_v, weight_u, weight_v, col, row
        )
        frame_curve = jnp.sum(curve, axis=0, keepdims=True)
        frame_grad = jnp.sum(depth_grad, axis=0, keepdims=True)
        inv_damped = 1.0 / ((1.0 + DEPTH_DAMPING) * frame_curve + DEPTH_FLOOR)
        lead = jnp.concatenate([jnp.concatenate(scaled_u, axis=0), jnp.concatenate(scaled_v, axis=0)], axis=1)
        pad = jnp.zeros((72, 2 * SLICE), F32)
        trail = jnp.concatenate(
            [
                jnp.concatenate([jnp.concatenate(jac_u, axis=0), jnp.concatenate(jac_v, axis=0)], axis=1),
                jnp.concatenate([resid_u, resid_v], axis=1),
                pad,
            ],
            axis=0,
        )
        hess = dot_nt(lead, trail, HIGHEST)
        stack = jnp.concatenate(cross, axis=0)
        right = jnp.concatenate(
            [stack, jnp.broadcast_to(frame_grad, (8, SLICE)) * (sub_row(8, SLICE) == 0).astype(F32), pad[:, :SLICE]],
            axis=0,
        )
        schur = dot_nt(stack * inv_damped, right, HIGHEST)
        small = jnp.where(same_edge, hess, 0.0) - schur
        for c in range(6):
            k_s[it, c] = small[8 * c : 8 * c + 8]
        for c in range(6, 8):
            k_s[it, c] = jnp.zeros((8, 128), F32)
        copies = exchange(lambda peer: k_s.at[it, peer], k_r.at[it], k_send.at[it], k_recv.at[it])
        k_r[it, me_e] = k_s[it, me_e]
        for copy in copies:
            copy.wait()
        total = k_r[it, 0]
        for e in range(1, EDGES):
            total = total + k_r[it, e]
        f_s[it] = total
        f_r[it, me_f] = total

        def frame_copy(d):
            return pltpu.make_async_remote_copy(
                src_ref=f_s.at[it],
                dst_ref=f_r.at[it, me_f],
                send_sem=f_send.at[it, d],
                recv_sem=f_recv.at[it, d],
                device_id={"frames": lax.rem(me_f + d, NF)},
                device_id_type=MESH,
            )

        def send(d, carry):
            frame_copy(d).start()
            return carry

        def arrive(d, carry):
            frame_copy(d).wait()
            return carry

        lax.fori_loop(1, NF, send, 0)
        lax.fori_loop(1, NF, arrive, 0)

        blocks = f_r[it].reshape(256, 128)
        left_sum = jnp.zeros((256, 128), F32)
        right_sum = jnp.zeros((256, 128), F32)
        for k in range(EDGES):
            rep = rep_s[k]
            left_sum = left_sum + jnp.take_along_axis(blocks, (lane256 // 32) * 8 + k, axis=1) * rep
            right_sum = right_sum + jnp.take_along_axis(blocks, (lane256 // 32) % 2 * 8 + 32 + k, axis=1) * rep
        rhs = jnp.sum(jnp.where((lane256 >= 48) & (lane256 < 56), blocks, 0.0), axis=1, keepdims=True)
        right_sum = jnp.where(lane256 < 64, right_sum, jnp.where(lane256 == 64, rhs, 0.0))
        row_s[it] = jnp.concatenate(
            [
                jnp.dot(sgnt_ref[...], left_sum, precision=HIGHEST, preferred_element_type=F32),
                jnp.dot(sgnt_ref[...], right_sum, precision=HIGHEST, preferred_element_type=F32),
            ],
            axis=1,
        )
        copies = exchange(lambda peer: row_s.at[it], row_r.at[it], r_send.at[it], r_recv.at[it])
        row_r[it, me_e] = row_s[it]
        for copy in copies:
            copy.wait()

        for c in range(6):
            for t in range(2):
                v = row_r[it, c, :, 128 * t : 128 * t + 128]
                diag = lane32 + 128 * t == sub32 + 32 * c
                mat[32 * c : 32 * c + 32, 128 * t : 128 * t + 128] = v + jnp.where(
                    diag, POSE_DAMPING * v + POSE_FLOOR, 0.0
                )

        def wide(p, carry):
            panel_step(mat, p, 2)
            return carry

        def narrow(p, carry):
            panel_step(mat, p, 1)
            return carry

        lax.fori_loop(0, 16, wide, 0)
        lax.fori_loop(16, 24, narrow, 0)

        steps = []
        for c in range(6):
            v = jnp.broadcast_to(mat[32 * c : 32 * c + 32, 0:1], (NF, 128))
            steps.append(jnp.sum(jnp.where(lane32 == sub32, v, 0.0), axis=0, keepdims=True))
        along = jnp.zeros((8, SLICE), F32)
        for c in range(6):
            along = along + along_edges(steps[c]) * cross[c]
        along = jnp.sum(along, axis=0, keepdims=True)
        poses = poses + jnp.concatenate(steps + [jnp.zeros((2, 128), F32)], axis=0)
        depth = depth + (frame_grad - along) * inv_damped

    pose_out[...] = jnp.broadcast_to(
        jnp.sum(jnp.where(lane8 == me_f, poses, 0.0), axis=1, keepdims=True), (8, 128)
    )
    d_s[...] = jnp.broadcast_to(depth, (8, SLICE))
    copies = exchange(lambda peer: d_s, depth_out, d_send, d_recv)
    depth_out[me_e] = d_s[...]
    for copy in copies:
        copy.wait()


def sub_row(rows, cols):
    return lax.broadcasted_iota(jnp.int32, (rows, cols), 0)


def gauss_newton(hidden, w_head, inv_depth, table, frame):
    pose_table = jnp.pad(table[::EDGES, :6].T, ((0, 2), (0, 128 - NF)))
    targets = table[:, 6].astype(jnp.int32)
    own_targets = lax.dynamic_slice_in_dim(targets, frame * EDGES, EDGES, 0)
    ids = jnp.arange(128)
    sgn = (own_targets[:, None] == ids[None, :]).astype(F32) - (ids[None, :] == frame).astype(F32)
    ids = jnp.arange(NF)
    sgnt = (targets[None, :] == ids[:, None]).astype(F32) - ((jnp.arange(NF * EDGES) // EDGES)[None, :] == ids[:, None])
    trep = jnp.pad(jnp.repeat(targets.reshape(NF, EDGES), EDGES, axis=0), ((0, 0), (0, 120)))
    wh = jnp.pad(w_head.T, ((0, 12), (0, 0)))[:8]
    vmem = pl.BlockSpec(memory_space=pltpu.VMEM)
    dma = pltpu.SemaphoreType.DMA
    pose_out, depth_out = pl.pallas_call(
        gn_kernel,
        out_shape=(
            jax.ShapeDtypeStruct((8, 128), F32),
            jax.ShapeDtypeStruct((EDGES, 8, SLICE), F32),
        ),
        in_specs=[vmem] * 7,
        out_specs=(vmem, vmem),
        scratch_shapes=[
            pltpu.VMEM((EDGES, 8, SLICE), F32),
            pltpu.VMEM((EDGES, 8, SLICE), F32),
            pltpu.VMEM((ITERS, 8, 8, 128), F32),
            pltpu.VMEM((ITERS, 8, 8, 128), F32),
            pltpu.VMEM((ITERS, 8, 128), F32),
            pltpu.VMEM((ITERS, NF, 8, 128), F32),
            pltpu.VMEM((ITERS, NF, 256), F32),
            pltpu.VMEM((ITERS, EDGES, NF, 256), F32),
            pltpu.VMEM((8, SLICE), F32),
            pltpu.VMEM((EDGES, 256, 128), F32),
            pltpu.VMEM((UNK, 256), F32),
            dma((EDGES,)),
            dma((EDGES,)),
            dma((ITERS, EDGES)),
            dma((ITERS, EDGES)),
            dma((ITERS, NF)),
            dma((ITERS, NF)),
            dma((ITERS, EDGES)),
            dma((ITERS, EDGES)),
            dma((EDGES,)),
            dma((EDGES,)),
        ],
        compiler_params=pltpu.CompilerParams(
            vmem_limit_bytes=32 * 1024 * 1024, collective_id=1, has_side_effects=True
        ),
        name="gauss_newton",
    )(hidden, wh, pose_table, sgn, sgnt, trep, inv_depth.reshape(EDGES, SLICE))
    return pose_out[:6, :1], depth_out[:, 0, :].reshape(1, PIX)


def per_device(fmap, context, poses, inv_depth, targets, w_corr, w_gates, w_cand, w_head):
    frame = lax.axis_index("frames")
    slot = lax.axis_index("edges")
    row = jnp.concatenate([poses[:, 0], targets.astype(F32), jnp.zeros((1,), F32)])
    table = lax.all_gather(row, ("frames", "edges"), axis=0)
    own = lax.dynamic_slice_in_dim(fmap[0], slot * SLICE, SLICE, 0)
    pieces = lax.all_gather(own, "frames", axis=0)
    goals = lax.dynamic_slice_in_dim(table[:, 6].astype(jnp.int32), frame * EDGES, EDGES, 0)
    chosen = jnp.take(pieces, jnp.clip(goals, 0, NF - 1), axis=0)
    target = lax.all_to_all(chosen, "edges", split_axis=0, concat_axis=0, tiled=True).reshape(PIX, CH)
    motion = encode(fmap[0], target, context[0, :, CH:], w_corr)
    hidden = recurrent_update(motion, context[0], w_gates, w_cand)
    new_poses, new_depth = gauss_newton(hidden, w_head, inv_depth, table, frame)
    return new_poses, new_depth, hidden[None]


def solution(mesh):
    return jax.shard_map(
        per_device,
        mesh=mesh,
        in_specs=(
            P("frames", None, None),
            P("frames", None, None),
            P(None, "frames"),
            P("frames", None),
            P(("frames", "edges")),
            P(),
            P(),
            P(),
            P(),
        ),
        out_specs=(P(None, "frames"), P("frames", None), P(("frames", "edges"), None, None)),
        check_vma=False,
    )
```

```python
import functools
import math

import jax
import jax.numpy as jnp
from jax import lax
from jax.experimental import pallas as pl
from jax.experimental.pallas import tpu as pltpu
from jax.sharding import PartitionSpec as P

HGT = 48
WID = 64
CH = 128
LEVELS = 4
RADIUS = 3
ITERS = 2
PIX = HGT * WID
NF = 32
EDGES = 8
SLICE = PIX // EDGES
ROWS = SLICE // WID
UNK = 6 * NF

FOCAL = 50.0
POSE_DAMPING = 0.1
POSE_FLOOR = 1.0
DEPTH_DAMPING = 0.1
DEPTH_FLOOR = 1.0
HIGHEST = lax.Precision.HIGHEST
F32 = jnp.float32
BF16 = jnp.bfloat16
MESH = pl.DeviceIdType.MESH


def dot_nt(a, b, precision=None):
    return lax.dot_general(a, b, (((1,), (1,)), ((), ())), precision=precision, preferred_element_type=F32)


HALF = SLICE // 2
XS = 4
ZS = NF // XS


def gather_kernel(
    fmap_ref, pose_ref, goal_ref, out_ref, table_ref,
    maps, chosen, goals_r, tile_s, goals_v, goals_m,
    own_sem, g_send, g_recv, t_send, t_recv, zr_send, zr_recv, zl_send, zl_recv,
    xa_send, xa_recv, xb_send, xb_recv, wr_send, wr_recv, wl_send, wl_recv, c_send, c_recv, m_sem,
):
    me_f = lax.axis_index("frames")
    me_e = lax.axis_index("edges")
    x, z = me_f // ZS, lax.rem(me_f, ZS)

    def frame(dx, dz):
        return lax.rem(x + dx, XS) * ZS + lax.rem(z + dz, ZS)

    own = []
    for h in range(2):
        copy = pltpu.make_async_copy(
            fmap_ref.at[pl.ds(pl.multiple_of(me_e * SLICE + h * HALF, HALF), HALF)],
            maps.at[x, z, h],
            own_sem.at[h],
        )
        copy.start()
        own.append(copy)

    barrier = pltpu.get_barrier_semaphore()
    for d in range(1, EDGES):
        pl.semaphore_signal(barrier, inc=1, device_id={"edges": lax.rem(me_e + d, EDGES)}, device_id_type=MESH)

    def greet(d, carry):
        pl.semaphore_signal(barrier, inc=1, device_id={"frames": lax.rem(me_f + d, NF)}, device_id_type=MESH)
        return carry

    lax.fori_loop(1, NF, greet, 0)
    for copy in own:
        copy.wait()
    pl.semaphore_wait(barrier, EDGES - 1 + NF - 1)

    def send(src, dst, send_sem, recv_sem, peer):
        copy = pltpu.make_async_remote_copy(
            src_ref=src, dst_ref=dst, send_sem=send_sem, recv_sem=recv_sem, device_id=peer, device_id_type=MESH
        )
        copy.start()
        return copy

    right, left = {"frames": frame(0, 1)}, {"frames": frame(0, ZS - 1)}

    def ring(s, way):
        zz = lax.rem(z + (ZS - s if way else s), ZS)
        ref = maps.at[x, zz, 0]
        if s == 3:
            ref = ref.at[pl.ds(0 if way else HALF // 2, HALF // 2)]
        if way:
            return send(ref, ref, zr_send.at[s], zr_recv.at[s], right)
        return send(ref, ref, zl_send.at[s], zl_recv.at[s], left)

    def across(zz, order):
        copies = []
        for d in range(1, XS):
            ref = maps.at[x, zz, 0]
            copies.append(
                send(ref, ref, xa_send.at[d - 1, order], xa_recv.at[d - 1, order], {"frames": frame(d, 0)})
            )
        return copies

    def ring_wide(s, way):
        zz = lax.rem(z + (ZS - s if way else s), ZS)
        copies = []
        for c in range(XS):
            ref = maps.at[c, zz, 1]
            if s == 3:
                ref = ref.at[pl.ds(0 if way else HALF // 2, HALF // 2)]
            if way:
                copies.append(send(ref, ref, wr_send.at[s, c], wr_recv.at[s, c], right))
            else:
                copies.append(send(ref, ref, wl_send.at[s, c], wl_recv.at[s, c], left))
        return copies

    zr, zl = [ring(0, True)], [ring(0, False)]
    xb = []
    for d in range(1, XS):
        ref = maps.at[x, z, 1]
        xb.append(send(ref, ref, xb_send.at[d - 1], xb_recv.at[d - 1], {"frames": frame(d, 0)}))
    goal_copies = []
    for d in range(1, EDGES):
        peer = lax.rem(me_e + d, EDGES)
        goal_copies.append(send(goal_ref, goals_r.at[me_e], g_send.at[d], g_recv.at[d], {"edges": peer}))
    goals_r[me_e] = goal_ref[...]
    xa = across(z, 0)

    for copy in xb:
        copy.wait_recv()
    wr, wl = [ring_wide(0, True)], [ring_wide(0, False)]

    for copy in goal_copies:
        copy.wait()
    goals = jnp.concatenate([goals_r[k, 0:1, :] for k in range(EDGES)], axis=0)
    goals_v[...] = goals
    to_scalar = pltpu.make_async_copy(goals_v, goals_m, m_sem)
    to_scalar.start()
    lane = lax.broadcasted_iota(jnp.int32, (8, 128), 1)
    tile = jnp.where(lane == 6, goals.astype(F32), pose_ref[...])
    tile_s[...] = tile
    table_ref[me_f] = tile

    def tile_copy(d):
        return pltpu.make_async_remote_copy(
            src_ref=tile_s,
            dst_ref=table_ref.at[me_f],
            send_sem=t_send.at[d],
            recv_sem=t_recv.at[d],
            device_id={"frames": lax.rem(me_f + d, NF)},
            device_id_type=MESH,
        )

    def tile_start(d, carry):
        tile_copy(d).start()
        return carry

    lax.fori_loop(1, NF, tile_start, 0)

    for s in range(1, 4):
        zr[s - 1].wait_recv()
        zr.append(ring(s, True))
        zl[s - 1].wait_recv()
        zl.append(ring(s, False))
        xa += across(lax.rem(z + ZS - s, ZS), 2 * s - 1)
        xa += across(lax.rem(z + s, ZS), 2 * s)
        for c in range(XS):
            wr[s - 1][c].wait_recv()
            wl[s - 1][c].wait_recv()
        wr.append(ring_wide(s, True))
        wl.append(ring_wide(s, False))
    zr[3].wait_recv()
    zl[3].wait_recv()
    xa += across(lax.rem(z + 4, ZS), 7)
    for c in range(XS):
        wr[3][c].wait_recv()
        wl[3][c].wait_recv()
    for copy in xa:
        copy.wait_recv()
    to_scalar.wait()

    for k in range(EDGES):
        goal = goals_m[k, 0]
        chosen[k] = maps[goal // ZS, lax.rem(goal, ZS)]
    swaps = []
    for d in range(1, EDGES):
        peer = lax.rem(me_e + d, EDGES)
        swaps.append(send(chosen.at[peer], out_ref.at[me_e], c_send.at[d], c_recv.at[d], {"edges": peer}))
    out_ref[me_e] = chosen[me_e]

    def tile_wait(d, carry):
        tile_copy(d).wait()
        return carry

    lax.fori_loop(1, NF, tile_wait, 0)
    for copy in swaps:
        copy.wait()
    for copy in zr + zl + xa + xb + sum(wr, []) + sum(wl, []):
        copy.wait_send()


def gather(fmap, poses, targets):
    pose = jnp.broadcast_to(jnp.pad(poses[:, 0], (0, 122))[None, :], (8, 128))
    goal = jnp.broadcast_to(targets.reshape(1, 1), (8, 128))
    vmem = pl.BlockSpec(memory_space=pltpu.VMEM)
    dma = pltpu.SemaphoreType.DMA
    return pl.pallas_call(
        gather_kernel,
        out_shape=(
            jax.ShapeDtypeStruct((EDGES, 2, HALF, CH), BF16),
            jax.ShapeDtypeStruct((NF, 8, 128), F32),
        ),
        in_specs=[pl.BlockSpec(memory_space=pl.ANY), vmem, vmem],
        out_specs=(vmem, vmem),
        scratch_shapes=[
            pltpu.VMEM((XS, ZS, 2, HALF, CH), BF16),
            pltpu.VMEM((EDGES, 2, HALF, CH), BF16),
            pltpu.VMEM((EDGES, 8, 128), jnp.int32),
            pltpu.VMEM((8, 128), F32),
            pltpu.VMEM((8, 128), jnp.int32),
            pltpu.SMEM((8, 128), jnp.int32),
            dma((2,)),
            dma((EDGES,)),
            dma((EDGES,)),
            dma((NF,)),
            dma((NF,)),
            dma((4,)),
            dma((4,)),
            dma((4,)),
            dma((4,)),
            dma((3, 8)),
            dma((3, 8)),
            dma((3,)),
            dma((3,)),
            dma((4, XS)),
            dma((4, XS)),
            dma((4, XS)),
            dma((4, XS)),
            dma((EDGES,)),
            dma((EDGES,)),
            dma(()),
        ],
        compiler_params=pltpu.CompilerParams(
            vmem_limit_bytes=32 * 1024 * 1024, collective_id=2, has_side_effects=True
        ),
        name="gather_maps",
    )(fmap, pose, goal)


def update_kernel(
    src_ref, tgt_ref, ctx_ref, w_ref, wg_ref, wc_ref, wh_ref, hid_ref, heads_ref,
    p0, p1, p2, p3, t1, f1, t2, f2, t3, sm, rm, upd,
):
    zero = jnp.zeros((3 * WID, CH), BF16)
    p0[pl.ds(0, 192), :] = zero
    p0[pl.ds(51 * 64, 192), :] = zero
    p1[pl.ds(0, 96), :] = zero[:96]
    p1[pl.ds(27 * 32, 96), :] = zero[:96]
    p2[pl.ds(0, 48), :] = zero[:48]
    p2[pl.ds(15 * 16, 48), :] = zero[:48]
    p3[pl.ds(0, 24), :] = jnp.zeros((24, CH), F32)
    p3[pl.ds(9 * 8, 24), :] = jnp.zeros((24, CH), F32)
    edge = jnp.zeros((WID, 6 * CH), BF16)
    for ref in (sm, rm):
        ref[pl.ds(0, WID), :] = edge
        ref[pl.ds(PIX + WID, WID), :] = edge

    p0[pl.ds(192, PIX), :] = tgt_ref[...]

    def fold_rows(r, carry):
        a = tgt_ref[pl.ds(r * 128, 64), :].astype(F32)
        b = tgt_ref[pl.ds(r * 128 + 64, 64), :].astype(F32)
        t1[pl.ds(r * 64, 64), :] = a + b
        return carry

    lax.fori_loop(0, HGT // 2, fold_rows, 0)
    f1[...] = 0.25 * (t1[pl.ds(0, 768, stride=2), :] + t1[pl.ds(1, 768, stride=2), :])
    p1[pl.ds(96, 768), :] = f1[...].astype(BF16)
    half = f1[...].reshape(12, 2, 32, CH)
    t2[...] = (half[:, 0] + half[:, 1]).reshape(384, CH)
    f2[...] = 0.25 * (t2[pl.ds(0, 192, stride=2), :] + t2[pl.ds(1, 192, stride=2), :])
    p2[pl.ds(48, 192), :] = f2[...].astype(BF16)
    half = f2[...].reshape(6, 2, 16, CH)
    t3[...] = (half[:, 0] + half[:, 1]).reshape(96, CH)
    f3 = 0.25 * (t3[pl.ds(0, 48, stride=2), :] + t3[pl.ds(1, 48, stride=2), :])
    p3[pl.ds(24, 48), :] = f3.astype(BF16).astype(F32)

    lane = lax.broadcasted_iota(jnp.int32, (8, 128), 1)
    sub = lax.broadcasted_iota(jnp.int32, (8, 128), 0)
    col = lane % WID
    scale = 1.0 / math.sqrt(CH)

    def rotate(x, level):
        amount = ((col >> level) + 5) % 8
        for bit in (1, 2, 4):
            x = jnp.where((amount // bit) % 2 == 1, pltpu.roll(x, 8 - bit, 0), x)
        return x

    def pick(vol, groups, level):
        acc = jnp.zeros((8, 128), F32)
        for g in range(groups):
            acc = jnp.where(jnp.abs(8 * g + sub - (col >> level)) <= RADIUS, vol[8 * g : 8 * g + 8], acc)
        return acc

    def spread(refs, start, lead, value):
        rows = value.shape[0]
        column = lax.broadcasted_iota(jnp.int32, value.shape, 0) % WID
        before = jnp.where(column == 0, 0.0, pltpu.roll(value, 1, 0))
        after = jnp.where(column == WID - 1, 0.0, pltpu.roll(value, rows - 1, 0))
        for dx, v in enumerate((before, value, after)):
            v = v.astype(BF16)
            for ref in refs:
                ref[pl.ds(start + WID, rows), 2 * CH * dx + lead : 2 * CH * dx + lead + CH] = v

    def block(q, carry):
        src = src_ref[pl.ds(q * 128, 128), :]
        parts = []
        vol = dot_nt(p0[pl.ds(q * 128, 512), :], src)
        rows = [pick(vol[64 * a : 64 * a + 64], 8, 0) for a in range(8)]
        for a in range(7):
            parts.append(rotate(jnp.where(lane < WID, rows[a], rows[a + 1]), 0))
        vol = dot_nt(p1[pl.ds(q * 32, 224), :], src)
        for a in range(7):
            parts.append(rotate(pick(vol[32 * a : 32 * a + 32], 4, 1), 1))
        vol = dot_nt(p2[pl.ds((q // 2) * 16, 112), :], src)
        for a in range(7):
            parts.append(rotate(pick(vol[16 * a : 16 * a + 16], 2, 2), 2))
        vol = dot_nt(p3[pl.ds((q // 4) * 8, 56), :].astype(BF16), src)
        for a in range(7):
            parts.append(rotate(pick(vol[8 * a : 8 * a + 8], 1, 3), 3))
        corr = (jnp.concatenate(parts, axis=0) * scale).astype(BF16)
        enc = lax.dot_general(corr, w_ref[...], (((0,), (0,)), ((), ())), preferred_element_type=F32)
        start = pl.multiple_of(q * 128, 128)
        ctx = ctx_ref[pl.ds(start, 128), :].astype(F32)
        motion = jnp.maximum(enc, 0.0) + jnp.maximum(ctx[:, CH:], 0.0)
        spread((sm, rm), start, CH, motion.astype(BF16).astype(F32))
        state = jnp.tanh(ctx[:, :CH]).astype(BF16).astype(F32)
        spread((sm,), start, 0, state)
        return carry

    lax.fori_loop(0, PIX // 128, block, 0, unroll=2)

    def gates(t, carry):
        start = pl.multiple_of(t * SLICE, SLICE)
        acc = jnp.zeros((SLICE, 2 * CH), F32)
        for dy in range(3):
            acc = acc + jnp.dot(sm[pl.ds(start + WID * dy, SLICE), :], wg_ref[dy], preferred_element_type=F32)
        gate = 0.5 * jnp.tanh(0.5 * acc) + 0.5
        upd[pl.ds(start, SLICE), :] = gate[:, :CH]
        state = sm[pl.ds(start + WID, SLICE), 2 * CH : 3 * CH].astype(F32)
        spread((rm,), start, 0, (gate[:, CH:] * state).astype(BF16).astype(F32))
        return carry

    lax.fori_loop(0, EDGES, gates, 0)

    def blend(t, carry):
        start = pl.multiple_of(t * SLICE, SLICE)
        acc = jnp.zeros((SLICE, CH), F32)
        for dy in range(3):
            acc = acc + jnp.dot(rm[pl.ds(start + WID * dy, SLICE), :], wc_ref[dy], preferred_element_type=F32)
        update = upd[pl.ds(start, SLICE), :]
        state = sm[pl.ds(start + WID, SLICE), 2 * CH : 3 * CH].astype(F32)
        hidden = ((1.0 - update) * state + update * jnp.tanh(acc)).astype(BF16)
        hid_ref[pl.ds(start, SLICE), :] = hidden
        heads_ref[t] = dot_nt(wh_ref[...], hidden)
        return carry

    lax.fori_loop(0, EDGES, blend, 0)


def update(source, target, context, w_corr, w_gates, w_cand, w_head):
    w_slots = jnp.pad(w_corr.reshape(28, 7, CH), ((0, 0), (0, 1), (0, 0))).reshape(224, CH)
    wh = jnp.pad(w_head.T, ((0, 12), (0, 0)))[:8]
    vmem = pl.BlockSpec(memory_space=pltpu.VMEM)
    return pl.pallas_call(
        update_kernel,
        out_shape=(jax.ShapeDtypeStruct((PIX, CH), BF16), jax.ShapeDtypeStruct((EDGES, 8, SLICE), F32)),
        in_specs=[vmem] * 7,
        out_specs=(vmem, vmem),
        scratch_shapes=[
            pltpu.VMEM((54 * 64, CH), BF16),
            pltpu.VMEM((30 * 32, CH), BF16),
            pltpu.VMEM((18 * 16, CH), BF16),
            pltpu.VMEM((12 * 8, CH), F32),
            pltpu.VMEM((1536, CH), F32),
            pltpu.VMEM((768, CH), F32),
            pltpu.VMEM((384, CH), F32),
            pltpu.VMEM((192, CH), F32),
            pltpu.VMEM((96, CH), F32),
            pltpu.VMEM((PIX + 2 * WID, 6 * CH), BF16),
            pltpu.VMEM((PIX + 2 * WID, 6 * CH), BF16),
            pltpu.VMEM((PIX, CH), F32),
        ],
        compiler_params=pltpu.CompilerParams(vmem_limit_bytes=48 * 1024 * 1024),
        cost_estimate=pl.CostEstimate(flops=7_000_000_000, bytes_accessed=6_500_000, transcendentals=2_000_000),
        name="edge_update",
    )(source, target, context, w_slots, w_gates.reshape(3, 6 * CH, 2 * CH), w_cand.reshape(3, 6 * CH, CH), wh)


def sigmoid(x):
    return 1.0 / (1.0 + jnp.exp(-x))


def edge_terms(rel, depth, flow_u, flow_v, weight_u, weight_v, col, row):
    center_x = (WID - 1) / 2.0
    center_y = (HGT - 1) / 2.0
    ray_x = (col - center_x) / FOCAL
    ray_y = (row - center_y) / FOCAL
    move_x, move_y, move_z, turn_x, turn_y, turn_z = rel
    point_x = ray_x + turn_y - turn_z * ray_y + depth * move_x
    point_y = ray_y + turn_z * ray_x - turn_x + depth * move_y
    point_z = 1.0 + turn_x * ray_y - turn_y * ray_x + depth * move_z
    inverse_z = 1.0 / point_z
    slope = FOCAL * inverse_z
    bend_u = -FOCAL * point_x * inverse_z * inverse_z
    bend_v = -FOCAL * point_y * inverse_z * inverse_z
    resid_u = col + flow_u - (FOCAL * point_x * inverse_z + center_x)
    resid_v = row + flow_v - (FOCAL * point_y * inverse_z + center_y)
    blank = jnp.zeros_like(slope)
    jac_u = [depth * slope, blank, depth * bend_u, bend_u * ray_y, slope - bend_u * ray_x, -slope * ray_y]
    jac_v = [blank, depth * slope, depth * bend_v, bend_v * ray_y - slope, -bend_v * ray_x, slope * ray_x]
    depth_u = slope * move_x + bend_u * move_z
    depth_v = slope * move_y + bend_v * move_z
    scaled_u = [j * weight_u for j in jac_u]
    scaled_v = [j * weight_v for j in jac_v]
    cross = [scaled_u[c] * depth_u + scaled_v[c] * depth_v for c in range(6)]
    curve = weight_u * depth_u * depth_u + weight_v * depth_v * depth_v
    depth_grad = weight_u * depth_u * resid_u + weight_v * depth_v * resid_v
    return jac_u, jac_v, scaled_u, scaled_v, resid_u, resid_v, cross, curve, depth_grad


def reciprocal(x):
    r = pl.reciprocal(x, approx=True)
    r = r * (2.0 - x * r)
    return r * (2.0 - x * r)


def pivot_rows(panel):
    tiles = len(panel)
    lead = panel[0]
    s = [[jnp.broadcast_to(lead[i : i + 1, j : j + 1], (8, 128)) for j in range(i + 1)] for i in range(8)]
    x = [[jnp.broadcast_to(v[i : i + 1, :], (8, 128)) for v in panel] for i in range(8)]
    low = [[None] * 8 for _ in range(8)]
    inv = []
    for j in range(0, 8, 2):
        k = j + 1
        r = reciprocal(s[j][j] * s[k][k] - s[k][j] * s[k][j])
        a, b, c = s[k][k] * r, -s[k][j] * r, s[j][j] * r
        inv.append((a, b, c))
        for i in range(k + 1, 8):
            low[i][j] = s[i][j] * a + s[i][k] * b
            low[i][k] = s[i][j] * b + s[i][k] * c
        for i in range(k + 1, 8):
            for m in range(k + 1, i + 1):
                s[i][m] = s[i][m] - (low[i][j] * s[m][j] + low[i][k] * s[m][k])
    for i in range(2, 8):
        for j in range(i - i % 2):
            x[i] = [x[i][t] - low[i][j] * x[j][t] for t in range(tiles)]
    for j in range(0, 8, 2):
        a, b, c = inv[j // 2]
        u, v = x[j], x[j + 1]
        x[j] = [a * u[t] + b * v[t] for t in range(tiles)]
        x[j + 1] = [b * u[t] + c * v[t] for t in range(tiles)]
    for i in range(5, -1, -1):
        for j in range(7, i + 1 - i % 2, -1):
            x[i] = [x[i][t] - low[j][i] * x[j][t] for t in range(tiles)]
    return x


def stack_rows(x):
    sub = lax.broadcasted_iota(jnp.int32, (8, 128), 0)
    out = []
    for t in range(len(x[0])):
        v = x[0][t]
        for i in range(1, 8):
            v = jnp.where(sub == i, x[i][t], v)
        out.append(v)
    return tuple(out)


def shift_lanes(vals):
    lane = lax.broadcasted_iota(jnp.int32, (1, 128), 1)
    rolled = [pltpu.roll(v, 120, 1) for v in vals]
    return [
        v if t == len(vals) - 1 else jnp.where(lane < 120, v, rolled[t + 1]) for t, v in enumerate(rolled)
    ]


def eliminate(mat, first, last, rows):
    tiles = len(rows)
    cols = [slice(128 * t, 128 * t + 128) for t in range(tiles)]

    def step(p, own):
        base = pl.multiple_of(p * 8, 8)
        after = pl.multiple_of(jnp.minimum(p + 1, UNK // 8 - 1) * 8, 8)
        panel = [mat[pl.ds(after, 8), c] for c in cols]
        factors = [jnp.broadcast_to(panel[0][:, i : i + 1], (8, 128)) for i in range(8)]
        ahead = []
        for t in range(tiles):
            q = [factors[i] * jnp.broadcast_to(own[t][i : i + 1], (8, 128)) for i in range(8)]
            ahead.append(panel[t] - (((q[0] + q[1]) + (q[2] + q[3])) + ((q[4] + q[5]) + (q[6] + q[7]))))
        fresh = stack_rows(pivot_rows(shift_lanes(ahead)))
        wide = jnp.concatenate([jnp.concatenate(own, axis=1), jnp.zeros((120, 128 * tiles), F32)], axis=0)
        change = jnp.dot(mat[:, 0:128], wide, precision=HIGHEST, preferred_element_type=F32)
        vals = shift_lanes([mat[:, c] - change[:, c] for c in cols])
        mine = shift_lanes(list(own))
        for t in range(tiles):
            mat[:, cols[t]] = vals[t]
        for t in range(tiles):
            mat[pl.ds(base, 8), cols[t]] = mine[t]
        return fresh

    return lax.fori_loop(first, last, step, tuple(rows))


def gn_kernel(
    heads_s, table_ref, depth_ref,
    pose_out, depth_out,
    heads_r, k_s, k_r, f_s, f_r, row_s, row_r, d_s, rep_s, sgnt_s, mat,
    h_send, h_recv, k_send, k_recv, f_send, f_recv, r_send, r_recv, d_send, d_recv,
):
    me_f = lax.axis_index("frames")
    me_e = lax.axis_index("edges")

    barrier = pltpu.get_barrier_semaphore()
    for d in range(1, EDGES):
        pl.semaphore_signal(barrier, inc=1, device_id={"edges": lax.rem(me_e + d, EDGES)}, device_id_type=MESH)

    def greet(d, carry):
        pl.semaphore_signal(barrier, inc=1, device_id={"frames": lax.rem(me_f + d, NF)}, device_id_type=MESH)
        return carry

    lax.fori_loop(1, NF, greet, 0)

    lane256 = lax.broadcasted_iota(jnp.int32, (256, 128), 1)
    frame256 = lax.broadcasted_iota(jnp.int32, (256, 128), 0) // 8
    own = (frame256 == lane256 % NF).astype(F32)
    table = table_ref[...]
    goal = jnp.broadcast_to(table[:, :, 6:7], (NF, EDGES, 128))
    for k in range(EDGES):
        same = jnp.broadcast_to(goal[:, k : k + 1, :], (NF, EDGES, 128)).reshape(256, 128)
        rep_s[k] = (same == (lane256 % NF).astype(F32)).astype(F32) - own
    signs = (goal.reshape(256, 128) == lane256.astype(F32)).astype(F32) - (frame256 == lane256).astype(F32)
    sgnt_s[...] = jnp.transpose(signs)[:NF]
    pl.semaphore_wait(barrier, EDGES - 1 + NF - 1)

    def exchange(src_of, dst_ref, send_sem, recv_sem):
        copies = []
        for d in range(1, EDGES):
            peer = lax.rem(me_e + d, EDGES)
            copy = pltpu.make_async_remote_copy(
                src_ref=src_of(peer),
                dst_ref=dst_ref.at[me_e],
                send_sem=send_sem.at[d],
                recv_sem=recv_sem.at[d],
                device_id={"edges": peer},
                device_id_type=MESH,
            )
            copy.start()
            copies.append(copy)
        return copies

    copies = exchange(lambda peer: heads_s.at[peer], heads_r, h_send, h_recv)
    heads_r[me_e] = heads_s[me_e]
    for copy in copies:
        copy.wait()

    def component(c):
        return jnp.concatenate([heads_r[k, c : c + 1, :] for k in range(EDGES)], axis=0)

    flow_u, flow_v = component(0), component(1)
    weight_u, weight_v = sigmoid(component(2)), sigmoid(component(3))
    pix = lax.broadcasted_iota(jnp.int32, (8, SLICE), 1)
    col = (pix % WID).astype(F32)
    row = (pix // WID + me_e * ROWS).astype(F32)
    depth = depth_ref[pl.ds(me_e, 1), :]

    k_lane = lax.broadcasted_iota(jnp.int32, (48, 128), 1)
    k_row = lax.broadcasted_iota(jnp.int32, (48, 128), 0)
    same_edge = (k_lane < 56) & (k_lane % 8 == k_row % 8)
    lane32 = lax.broadcasted_iota(jnp.int32, (NF, 128), 1)
    sub32 = lax.broadcasted_iota(jnp.int32, (NF, 128), 0)
    lane8 = lax.broadcasted_iota(jnp.int32, (8, 128), 1)
    sub8 = lax.broadcasted_iota(jnp.int32, (8, 128), 0)

    goal = jnp.broadcast_to(table_ref[me_f][:, 6:7], (8, 128))
    sgn = (goal == lane8.astype(F32)).astype(F32) - (lane8 == me_f).astype(F32)
    first = table_ref[:, 0, :]
    poses = [
        jnp.sum(jnp.where(lane32 == sub32, jnp.broadcast_to(first[:, c : c + 1], (NF, 128)), 0.0), axis=0, keepdims=True)
        for c in range(6)
    ]
    poses = jnp.concatenate(poses + [jnp.zeros((2, 128), F32)], axis=0)

    def along_edges(vector):
        return jnp.sum(sgn * vector, axis=1, keepdims=True)

    for it in range(ITERS):
        rel = [along_edges(poses[c : c + 1, :]) for c in range(6)]
        jac_u, jac_v, scaled_u, scaled_v, resid_u, resid_v, cross, curve, depth_grad = edge_terms(
            rel, depth, flow_u, flow_v, weight_u, weight_v, col, row
        )
        frame_curve = jnp.sum(curve, axis=0, keepdims=True)
        frame_grad = jnp.sum(depth_grad, axis=0, keepdims=True)
        inv_damped = 1.0 / ((1.0 + DEPTH_DAMPING) * frame_curve + DEPTH_FLOOR)
        lead = jnp.concatenate([jnp.concatenate(scaled_u, axis=0), jnp.concatenate(scaled_v, axis=0)], axis=1)
        pad = jnp.zeros((72, 2 * SLICE), F32)
        trail = jnp.concatenate(
            [
                jnp.concatenate([jnp.concatenate(jac_u, axis=0), jnp.concatenate(jac_v, axis=0)], axis=1),
                jnp.concatenate([resid_u, resid_v], axis=1),
                pad,
            ],
            axis=0,
        )
        hess = dot_nt(lead, trail, HIGHEST)
        stack = jnp.concatenate(cross, axis=0)
        right = jnp.concatenate(
            [stack, jnp.broadcast_to(frame_grad, (8, SLICE)) * (sub_row(8, SLICE) == 0).astype(F32), pad[:, :SLICE]],
            axis=0,
        )
        schur = dot_nt(stack * inv_damped, right, HIGHEST)
        small = jnp.where(same_edge, hess, 0.0) - schur
        for c in range(6):
            k_s[it, c] = small[8 * c : 8 * c + 8]
        for c in range(6, 8):
            k_s[it, c] = jnp.zeros((8, 128), F32)
        copies = exchange(lambda peer: k_s.at[it, peer], k_r.at[it], k_send.at[it], k_recv.at[it])
        k_r[it, me_e] = k_s[it, me_e]
        for copy in copies:
            copy.wait()
        total = k_r[it, 0]
        for e in range(1, EDGES):
            total = total + k_r[it, e]
        f_s[it] = total
        f_r[it, me_f] = total

        def frame_copy(d):
            return pltpu.make_async_remote_copy(
                src_ref=f_s.at[it],
                dst_ref=f_r.at[it, me_f],
                send_sem=f_send.at[it, d],
                recv_sem=f_recv.at[it, d],
                device_id={"frames": lax.rem(me_f + d, NF)},
                device_id_type=MESH,
            )

        def send(d, carry):
            frame_copy(d).start()
            return carry

        def arrive(d, carry):
            frame_copy(d).wait()
            return carry

        lax.fori_loop(1, NF, send, 0)
        lax.fori_loop(1, NF, arrive, 0)

        blocks = f_r[it].reshape(256, 128)
        left_sum = jnp.zeros((256, 128), F32)
        right_sum = jnp.zeros((256, 128), F32)
        for k in range(EDGES):
            rep = rep_s[k]
            left_sum = left_sum + jnp.take_along_axis(blocks, (lane256 // 32) * 8 + k, axis=1) * rep
            right_sum = right_sum + jnp.take_along_axis(blocks, (lane256 // 32) % 2 * 8 + 32 + k, axis=1) * rep
        rhs = jnp.sum(jnp.where((lane256 >= 48) & (lane256 < 56), blocks, 0.0), axis=1, keepdims=True)
        right_sum = jnp.where(lane256 < 64, right_sum, jnp.where(lane256 == 64, rhs, 0.0))
        row_s[it] = jnp.concatenate(
            [
                jnp.dot(sgnt_s[...], left_sum, precision=HIGHEST, preferred_element_type=F32),
                jnp.dot(sgnt_s[...], right_sum, precision=HIGHEST, preferred_element_type=F32),
            ],
            axis=1,
        )
        copies = exchange(lambda peer: row_s.at[it], row_r.at[it], r_send.at[it], r_recv.at[it])
        row_r[it, me_e] = row_s[it]
        for copy in copies:
            copy.wait()

        for c in range(6):
            for t in range(2):
                v = row_r[it, c, :, 128 * t : 128 * t + 128]
                diag = lane32 + 128 * t == sub32 + 32 * c
                mat[32 * c : 32 * c + 32, 128 * t : 128 * t + 128] = v + jnp.where(
                    diag, POSE_DAMPING * v + POSE_FLOOR, 0.0
                )

        rows = stack_rows(pivot_rows([mat[0:8, 0:128], mat[0:8, 128:256]]))
        rows = eliminate(mat, 0, 9, rows)
        eliminate(mat, 9, UNK // 8, rows[:1])

        steps = []
        for c in range(6):
            v = jnp.broadcast_to(mat[32 * c : 32 * c + 32, 0:1], (NF, 128))
            steps.append(jnp.sum(jnp.where(lane32 == sub32, v, 0.0), axis=0, keepdims=True))
        along = jnp.zeros((8, SLICE), F32)
        for c in range(6):
            along = along + along_edges(steps[c]) * cross[c]
        along = jnp.sum(along, axis=0, keepdims=True)
        poses = poses + jnp.concatenate(steps + [jnp.zeros((2, 128), F32)], axis=0)
        depth = depth + (frame_grad - along) * inv_damped

    pose_out[...] = jnp.broadcast_to(
        jnp.sum(jnp.where(lane8 == me_f, poses, 0.0), axis=1, keepdims=True), (8, 128)
    )
    d_s[...] = jnp.broadcast_to(depth, (8, SLICE))
    copies = exchange(lambda peer: d_s, depth_out, d_send, d_recv)
    depth_out[me_e] = d_s[...]
    for copy in copies:
        copy.wait()


def sub_row(rows, cols):
    return lax.broadcasted_iota(jnp.int32, (rows, cols), 0)


def gauss_newton(heads, inv_depth, table):
    vmem = pl.BlockSpec(memory_space=pltpu.VMEM)
    dma = pltpu.SemaphoreType.DMA
    pose_out, depth_out = pl.pallas_call(
        gn_kernel,
        out_shape=(
            jax.ShapeDtypeStruct((8, 128), F32),
            jax.ShapeDtypeStruct((EDGES, 8, SLICE), F32),
        ),
        in_specs=[vmem] * 3,
        out_specs=(vmem, vmem),
        scratch_shapes=[
            pltpu.VMEM((EDGES, 8, SLICE), F32),
            pltpu.VMEM((ITERS, 8, 8, 128), F32),
            pltpu.VMEM((ITERS, 8, 8, 128), F32),
            pltpu.VMEM((ITERS, 8, 128), F32),
            pltpu.VMEM((ITERS, NF, 8, 128), F32),
            pltpu.VMEM((ITERS, NF, 256), F32),
            pltpu.VMEM((ITERS, EDGES, NF, 256), F32),
            pltpu.VMEM((8, SLICE), F32),
            pltpu.VMEM((EDGES, 256, 128), F32),
            pltpu.VMEM((NF, 256), F32),
            pltpu.VMEM((UNK, 256), F32),
            dma((EDGES,)),
            dma((EDGES,)),
            dma((ITERS, EDGES)),
            dma((ITERS, EDGES)),
            dma((ITERS, NF)),
            dma((ITERS, NF)),
            dma((ITERS, EDGES)),
            dma((ITERS, EDGES)),
            dma((EDGES,)),
            dma((EDGES,)),
        ],
        compiler_params=pltpu.CompilerParams(
            vmem_limit_bytes=32 * 1024 * 1024, collective_id=1, has_side_effects=True
        ),
        name="gauss_newton",
    )(heads, table, inv_depth.reshape(EDGES, SLICE))
    return pose_out[:6, :1], depth_out[:, 0, :].reshape(1, PIX)


def per_device(fmap, context, poses, inv_depth, targets, w_corr, w_gates, w_cand, w_head):
    target, table = gather(fmap[0], poses, targets)
    hidden, heads = update(fmap[0], target.reshape(PIX, CH), context[0], w_corr, w_gates, w_cand, w_head)
    new_poses, new_depth = gauss_newton(heads, inv_depth, table)
    return new_poses, new_depth, hidden[None]


def solution(mesh):
    return jax.shard_map(
        per_device,
        mesh=mesh,
        in_specs=(
            P("frames", None, None),
            P("frames", None, None),
            P(None, "frames"),
            P("frames", None),
            P(("frames", "edges")),
            P(),
            P(),
            P(),
            P(),
        ),
        out_specs=(P(None, "frames"), P("frames", None), P(("frames", "edges"), None, None)),
        check_vma=False,
    )
```

```python
import functools
import math

import jax
import jax.numpy as jnp
from jax import lax
from jax.experimental import pallas as pl
from jax.experimental.pallas import tpu as pltpu
from jax.sharding import PartitionSpec as P

HGT = 48
WID = 64
CH = 128
LEVELS = 4
RADIUS = 3
ITERS = 2
PIX = HGT * WID
NF = 32
EDGES = 8
SLICE = PIX // EDGES
ROWS = SLICE // WID
UNK = 6 * NF

FOCAL = 50.0
POSE_DAMPING = 0.1
POSE_FLOOR = 1.0
DEPTH_DAMPING = 0.1
DEPTH_FLOOR = 1.0
HIGHEST = lax.Precision.HIGHEST
F32 = jnp.float32
BF16 = jnp.bfloat16
MESH = pl.DeviceIdType.MESH


def dot_nt(a, b, precision=None):
    return lax.dot_general(a, b, (((1,), (1,)), ((), ())), precision=precision, preferred_element_type=F32)


HALF = SLICE // 2
XS = 4
ZS = NF // XS
FAR_EDGES = sorted(
    [(dy, dc) for dy in range(4) for dc in range(2) if dy + dc > 0], key=lambda d: -(2 * min(d[0], 4 - d[0]) + d[1])
)
FAR_FRAMES = sorted(
    [(dx, dz) for dx in range(XS) for dz in range(ZS) if dx + dz > 0],
    key=lambda d: -(min(d[0], XS - d[0]) + min(d[1], ZS - d[1])),
)


def gather_kernel(
    fmap_ref, pose_ref, goal_ref, out_ref, table_ref,
    maps_a, maps_b, chosen_a, chosen_b, goals_s, goals_r, goals_v, goals_m,
    own_sem, g_send, g_recv, tx_send, tx_recv, tz_send, tz_recv, zr_send, zr_recv, zl_send, zl_recv,
    xa_send, xa_recv, xb_send, xb_recv, wr_send, wr_recv, wl_send, wl_recv,
    ca_send, ca_recv, cb_send, cb_recv, m_sem,
):
    me_f = lax.axis_index("frames")
    me_e = lax.axis_index("edges")
    x, z = me_f // ZS, lax.rem(me_f, ZS)

    def frame(dx, dz):
        return {"frames": lax.rem(x + dx, XS) * ZS + lax.rem(z + dz, ZS)}

    edge_peers = [lax.rem(me_e // 2 + dy, EDGES // 2) * 2 + lax.rem(me_e + dc, 2) for dy, dc in FAR_EDGES]

    own = []
    for h, maps in enumerate((maps_a, maps_b)):
        copy = pltpu.make_async_copy(
            fmap_ref.at[pl.ds(pl.multiple_of(me_e * SLICE + h * HALF, HALF), HALF)], maps.at[x, z], own_sem.at[h]
        )
        copy.start()
        own.append(copy)

    barrier = pltpu.get_barrier_semaphore()
    for dz in (4, 3, 5, 2, 6, 1, 7):
        pl.semaphore_signal(barrier, inc=1, device_id=frame(0, dz), device_id_type=MESH)
    for dx in (2, 1, 3):
        pl.semaphore_signal(barrier, inc=1, device_id=frame(dx, 0), device_id_type=MESH)
    for peer in edge_peers:
        pl.semaphore_signal(barrier, inc=1, device_id={"edges": peer}, device_id_type=MESH)
    goals_s[...] = jnp.full((8, 128), goal_ref[0], jnp.int32)
    goals_r[me_e] = goals_s[...]
    for copy in own:
        copy.wait()
    pl.semaphore_wait(barrier, ZS - 1 + XS - 1 + EDGES - 1)

    def send(src, dst, send_sem, recv_sem, peer):
        copy = pltpu.make_async_remote_copy(
            src_ref=src, dst_ref=dst, send_sem=send_sem, recv_sem=recv_sem, device_id=peer, device_id_type=MESH
        )
        copy.start()
        return copy

    right, left = frame(0, 1), frame(0, ZS - 1)

    def passed_on(maps, column, s, way):
        zz = lax.rem(z + (ZS - s if way else s), ZS)
        if s < 3:
            return maps.at[column, zz]
        return maps.at[column, zz, pl.ds(0 if way else HALF // 2, HALF // 2)]

    def ring(s, way):
        ref = passed_on(maps_a, x, s, way)
        if way:
            return send(ref, ref, zr_send.at[s], zr_recv.at[s], right)
        return send(ref, ref, zl_send.at[s], zl_recv.at[s], left)

    def across(zz, order):
        ref = maps_a.at[x, zz]
        return [
            send(ref, ref, xa_send.at[d - 1, order], xa_recv.at[d - 1, order], frame(d, 0)) for d in (2, 1, 3)
        ]

    def ring_wide(s, way, c):
        ref = passed_on(maps_b, lax.rem(x + c, XS), s, way)
        if way:
            return send(ref, ref, wr_send.at[s, c], wr_recv.at[s, c], right)
        return send(ref, ref, wl_send.at[s, c], wl_recv.at[s, c], left)

    xb = []
    for d in (2, 1, 3):
        ref = maps_b.at[x, z]
        xb.append(send(ref, ref, xb_send.at[d - 1], xb_recv.at[d - 1], frame(d, 0)))
    zr, zl = [ring(0, True)], [ring(0, False)]
    wr = [[None] * XS for _ in range(4)]
    wl = [[None] * XS for _ in range(4)]
    wr[0][0], wl[0][0] = ring_wide(0, True, 0), ring_wide(0, False, 0)
    goal_copies = [
        send(goals_s, goals_r.at[me_e], g_send.at[d], g_recv.at[d], {"edges": peer})
        for d, peer in enumerate(edge_peers)
    ]
    xa = across(z, 0)
    by_distance = dict(zip((2, 1, 3), xb))
    for c in (1, 3, 2):
        by_distance[XS - c].wait_recv()
        wr[0][c], wl[0][c] = ring_wide(0, True, c), ring_wide(0, False, c)

    for s in range(1, 4):
        zr[s - 1].wait_recv()
        zr.append(ring(s, True))
        xa += across(lax.rem(z + ZS - s, ZS), 2 * s - 1)
        zl[s - 1].wait_recv()
        zl.append(ring(s, False))
        xa += across(lax.rem(z + s, ZS), 2 * s)
        for c in (0, 1, 3, 2):
            wr[s - 1][c].wait_recv()
            wr[s][c] = ring_wide(s, True, c)
            wl[s - 1][c].wait_recv()
            wl[s][c] = ring_wide(s, False, c)
        if s == 1:
            for copy in goal_copies:
                copy.wait()
            goals = jnp.concatenate([goals_r[k, 0:1, :] for k in range(EDGES)], axis=0)
            goals_v[...] = goals
            to_scalar = pltpu.make_async_copy(goals_v, goals_m, m_sem)
            to_scalar.start()
            lane = lax.broadcasted_iota(jnp.int32, (8, 128), 1)
            tile = jnp.where(lane == 6, goals.astype(F32), 0.0)
            for c in range(6):
                tile = jnp.where(lane == c, pose_ref[0, c], tile)
            table_ref[z, x] = tile
            ref = table_ref.at[z, x]
            tx = [send(ref, ref, tx_send.at[d], tx_recv.at[d], frame(d, 0)) for d in (2, 1, 3)]
    zr[3].wait_recv()
    zl[3].wait_recv()
    xa += across(lax.rem(z + 4, ZS), 7)
    for copy in tx:
        copy.wait_recv()
    ref = table_ref.at[z]
    tz = [send(ref, ref, tz_send.at[d], tz_recv.at[d], frame(0, d)) for d in (4, 3, 5, 2, 6, 1, 7)]
    to_scalar.wait()
    for copy in xa:
        copy.wait_recv()

    def swap(maps, chosen, h, send_sem, recv_sem):
        mine = pl.ds(pl.multiple_of(me_e * SLICE + h * HALF, HALF), HALF)
        for k in range(EDGES):
            goal = goals_m[k, 0]
            chosen[k] = maps[goal // ZS, lax.rem(goal, ZS)]
        copies = [
            send(chosen.at[peer], out_ref.at[mine], send_sem.at[d], recv_sem.at[d], {"edges": peer})
            for d, peer in enumerate(edge_peers)
        ]
        out_ref[mine, :] = chosen[me_e]
        return copies

    swaps = swap(maps_a, chosen_a, 0, ca_send, ca_recv)
    for c in range(XS):
        wr[3][c].wait_recv()
        wl[3][c].wait_recv()
    swaps += swap(maps_b, chosen_b, 1, cb_send, cb_recv)
    for copy in tz:
        copy.wait_recv()
    for copy in swaps:
        copy.wait_recv()
    for copy in zr + zl + xa + xb + sum(wr, []) + sum(wl, []) + tx + tz + swaps:
        copy.wait_send()


def gather(fmap, poses, targets):
    vmem = pl.BlockSpec(memory_space=pltpu.VMEM)
    dma = pltpu.SemaphoreType.DMA
    return pl.pallas_call(
        gather_kernel,
        out_shape=(
            jax.ShapeDtypeStruct((PIX, CH), BF16),
            jax.ShapeDtypeStruct((ZS, XS, 8, 128), F32),
        ),
        in_specs=[
            pl.BlockSpec(memory_space=pl.ANY),
            pl.BlockSpec(memory_space=pltpu.SMEM),
            pl.BlockSpec(memory_space=pltpu.SMEM),
        ],
        out_specs=(vmem, vmem),
        scratch_shapes=[
            pltpu.VMEM((XS, ZS, HALF, CH), BF16),
            pltpu.VMEM((XS, ZS, HALF, CH), BF16),
            pltpu.VMEM((EDGES, HALF, CH), BF16),
            pltpu.VMEM((EDGES, HALF, CH), BF16),
            pltpu.VMEM((8, 128), jnp.int32),
            pltpu.VMEM((EDGES, 8, 128), jnp.int32),
            pltpu.VMEM((8, 128), jnp.int32),
            pltpu.SMEM((8, 128), jnp.int32),
            dma((2,)),
            dma((EDGES,)),
            dma((EDGES,)),
            dma((XS,)),
            dma((XS,)),
            dma((ZS,)),
            dma((ZS,)),
            dma((4,)),
            dma((4,)),
            dma((4,)),
            dma((4,)),
            dma((3, 8)),
            dma((3, 8)),
            dma((3,)),
            dma((3,)),
            dma((4, XS)),
            dma((4, XS)),
            dma((4, XS)),
            dma((4, XS)),
            dma((EDGES,)),
            dma((EDGES,)),
            dma((EDGES,)),
            dma((EDGES,)),
            dma(()),
        ],
        compiler_params=pltpu.CompilerParams(
            vmem_limit_bytes=60 * 1024 * 1024, collective_id=2, has_side_effects=True
        ),
        name="gather_maps",
    )(fmap, poses.T, targets)


def update_kernel(
    src_hbm, tgt_hbm, ctx_hbm, wg_hbm, wc_hbm, w_ref, wh_ref, hid_ref, heads_ref,
    src_ref, ctx_ref, wg_ref, wc_ref, wd_ref, w_slot, p0, p1, p2, p3, t1, f1, t2, f2, t3, sm, rm, upd, sems,
):
    loads = [
        pltpu.make_async_copy(a, b, sems.at[i])
        for i, (a, b) in enumerate(
            (
                (tgt_hbm, p0.at[pl.ds(192, PIX)]),
                (src_hbm, src_ref),
                (ctx_hbm, ctx_ref),
                (wg_hbm, wg_ref),
                (wc_hbm.at[0], wc_ref.at[:, pl.ds(0, CH)]),
                (wc_hbm.at[1], wc_ref.at[:, pl.ds(CH, CH)]),
                (wc_hbm.at[2], wd_ref),
            )
        )
    ]
    for load in loads:
        load.start()
    for g in range(4 * 7):
        w_slot[8 * g : 8 * g + 8] = jnp.concatenate(
            [w_ref[7 * g : 7 * g + 7].astype(F32), jnp.zeros((1, CH), F32)], axis=0
        )
    w_slots = w_slot[...].astype(BF16)
    w_head = jnp.concatenate([wh_ref[...].astype(F32), jnp.zeros((4, CH), F32)], axis=0).astype(BF16)
    zero = jnp.zeros((3 * WID, CH), BF16)
    p0[pl.ds(0, 192), :] = zero
    p0[pl.ds(51 * 64, 192), :] = zero
    p1[pl.ds(0, 96), :] = zero[:96]
    p1[pl.ds(27 * 32, 96), :] = zero[:96]
    p2[pl.ds(0, 48), :] = zero[:48]
    p2[pl.ds(15 * 16, 48), :] = zero[:48]
    p3[pl.ds(0, 24), :] = jnp.zeros((24, CH), F32)
    p3[pl.ds(9 * 8, 24), :] = jnp.zeros((24, CH), F32)
    edge = jnp.zeros((WID, 6 * CH), BF16)
    for ref in (sm, rm):
        ref[pl.ds(0, WID), :] = edge
        ref[pl.ds(PIX + WID, WID), :] = edge

    loads[0].wait()

    def fold_rows(r, carry):
        a = p0[pl.ds(r * 128 + 192, 64), :].astype(F32)
        b = p0[pl.ds(r * 128 + 256, 64), :].astype(F32)
        t1[pl.ds(r * 64, 64), :] = a + b
        return carry

    lax.fori_loop(0, HGT // 2, fold_rows, 0)
    f1[...] = 0.25 * (t1[pl.ds(0, 768, stride=2), :] + t1[pl.ds(1, 768, stride=2), :])
    p1[pl.ds(96, 768), :] = f1[...].astype(BF16)
    half = f1[...].reshape(12, 2, 32, CH)
    t2[...] = (half[:, 0] + half[:, 1]).reshape(384, CH)
    f2[...] = 0.25 * (t2[pl.ds(0, 192, stride=2), :] + t2[pl.ds(1, 192, stride=2), :])
    p2[pl.ds(48, 192), :] = f2[...].astype(BF16)
    half = f2[...].reshape(6, 2, 16, CH)
    t3[...] = (half[:, 0] + half[:, 1]).reshape(96, CH)
    f3 = 0.25 * (t3[pl.ds(0, 48, stride=2), :] + t3[pl.ds(1, 48, stride=2), :])
    p3[pl.ds(24, 48), :] = f3.astype(BF16).astype(F32)

    lane = lax.broadcasted_iota(jnp.int32, (8, 128), 1)
    sub = lax.broadcasted_iota(jnp.int32, (8, 128), 0)
    col = lane % WID
    scale = 1.0 / math.sqrt(CH)

    def rotate(x, level):
        amount = ((col >> level) + 5) % 8
        for bit in (1, 2, 4):
            x = jnp.where((amount // bit) % 2 == 1, pltpu.roll(x, 8 - bit, 0), x)
        return x

    def pick(vol, groups, level):
        acc = jnp.zeros((8, 128), F32)
        for g in range(groups):
            acc = jnp.where(jnp.abs(8 * g + sub - (col >> level)) <= RADIUS, vol[8 * g : 8 * g + 8], acc)
        return acc

    def spread(refs, start, lead, value):
        rows = value.shape[0]
        column = lax.broadcasted_iota(jnp.int32, value.shape, 0) % WID
        before = jnp.where(column == 0, 0.0, pltpu.roll(value, 1, 0))
        after = jnp.where(column == WID - 1, 0.0, pltpu.roll(value, rows - 1, 0))
        for dx, v in enumerate((before, value, after)):
            v = v.astype(BF16)
            for ref in refs:
                ref[pl.ds(start + WID, rows), 2 * CH * dx + lead : 2 * CH * dx + lead + CH] = v

    def block(q, carry):
        src = src_ref[pl.ds(q * 128, 128), :]
        parts = []
        vol = dot_nt(p0[pl.ds(q * 128, 512), :], src)
        rows = [pick(vol[64 * a : 64 * a + 64], 8, 0) for a in range(8)]
        for a in range(7):
            parts.append(rotate(jnp.where(lane < WID, rows[a], rows[a + 1]), 0))
        vol = dot_nt(p1[pl.ds(q * 32, 224), :], src)
        for a in range(7):
            parts.append(rotate(pick(vol[32 * a : 32 * a + 32], 4, 1), 1))
        vol = dot_nt(p2[pl.ds((q // 2) * 16, 112), :], src)
        for a in range(7):
            parts.append(rotate(pick(vol[16 * a : 16 * a + 16], 2, 2), 2))
        vol = dot_nt(p3[pl.ds((q // 4) * 8, 56), :].astype(BF16), src)
        for a in range(7):
            parts.append(rotate(pick(vol[8 * a : 8 * a + 8], 1, 3), 3))
        corr = (jnp.concatenate(parts, axis=0) * scale).astype(BF16)
        enc = lax.dot_general(corr, w_slots, (((0,), (0,)), ((), ())), preferred_element_type=F32)
        start = pl.multiple_of(q * 128, 128)
        ctx = ctx_ref[pl.ds(start, 128), :].astype(F32)
        motion = jnp.maximum(enc, 0.0) + jnp.maximum(ctx[:, CH:], 0.0)
        spread((sm, rm), start, CH, motion.astype(BF16).astype(F32))
        state = jnp.tanh(ctx[:, :CH]).astype(BF16).astype(F32)
        spread((sm,), start, 0, state)
        return carry

    loads[1].wait()
    loads[2].wait()
    lax.fori_loop(0, PIX // 128, block, 0, unroll=4)
    for load in loads[3:]:
        load.wait()

    def gates(t, carry):
        start = pl.multiple_of(t * SLICE, SLICE)
        acc = jnp.zeros((SLICE, 2 * CH), F32)
        for dy in range(3):
            acc = acc + jnp.dot(sm[pl.ds(start + WID * dy, SLICE), :], wg_ref[dy], preferred_element_type=F32)
        gate = 0.5 * jnp.tanh(0.5 * acc) + 0.5
        upd[pl.ds(start, SLICE), :] = gate[:, :CH]
        state = sm[pl.ds(start + WID, SLICE), 2 * CH : 3 * CH].astype(F32)
        spread((rm,), start, 0, (gate[:, CH:] * state).astype(BF16).astype(F32))
        return carry

    lax.fori_loop(0, EDGES, gates, 0)

    def blend(t, carry):
        start = pl.multiple_of(t * SLICE, SLICE)
        both = jnp.dot(rm[pl.ds(start, SLICE + WID), :], wc_ref[...], preferred_element_type=F32)
        last = jnp.dot(rm[pl.ds(start + 2 * WID, SLICE), :], wd_ref[...], preferred_element_type=F32)
        acc = both[:SLICE, :CH] + both[WID:, CH:] + last
        update = upd[pl.ds(start, SLICE), :]
        state = sm[pl.ds(start + WID, SLICE), 2 * CH : 3 * CH].astype(F32)
        hidden = ((1.0 - update) * state + update * jnp.tanh(acc)).astype(BF16)
        hid_ref[pl.ds(start, SLICE), :] = hidden
        return carry

    lax.fori_loop(0, EDGES, blend, 0)
    for t in range(EDGES):
        heads_ref[t] = dot_nt(w_head, hid_ref[pl.ds(t * SLICE, SLICE), :])


def update(source, target, context, w_corr, w_gates, w_cand, w_head):
    vmem = pl.BlockSpec(memory_space=pltpu.VMEM)
    return pl.pallas_call(
        update_kernel,
        out_shape=(jax.ShapeDtypeStruct((PIX, CH), BF16), jax.ShapeDtypeStruct((EDGES, 8, SLICE), F32)),
        in_specs=[pl.BlockSpec(memory_space=pl.ANY)] * 5 + [vmem] * 2,
        out_specs=(vmem, vmem),
        scratch_shapes=[
            pltpu.VMEM((PIX, CH), BF16),
            pltpu.VMEM((PIX, 2 * CH), BF16),
            pltpu.VMEM((3, 6 * CH, 2 * CH), BF16),
            pltpu.VMEM((6 * CH, 2 * CH), BF16),
            pltpu.VMEM((6 * CH, CH), BF16),
            pltpu.VMEM((224, CH), F32),
            pltpu.VMEM((54 * 64, CH), BF16),
            pltpu.VMEM((30 * 32, CH), BF16),
            pltpu.VMEM((18 * 16, CH), BF16),
            pltpu.VMEM((12 * 8, CH), F32),
            pltpu.VMEM((1536, CH), F32),
            pltpu.VMEM((768, CH), F32),
            pltpu.VMEM((384, CH), F32),
            pltpu.VMEM((192, CH), F32),
            pltpu.VMEM((96, CH), F32),
            pltpu.VMEM((PIX + 2 * WID, 6 * CH), BF16),
            pltpu.VMEM((PIX + 2 * WID, 6 * CH), BF16),
            pltpu.VMEM((PIX, CH), F32),
            pltpu.SemaphoreType.DMA((7,)),
        ],
        compiler_params=pltpu.CompilerParams(vmem_limit_bytes=60 * 1024 * 1024),
        cost_estimate=pl.CostEstimate(flops=7_000_000_000, bytes_accessed=6_500_000, transcendentals=2_000_000),
        name="edge_update",
    )(
        source, target, context, w_gates.reshape(3, 6 * CH, 2 * CH), w_cand.reshape(3, 6 * CH, CH), w_corr, w_head.T
    )


def sigmoid(x):
    return 1.0 / (1.0 + jnp.exp(-x))


def edge_terms(rel, depth, flow_u, flow_v, weight_u, weight_v, col, row):
    center_x = (WID - 1) / 2.0
    center_y = (HGT - 1) / 2.0
    ray_x = (col - center_x) / FOCAL
    ray_y = (row - center_y) / FOCAL
    move_x, move_y, move_z, turn_x, turn_y, turn_z = rel
    point_x = ray_x + turn_y - turn_z * ray_y + depth * move_x
    point_y = ray_y + turn_z * ray_x - turn_x + depth * move_y
    point_z = 1.0 + turn_x * ray_y - turn_y * ray_x + depth * move_z
    inverse_z = 1.0 / point_z
    slope = FOCAL * inverse_z
    bend_u = -FOCAL * point_x * inverse_z * inverse_z
    bend_v = -FOCAL * point_y * inverse_z * inverse_z
    resid_u = col + flow_u - (FOCAL * point_x * inverse_z + center_x)
    resid_v = row + flow_v - (FOCAL * point_y * inverse_z + center_y)
    blank = jnp.zeros_like(slope)
    jac_u = [depth * slope, blank, depth * bend_u, bend_u * ray_y, slope - bend_u * ray_x, -slope * ray_y]
    jac_v = [blank, depth * slope, depth * bend_v, bend_v * ray_y - slope, -bend_v * ray_x, slope * ray_x]
    depth_u = slope * move_x + bend_u * move_z
    depth_v = slope * move_y + bend_v * move_z
    scaled_u = [j * weight_u for j in jac_u]
    scaled_v = [j * weight_v for j in jac_v]
    cross = [scaled_u[c] * depth_u + scaled_v[c] * depth_v for c in range(6)]
    curve = weight_u * depth_u * depth_u + weight_v * depth_v * depth_v
    depth_grad = weight_u * depth_u * resid_u + weight_v * depth_v * resid_v
    return jac_u, jac_v, scaled_u, scaled_v, resid_u, resid_v, cross, curve, depth_grad


def reciprocal(x):
    r = pl.reciprocal(x, approx=True)
    r = r * (2.0 - x * r)
    return r * (2.0 - x * r)


def pivot_rows(panel, lead, first):
    tiles = len(panel)
    s = [
        [jnp.broadcast_to(lead[i : i + 1, first + j : first + j + 1], (8, 128)) for j in range(i + 1)]
        for i in range(8)
    ]
    x = [[jnp.broadcast_to(v[i : i + 1, :], (8, 128)) for v in panel] for i in range(8)]
    low = [[None] * 8 for _ in range(8)]
    inv = []
    for j in range(0, 8, 2):
        k = j + 1
        r = reciprocal(s[j][j] * s[k][k] - s[k][j] * s[k][j])
        a, b, c = s[k][k] * r, -s[k][j] * r, s[j][j] * r
        inv.append((a, b, c))
        for i in range(k + 1, 8):
            low[i][j] = s[i][j] * a + s[i][k] * b
            low[i][k] = s[i][j] * b + s[i][k] * c
        for i in range(k + 1, 8):
            for m in range(k + 1, i + 1):
                s[i][m] = s[i][m] - (low[i][j] * s[m][j] + low[i][k] * s[m][k])
    for i in range(2, 8):
        for j in range(i - i % 2):
            x[i] = [x[i][t] - low[i][j] * x[j][t] for t in range(tiles)]
    for j in range(0, 8, 2):
        a, b, c = inv[j // 2]
        u, v = x[j], x[j + 1]
        x[j] = [a * u[t] + b * v[t] for t in range(tiles)]
        x[j + 1] = [b * u[t] + c * v[t] for t in range(tiles)]
    for i in range(5, -1, -1):
        for j in range(7, i + 1 - i % 2, -1):
            x[i] = [x[i][t] - low[j][i] * x[j][t] for t in range(tiles)]
    return x


def stack_rows(x):
    sub = lax.broadcasted_iota(jnp.int32, (8, 128), 0)
    out = []
    for t in range(len(x[0])):
        v = x[0][t]
        for i in range(1, 8):
            v = jnp.where(sub == i, x[i][t], v)
        out.append(v)
    return tuple(out)


def shift_lanes(vals):
    lane = lax.broadcasted_iota(jnp.int32, (1, 128), 1)
    rolled = [pltpu.roll(v, 120, 1) for v in vals]
    return [
        v if t == len(vals) - 1 else jnp.where(lane < 120, v, rolled[t + 1]) for t, v in enumerate(rolled)
    ]


def eliminate(mat, first, last, rows):
    tiles = len(rows)
    cols = [slice(128 * t, 128 * t + 128) for t in range(tiles)]

    def step(p, own):
        base = pl.multiple_of(p * 8, 8)
        after = pl.multiple_of(jnp.minimum(p + 1, UNK // 8 - 1) * 8, 8)
        panel = [mat[pl.ds(after, 8), c] for c in cols]
        factors = [jnp.broadcast_to(panel[0][:, i : i + 1], (8, 128)) for i in range(8)]
        ahead = []
        for t in range(tiles):
            q = [factors[i] * jnp.broadcast_to(own[t][i : i + 1], (8, 128)) for i in range(8)]
            ahead.append(panel[t] - (((q[0] + q[1]) + (q[2] + q[3])) + ((q[4] + q[5]) + (q[6] + q[7]))))
        fresh = stack_rows(pivot_rows(shift_lanes(ahead), ahead[0], 8))
        wide = jnp.concatenate([jnp.concatenate(own, axis=1), jnp.zeros((120, 128 * tiles), F32)], axis=0)
        change = jnp.dot(mat[:, 0:128], wide, precision=HIGHEST, preferred_element_type=F32)
        vals = shift_lanes([mat[:, c] - change[:, c] for c in cols])
        mine = shift_lanes(list(own))
        for t in range(tiles):
            mat[:, cols[t]] = vals[t]
        for t in range(tiles):
            mat[pl.ds(base, 8), cols[t]] = mine[t]
        return fresh

    return lax.fori_loop(first, last, step, tuple(rows))


def gn_kernel(
    heads_s, table_ref, depth_ref,
    pose_out, depth_out,
    heads_r, k_s, k_r, f_s, f_r, row_s, row_r, d_s, rep_s, sgnt_s, mat,
    h_send, h_recv, k_send, k_recv, f_send, f_recv, r_send, r_recv, d_send, d_recv, own_sem,
):
    me_f = lax.axis_index("frames")
    me_e = lax.axis_index("edges")

    barrier = pltpu.get_barrier_semaphore()
    for d in range(1, EDGES):
        pl.semaphore_signal(barrier, inc=1, device_id={"edges": lax.rem(me_e + d, EDGES)}, device_id_type=MESH)

    def greet(d, carry):
        pl.semaphore_signal(barrier, inc=1, device_id={"frames": lax.rem(me_f + d, NF)}, device_id_type=MESH)
        return carry

    lax.fori_loop(1, NF, greet, 0)

    lane256 = lax.broadcasted_iota(jnp.int32, (256, 128), 1)
    frame256 = lax.broadcasted_iota(jnp.int32, (256, 128), 0) // 8
    own = (frame256 == lane256 % NF).astype(F32)
    table = jnp.concatenate([table_ref[:, c] for c in range(XS)], axis=0)
    goal = jnp.broadcast_to(table[:, :, 6:7], (NF, EDGES, 128))
    for k in range(EDGES):
        same = jnp.broadcast_to(goal[:, k : k + 1, :], (NF, EDGES, 128)).reshape(256, 128)
        rep_s[k] = (same == (lane256 % NF).astype(F32)).astype(F32) - own
    signs = (goal.reshape(256, 128) == lane256.astype(F32)).astype(F32) - (frame256 == lane256).astype(F32)
    sgnt_s[...] = jnp.transpose(signs)[:NF]
    pl.semaphore_wait(barrier, EDGES - 1 + NF - 1)

    def exchange(src_of, dst_ref, send_sem, recv_sem):
        copies = []
        for d, (dy, dc) in enumerate(FAR_EDGES):
            peer = lax.rem(me_e // 2 + dy, EDGES // 2) * 2 + lax.rem(me_e + dc, 2)
            copy = pltpu.make_async_remote_copy(
                src_ref=src_of(peer),
                dst_ref=dst_ref,
                send_sem=send_sem.at[d],
                recv_sem=recv_sem.at[d],
                device_id={"edges": peer},
                device_id_type=MESH,
            )
            copy.start()
            copies.append(copy)
        return copies

    copies = exchange(lambda peer: heads_s.at[peer], heads_r.at[me_e], h_send, h_recv)
    own_heads = pltpu.make_async_copy(heads_s.at[me_e], heads_r.at[me_e], own_sem)
    own_heads.start()
    for copy in copies:
        copy.wait_recv()
    own_heads.wait()
    for copy in copies:
        copy.wait_send()

    def component(c):
        return jnp.concatenate([heads_r[k, c : c + 1, :] for k in range(EDGES)], axis=0)

    flow_u, flow_v = component(0), component(1)
    weight_u, weight_v = sigmoid(component(2)), sigmoid(component(3))
    pix = lax.broadcasted_iota(jnp.int32, (8, SLICE), 1)
    col = (pix % WID).astype(F32)
    row = (pix // WID + me_e * ROWS).astype(F32)
    depth = depth_ref[:, pl.ds(pl.multiple_of(me_e * SLICE, SLICE), SLICE)]

    k_lane = lax.broadcasted_iota(jnp.int32, (48, 128), 1)
    k_row = lax.broadcasted_iota(jnp.int32, (48, 128), 0)
    same_edge = (k_lane < 56) & (k_lane % 8 == k_row % 8)
    lane32 = lax.broadcasted_iota(jnp.int32, (NF, 128), 1)
    sub32 = lax.broadcasted_iota(jnp.int32, (NF, 128), 0)
    lane8 = lax.broadcasted_iota(jnp.int32, (8, 128), 1)
    sub8 = lax.broadcasted_iota(jnp.int32, (8, 128), 0)

    goal = jnp.broadcast_to(table_ref[lax.rem(me_f, ZS), me_f // ZS][:, 6:7], (8, 128))
    sgn = (goal == lane8.astype(F32)).astype(F32) - (lane8 == me_f).astype(F32)
    first = table[:, 0, :]
    poses = [
        jnp.sum(jnp.where(lane32 == sub32, jnp.broadcast_to(first[:, c : c + 1], (NF, 128)), 0.0), axis=0, keepdims=True)
        for c in range(6)
    ]
    poses = jnp.concatenate(poses + [jnp.zeros((2, 128), F32)], axis=0)

    def along_edges(vector):
        return jnp.sum(sgn * vector, axis=1, keepdims=True)

    for it in range(ITERS):
        rel = [along_edges(poses[c : c + 1, :]) for c in range(6)]
        jac_u, jac_v, scaled_u, scaled_v, resid_u, resid_v, cross, curve, depth_grad = edge_terms(
            rel, depth, flow_u, flow_v, weight_u, weight_v, col, row
        )
        frame_curve = jnp.sum(curve, axis=0, keepdims=True)
        frame_grad = jnp.sum(depth_grad, axis=0, keepdims=True)
        inv_damped = 1.0 / ((1.0 + DEPTH_DAMPING) * frame_curve + DEPTH_FLOOR)
        lead = jnp.concatenate([jnp.concatenate(scaled_u, axis=0), jnp.concatenate(scaled_v, axis=0)], axis=1)
        pad = jnp.zeros((72, 2 * SLICE), F32)
        trail = jnp.concatenate(
            [
                jnp.concatenate([jnp.concatenate(jac_u, axis=0), jnp.concatenate(jac_v, axis=0)], axis=1),
                jnp.concatenate([resid_u, resid_v], axis=1),
                pad,
            ],
            axis=0,
        )
        hess = dot_nt(lead, trail, HIGHEST)
        stack = jnp.concatenate(cross, axis=0)
        right = jnp.concatenate(
            [stack, jnp.broadcast_to(frame_grad, (8, SLICE)) * (sub_row(8, SLICE) == 0).astype(F32), pad[:, :SLICE]],
            axis=0,
        )
        schur = dot_nt(stack * inv_damped, right, HIGHEST)
        small = jnp.where(same_edge, hess, 0.0) - schur
        for c in range(6):
            k_s[it, c] = small[8 * c : 8 * c + 8]
        for c in range(6, 8):
            k_s[it, c] = jnp.zeros((8, 128), F32)
        copies = exchange(lambda peer: k_s.at[it, peer], k_r.at[it, me_e], k_send.at[it], k_recv.at[it])
        k_r[it, me_e] = k_s[it, me_e]
        for copy in copies:
            copy.wait()
        total = k_r[it, 0]
        for e in range(1, EDGES):
            total = total + k_r[it, e]
        f_s[it] = total
        f_r[it, me_f] = total

        copies = []
        for d, (dx, dz) in enumerate(FAR_FRAMES):
            peer = lax.rem(me_f // ZS + dx, XS) * ZS + lax.rem(me_f + dz, ZS)
            copy = pltpu.make_async_remote_copy(
                src_ref=f_s.at[it],
                dst_ref=f_r.at[it, me_f],
                send_sem=f_send.at[it, d],
                recv_sem=f_recv.at[it, d],
                device_id={"frames": peer},
                device_id_type=MESH,
            )
            copy.start()
            copies.append(copy)
        for copy in copies:
            copy.wait_recv()
        for copy in copies:
            copy.wait_send()

        blocks = f_r[it].reshape(256, 128)
        left_sum = jnp.zeros((256, 128), F32)
        right_sum = jnp.zeros((256, 128), F32)
        for k in range(EDGES):
            rep = rep_s[k]
            left_sum = left_sum + jnp.take_along_axis(blocks, (lane256 // 32) * 8 + k, axis=1) * rep
            right_sum = right_sum + jnp.take_along_axis(blocks, (lane256 // 32) % 2 * 8 + 32 + k, axis=1) * rep
        rhs = jnp.sum(jnp.where((lane256 >= 48) & (lane256 < 56), blocks, 0.0), axis=1, keepdims=True)
        right_sum = jnp.where(lane256 < 64, right_sum, jnp.where(lane256 == 64, rhs, 0.0))
        row_s[it] = jnp.concatenate(
            [
                jnp.dot(sgnt_s[...], left_sum, precision=HIGHEST, preferred_element_type=F32),
                jnp.dot(sgnt_s[...], right_sum, precision=HIGHEST, preferred_element_type=F32),
            ],
            axis=1,
        )
        copies = exchange(lambda peer: row_s.at[it], row_r.at[it, me_e], r_send.at[it], r_recv.at[it])
        row_r[it, me_e] = row_s[it]
        for copy in copies:
            copy.wait()

        for c in range(6):
            for t in range(2):
                v = row_r[it, c, :, 128 * t : 128 * t + 128]
                diag = lane32 + 128 * t == sub32 + 32 * c
                mat[32 * c : 32 * c + 32, 128 * t : 128 * t + 128] = v + jnp.where(
                    diag, POSE_DAMPING * v + POSE_FLOOR, 0.0
                )

        rows = stack_rows(pivot_rows([mat[0:8, 0:128], mat[0:8, 128:256]], mat[0:8, 0:128], 0))
        rows = eliminate(mat, 0, 9, rows)
        eliminate(mat, 9, UNK // 8, rows[:1])

        steps = []
        for c in range(6):
            v = jnp.broadcast_to(mat[32 * c : 32 * c + 32, 0:1], (NF, 128))
            steps.append(jnp.sum(jnp.where(lane32 == sub32, v, 0.0), axis=0, keepdims=True))
        along = jnp.zeros((8, SLICE), F32)
        for c in range(6):
            along = along + along_edges(steps[c]) * cross[c]
        along = jnp.sum(along, axis=0, keepdims=True)
        poses = poses + jnp.concatenate(steps + [jnp.zeros((2, 128), F32)], axis=0)
        depth = depth + (frame_grad - along) * inv_damped

    mine = jnp.sum(jnp.where(lane8 == me_f, poses, 0.0), axis=1, keepdims=True)
    pose_out[...] = jnp.sum(jnp.where(lane8 == sub_row(8, 128), mine, 0.0), axis=0, keepdims=True)
    d_s[...] = depth
    place = depth_out.at[:, pl.ds(pl.multiple_of(me_e * SLICE, SLICE), SLICE)]
    copies = exchange(lambda peer: d_s, place, d_send, d_recv)
    place[...] = depth
    for copy in copies:
        copy.wait()


def sub_row(rows, cols):
    return lax.broadcasted_iota(jnp.int32, (rows, cols), 0)


def gauss_newton(heads, inv_depth, table):
    vmem = pl.BlockSpec(memory_space=pltpu.VMEM)
    dma = pltpu.SemaphoreType.DMA
    pose_out, depth_out = pl.pallas_call(
        gn_kernel,
        out_shape=(
            jax.ShapeDtypeStruct((1, 128), F32),
            jax.ShapeDtypeStruct((1, PIX), F32),
        ),
        in_specs=[pl.BlockSpec(memory_space=pl.ANY), vmem, vmem],
        out_specs=(vmem, vmem),
        scratch_shapes=[
            pltpu.VMEM((EDGES, 8, SLICE), F32),
            pltpu.VMEM((ITERS, 8, 8, 128), F32),
            pltpu.VMEM((ITERS, 8, 8, 128), F32),
            pltpu.VMEM((ITERS, 8, 128), F32),
            pltpu.VMEM((ITERS, NF, 8, 128), F32),
            pltpu.VMEM((ITERS, NF, 256), F32),
            pltpu.VMEM((ITERS, EDGES, NF, 256), F32),
            pltpu.VMEM((1, SLICE), F32),
            pltpu.VMEM((EDGES, 256, 128), F32),
            pltpu.VMEM((NF, 256), F32),
            pltpu.VMEM((UNK, 256), F32),
            dma((EDGES,)),
            dma((EDGES,)),
            dma((ITERS, EDGES)),
            dma((ITERS, EDGES)),
            dma((ITERS, NF)),
            dma((ITERS, NF)),
            dma((ITERS, EDGES)),
            dma((ITERS, EDGES)),
            dma((EDGES,)),
            dma((EDGES,)),
            dma(()),
        ],
        compiler_params=pltpu.CompilerParams(
            vmem_limit_bytes=60 * 1024 * 1024, collective_id=1, has_side_effects=True
        ),
        name="gauss_newton",
    )(heads, table, inv_depth)
    return pose_out[:, :6].T, depth_out


def per_device(fmap, context, poses, inv_depth, targets, w_corr, w_gates, w_cand, w_head):
    target, table = gather(fmap[0], poses, targets)
    hidden, heads = update(fmap[0], target, context[0], w_corr, w_gates, w_cand, w_head)
    new_poses, new_depth = gauss_newton(heads, inv_depth, table)
    return new_poses, new_depth, hidden[None]


def solution(mesh):
    return jax.shard_map(
        per_device,
        mesh=mesh,
        in_specs=(
            P("frames", None, None),
            P("frames", None, None),
            P(None, "frames"),
            P("frames", None),
            P(("frames", "edges")),
            P(),
            P(),
            P(),
            P(),
        ),
        out_specs=(P(None, "frames"), P("frames", None), P(("frames", "edges"), None, None)),
        check_vma=False,
    )
```

```python
import functools
import math

import jax
import jax.numpy as jnp
from jax import lax
from jax.experimental import pallas as pl
from jax.experimental.pallas import tpu as pltpu
from jax.sharding import PartitionSpec as P

HGT = 48
WID = 64
CH = 128
LEVELS = 4
RADIUS = 3
ITERS = 2
PIX = HGT * WID
NF = 32
EDGES = 8
SLICE = PIX // EDGES
ROWS = SLICE // WID
TILE = PIX // 3
UNK = 6 * NF

FOCAL = 50.0
POSE_DAMPING = 0.1
POSE_FLOOR = 1.0
DEPTH_DAMPING = 0.1
DEPTH_FLOOR = 1.0
HIGHEST = lax.Precision.HIGHEST
F32 = jnp.float32
BF16 = jnp.bfloat16
MESH = pl.DeviceIdType.MESH


def dot_nt(a, b, precision=None):
    return lax.dot_general(a, b, (((1,), (1,)), ((), ())), precision=precision, preferred_element_type=F32)


PART_A = 224
PART_B = SLICE - PART_A
XS = 4
ZS = NF // XS
FAR_EDGES = sorted(
    [(dy, dc) for dy in range(4) for dc in range(2) if dy + dc > 0], key=lambda d: -(2 * min(d[0], 4 - d[0]) + d[1])
)
FAR_FRAMES = sorted(
    [(dx, dz) for dx in range(XS) for dz in range(ZS) if dx + dz > 0],
    key=lambda d: -(min(d[0], XS - d[0]) + min(d[1], ZS - d[1])),
)


def gather_kernel(
    fmap_ref, pose_ref, goal_ref, out_ref, table_ref,
    maps_a, maps_b, chosen_a, chosen_b, goals_s, goals_r, goals_v, goals_m,
    own_sem, g_send, g_recv, tx_send, tx_recv, tz_send, tz_recv, za_send, za_recv,
    xa_send, xa_recv, xb_send, xb_recv, wr_send, wr_recv, wl_send, wl_recv,
    ca_send, ca_recv, cb_send, cb_recv, m_sem,
):
    me_f = lax.axis_index("frames")
    me_e = lax.axis_index("edges")
    x, z = me_f // ZS, lax.rem(me_f, ZS)

    def frame(dx, dz):
        return {"frames": lax.rem(x + dx, XS) * ZS + lax.rem(z + dz, ZS)}

    edge_peers = [lax.rem(me_e // 2 + dy, EDGES // 2) * 2 + lax.rem(me_e + dc, 2) for dy, dc in FAR_EDGES]

    def rows_of(h):
        return pl.ds(pl.multiple_of(me_e * SLICE + h * PART_A, 32), PART_B if h else PART_A)

    own = []
    for h, maps in enumerate((maps_a, maps_b)):
        copy = pltpu.make_async_copy(fmap_ref.at[rows_of(h)], maps.at[x, z], own_sem.at[h])
        copy.start()
        own.append(copy)

    barrier = pltpu.get_barrier_semaphore()
    for dz in (4, 3, 5, 2, 6, 1, 7):
        pl.semaphore_signal(barrier, inc=1, device_id=frame(0, dz), device_id_type=MESH)
    for dx in (2, 1, 3):
        pl.semaphore_signal(barrier, inc=1, device_id=frame(dx, 0), device_id_type=MESH)
    for peer in edge_peers:
        pl.semaphore_signal(barrier, inc=1, device_id={"edges": peer}, device_id_type=MESH)
    goals_s[...] = jnp.full((8, 128), goal_ref[0], jnp.int32)
    goals_r[me_e] = goals_s[...]
    for copy in own:
        copy.wait()
    pl.semaphore_wait(barrier, ZS - 1 + XS - 1 + EDGES - 1)

    def send(src, dst, send_sem, recv_sem, peer):
        copy = pltpu.make_async_remote_copy(
            src_ref=src, dst_ref=dst, send_sem=send_sem, recv_sem=recv_sem, device_id=peer, device_id_type=MESH
        )
        copy.start()
        return copy

    def across(dz, order):
        ref = maps_a.at[x, lax.rem(z + dz, ZS)]
        return [
            send(ref, ref, xa_send.at[d - 1, order], xa_recv.at[d - 1, order], frame(d, 0)) for d in (2, 1, 3)
        ]

    def ring_wide(s, way, c):
        zz = lax.rem(z + (ZS - s if way else s), ZS)
        ref = maps_b.at[pl.ds(2 * c, 2), zz]
        if s == 3:
            ref = maps_b.at[pl.ds(2 * c, 2), zz, pl.ds(0 if way else PART_B // 2, PART_B // 2)]
        if way:
            return send(ref, ref, wr_send.at[s, c], wr_recv.at[s, c], frame(0, 1))
        return send(ref, ref, wl_send.at[s, c], wl_recv.at[s, c], frame(0, ZS - 1))

    def pass_wide(s):
        for c in range(2):
            wr[s - 1][c].wait_recv()
            wr[s][c] = ring_wide(s, True, c)
            wl[s - 1][c].wait_recv()
            wl[s][c] = ring_wide(s, False, c)

    def jump(slot, block, dz, part=None):
        ref = maps_a.at[x, lax.rem(z + block, ZS)]
        if part is not None:
            ref = ref.at[pl.ds(part * (PART_A // 2), PART_A // 2)]
        return send(ref, ref, za_send.at[slot], za_recv.at[slot], frame(0, dz))

    xb = {}
    for d in (2, 1, 3):
        ref = maps_b.at[x, z]
        xb[d] = send(ref, ref, xb_send.at[d - 1], xb_recv.at[d - 1], frame(d, 0))
    za = [jump(0, 0, 2), jump(1, 0, 6), jump(2, 0, 1), jump(3, 0, 7)]
    goal_copies = [
        send(goals_s, goals_r.at[me_e], g_send.at[d], g_recv.at[d], {"edges": peer})
        for d, peer in enumerate(edge_peers)
    ]
    wr = [[None] * 2 for _ in range(4)]
    wl = [[None] * 2 for _ in range(4)]
    xa = across(0, 0)
    for d in (1, 3, 2):
        xb[d].wait_recv()
    for c in range(2):
        wr[0][c], wl[0][c] = ring_wide(0, True, c), ring_wide(0, False, c)

    za[2].wait_recv()
    za.append(jump(4, 7, 2))
    xa += across(7, 1)
    za[3].wait_recv()
    za.append(jump(5, 1, 6))
    xa += across(1, 2)
    za[0].wait_recv()
    za.append(jump(6, 6, 2, 0))
    za[1].wait_recv()
    za.append(jump(7, 2, 6, 1))
    xa += across(6, 3)
    xa += across(2, 4)

    for copy in goal_copies:
        copy.wait_recv()
    goals = jnp.concatenate([goals_r[k, 0:1, :] for k in range(EDGES)], axis=0)
    goals_v[...] = goals
    to_scalar = pltpu.make_async_copy(goals_v, goals_m, m_sem)
    to_scalar.start()
    lane = lax.broadcasted_iota(jnp.int32, (8, 128), 1)
    tile = jnp.where(lane == 6, goals.astype(F32), 0.0)
    for c in range(6):
        tile = jnp.where(lane == c, pose_ref[0, c], tile)
    table_ref[z, x] = tile
    ref = table_ref.at[z, x]
    tx = [send(ref, ref, tx_send.at[d], tx_recv.at[d], frame(d, 0)) for d in (2, 1, 3)]

    pass_wide(1)
    za[4].wait_recv()
    xa += across(5, 5)
    za[5].wait_recv()
    xa += across(3, 6)
    za[6].wait_recv()
    za[7].wait_recv()
    xa += across(4, 7)
    for copy in tx:
        copy.wait_recv()
    ref = table_ref.at[z]
    tz = [send(ref, ref, tz_send.at[d], tz_recv.at[d], frame(0, d)) for d in (4, 3, 5, 2, 6, 1, 7)]
    pass_wide(2)
    pass_wide(3)
    to_scalar.wait()
    for copy in xa:
        copy.wait_recv()

    def swap(maps, chosen, h, send_sem, recv_sem):
        mine = rows_of(h)
        for k in range(EDGES):
            goal = goals_m[k, 0]
            chosen[k] = maps[goal // ZS, lax.rem(goal, ZS)]
        copies = [
            send(chosen.at[peer], out_ref.at[mine], send_sem.at[d], recv_sem.at[d], {"edges": peer})
            for d, peer in enumerate(edge_peers)
        ]
        out_ref[mine, :] = chosen[me_e]
        return copies

    swaps = swap(maps_a, chosen_a, 0, ca_send, ca_recv)
    for c in range(2):
        wr[3][c].wait_recv()
        wl[3][c].wait_recv()
    swaps += swap(maps_b, chosen_b, 1, cb_send, cb_recv)
    for copy in tz:
        copy.wait_recv()
    for copy in swaps:
        copy.wait_recv()
    for copy in za + xa + list(xb.values()) + sum(wr, []) + sum(wl, []) + goal_copies + tx + tz + swaps:
        copy.wait_send()


def gather(fmap, poses, targets):
    vmem = pl.BlockSpec(memory_space=pltpu.VMEM)
    dma = pltpu.SemaphoreType.DMA
    return pl.pallas_call(
        gather_kernel,
        out_shape=(
            jax.ShapeDtypeStruct((PIX, CH), BF16),
            jax.ShapeDtypeStruct((ZS, XS, 8, 128), F32),
        ),
        in_specs=[
            pl.BlockSpec(memory_space=pl.ANY),
            pl.BlockSpec(memory_space=pltpu.SMEM),
            pl.BlockSpec(memory_space=pltpu.SMEM),
        ],
        out_specs=(vmem, vmem),
        scratch_shapes=[
            pltpu.VMEM((XS, ZS, PART_A, CH), BF16),
            pltpu.VMEM((XS, ZS, PART_B, CH), BF16),
            pltpu.VMEM((EDGES, PART_A, CH), BF16),
            pltpu.VMEM((EDGES, PART_B, CH), BF16),
            pltpu.VMEM((8, 128), jnp.int32),
            pltpu.VMEM((EDGES, 8, 128), jnp.int32),
            pltpu.VMEM((8, 128), jnp.int32),
            pltpu.SMEM((8, 128), jnp.int32),
            dma((2,)),
            dma((EDGES,)),
            dma((EDGES,)),
            dma((XS,)),
            dma((XS,)),
            dma((ZS,)),
            dma((ZS,)),
            dma((8,)),
            dma((8,)),
            dma((3, 8)),
            dma((3, 8)),
            dma((3,)),
            dma((3,)),
            dma((4, 2)),
            dma((4, 2)),
            dma((4, 2)),
            dma((4, 2)),
            dma((EDGES,)),
            dma((EDGES,)),
            dma((EDGES,)),
            dma((EDGES,)),
            dma(()),
        ],
        compiler_params=pltpu.CompilerParams(
            vmem_limit_bytes=60 * 1024 * 1024, collective_id=2, has_side_effects=True
        ),
        name="gather_maps",
    )(fmap, poses.T, targets)


def update_kernel(
    src_hbm, tgt_hbm, ctx_hbm, wg_hbm, wc_hbm, w_ref, wh_ref, hid_ref, heads_ref,
    src_ref, ctx_ref, wg_ref, wc_ref, wd_ref, w_slot, p0, p1, p2, p3, t1, f1, t2, f2, t3, sm, rm, upd, sems,
):
    loads = [
        pltpu.make_async_copy(a, b, sems.at[i])
        for i, (a, b) in enumerate(
            (
                (tgt_hbm, p0.at[pl.ds(192, PIX)]),
                (src_hbm, src_ref),
                (ctx_hbm, ctx_ref),
                (wg_hbm, wg_ref),
                (wc_hbm.at[0], wc_ref.at[:, pl.ds(0, CH)]),
                (wc_hbm.at[1], wc_ref.at[:, pl.ds(CH, CH)]),
                (wc_hbm.at[2], wd_ref),
            )
        )
    ]
    for load in loads:
        load.start()
    for g in range(4 * 7):
        w_slot[8 * g : 8 * g + 8] = jnp.concatenate(
            [w_ref[7 * g : 7 * g + 7].astype(F32), jnp.zeros((1, CH), F32)], axis=0
        )
    w_slots = w_slot[...].astype(BF16)
    w_head = jnp.concatenate([wh_ref[...].astype(F32), jnp.zeros((4, CH), F32)], axis=0).astype(BF16)
    zero = jnp.zeros((3 * WID, CH), BF16)
    p0[pl.ds(0, 192), :] = zero
    p0[pl.ds(51 * 64, 192), :] = zero
    p1[pl.ds(0, 96), :] = zero[:96]
    p1[pl.ds(27 * 32, 96), :] = zero[:96]
    p2[pl.ds(0, 48), :] = zero[:48]
    p2[pl.ds(15 * 16, 48), :] = zero[:48]
    p3[pl.ds(0, 24), :] = jnp.zeros((24, CH), F32)
    p3[pl.ds(9 * 8, 24), :] = jnp.zeros((24, CH), F32)
    edge = jnp.zeros((WID, 6 * CH), BF16)
    for ref in (sm, rm):
        ref[pl.ds(0, WID), :] = edge
        ref[pl.ds(PIX + WID, WID), :] = edge

    loads[0].wait()

    def fold_rows(r, carry):
        a = p0[pl.ds(r * 128 + 192, 64), :].astype(F32)
        b = p0[pl.ds(r * 128 + 256, 64), :].astype(F32)
        t1[pl.ds(r * 64, 64), :] = a + b
        return carry

    lax.fori_loop(0, HGT // 2, fold_rows, 0)
    f1[...] = 0.25 * (t1[pl.ds(0, 768, stride=2), :] + t1[pl.ds(1, 768, stride=2), :])
    p1[pl.ds(96, 768), :] = f1[...].astype(BF16)
    half = f1[...].reshape(12, 2, 32, CH)
    t2[...] = (half[:, 0] + half[:, 1]).reshape(384, CH)
    f2[...] = 0.25 * (t2[pl.ds(0, 192, stride=2), :] + t2[pl.ds(1, 192, stride=2), :])
    p2[pl.ds(48, 192), :] = f2[...].astype(BF16)
    half = f2[...].reshape(6, 2, 16, CH)
    t3[...] = (half[:, 0] + half[:, 1]).reshape(96, CH)
    f3 = 0.25 * (t3[pl.ds(0, 48, stride=2), :] + t3[pl.ds(1, 48, stride=2), :])
    p3[pl.ds(24, 48), :] = f3.astype(BF16).astype(F32)

    lane = lax.broadcasted_iota(jnp.int32, (8, 128), 1)
    sub = lax.broadcasted_iota(jnp.int32, (8, 128), 0)
    col = lane % WID
    scale = 1.0 / math.sqrt(CH)

    def rotate(x, level):
        amount = ((col >> level) + 5) % 8
        for bit in (1, 2, 4):
            x = jnp.where((amount // bit) % 2 == 1, pltpu.roll(x, 8 - bit, 0), x)
        return x

    def pick(vol, groups, level):
        acc = jnp.zeros((8, 128), F32)
        for g in range(groups):
            acc = jnp.where(jnp.abs(8 * g + sub - (col >> level)) <= RADIUS, vol[8 * g : 8 * g + 8], acc)
        return acc

    def spread(refs, start, lead, value):
        rows = value.shape[0]
        column = lax.broadcasted_iota(jnp.int32, value.shape, 0) % WID
        before = jnp.where(column == 0, 0.0, pltpu.roll(value, 1, 0))
        after = jnp.where(column == WID - 1, 0.0, pltpu.roll(value, rows - 1, 0))
        for dx, v in enumerate((before, value, after)):
            v = v.astype(BF16)
            for ref in refs:
                ref[pl.ds(start + WID, rows), 2 * CH * dx + lead : 2 * CH * dx + lead + CH] = v

    def block(q, carry):
        src = src_ref[pl.ds(q * 128, 128), :]
        parts = []
        vol = dot_nt(p0[pl.ds(q * 128, 512), :], src)
        rows = [pick(vol[64 * a : 64 * a + 64], 8, 0) for a in range(8)]
        for a in range(7):
            parts.append(rotate(jnp.where(lane < WID, rows[a], rows[a + 1]), 0))
        vol = dot_nt(p1[pl.ds(q * 32, 224), :], src)
        for a in range(7):
            parts.append(rotate(pick(vol[32 * a : 32 * a + 32], 4, 1), 1))
        vol = dot_nt(p2[pl.ds((q // 2) * 16, 112), :], src)
        for a in range(7):
            parts.append(rotate(pick(vol[16 * a : 16 * a + 16], 2, 2), 2))
        vol = dot_nt(p3[pl.ds((q // 4) * 8, 56), :].astype(BF16), src)
        for a in range(7):
            parts.append(rotate(pick(vol[8 * a : 8 * a + 8], 1, 3), 3))
        corr = (jnp.concatenate(parts, axis=0) * scale).astype(BF16)
        enc = lax.dot_general(corr, w_slots, (((0,), (0,)), ((), ())), preferred_element_type=F32)
        start = pl.multiple_of(q * 128, 128)
        ctx = ctx_ref[pl.ds(start, 128), :].astype(F32)
        motion = jnp.maximum(enc, 0.0) + jnp.maximum(ctx[:, CH:], 0.0)
        spread((sm, rm), start, CH, motion.astype(BF16).astype(F32))
        state = jnp.tanh(ctx[:, :CH]).astype(BF16).astype(F32)
        spread((sm,), start, 0, state)
        return carry

    loads[1].wait()
    loads[2].wait()
    lax.fori_loop(0, PIX // 128, block, 0, unroll=8)
    for load in loads[3:]:
        load.wait()

    def gates(t, carry):
        start = pl.multiple_of(t * TILE, TILE)
        acc = jnp.zeros((TILE, 2 * CH), F32)
        for dy in range(3):
            acc = acc + jnp.dot(sm[pl.ds(start + WID * dy, TILE), :], wg_ref[dy], preferred_element_type=F32)
        gate = 0.5 * jnp.tanh(0.5 * acc) + 0.5
        upd[pl.ds(start, TILE), :] = gate[:, :CH]
        state = sm[pl.ds(start + WID, TILE), 2 * CH : 3 * CH].astype(F32)
        spread((rm,), start, 0, (gate[:, CH:] * state).astype(BF16).astype(F32))
        return carry

    lax.fori_loop(0, PIX // TILE, gates, 0)

    def blend(t, carry):
        start = pl.multiple_of(t * TILE, TILE)
        both = jnp.dot(rm[pl.ds(start, TILE + WID), :], wc_ref[...], preferred_element_type=F32)
        last = jnp.dot(rm[pl.ds(start + 2 * WID, TILE), :], wd_ref[...], preferred_element_type=F32)
        acc = both[:TILE, :CH] + both[WID:, CH:] + last
        update = upd[pl.ds(start, TILE), :]
        state = sm[pl.ds(start + WID, TILE), 2 * CH : 3 * CH].astype(F32)
        hidden = ((1.0 - update) * state + update * jnp.tanh(acc)).astype(BF16)
        hid_ref[pl.ds(start, TILE), :] = hidden
        return carry

    lax.fori_loop(0, PIX // TILE, blend, 0)
    for t in range(EDGES):
        heads_ref[t] = dot_nt(w_head, hid_ref[pl.ds(t * SLICE, SLICE), :])


def update(source, target, context, w_corr, w_gates, w_cand, w_head):
    vmem = pl.BlockSpec(memory_space=pltpu.VMEM)
    return pl.pallas_call(
        update_kernel,
        out_shape=(jax.ShapeDtypeStruct((PIX, CH), BF16), jax.ShapeDtypeStruct((EDGES, 8, SLICE), F32)),
        in_specs=[pl.BlockSpec(memory_space=pl.ANY)] * 5 + [vmem] * 2,
        out_specs=(vmem, vmem),
        scratch_shapes=[
            pltpu.VMEM((PIX, CH), BF16),
            pltpu.VMEM((PIX, 2 * CH), BF16),
            pltpu.VMEM((3, 6 * CH, 2 * CH), BF16),
            pltpu.VMEM((6 * CH, 2 * CH), BF16),
            pltpu.VMEM((6 * CH, CH), BF16),
            pltpu.VMEM((224, CH), F32),
            pltpu.VMEM((54 * 64, CH), BF16),
            pltpu.VMEM((30 * 32, CH), BF16),
            pltpu.VMEM((18 * 16, CH), BF16),
            pltpu.VMEM((12 * 8, CH), F32),
            pltpu.VMEM((1536, CH), F32),
            pltpu.VMEM((768, CH), F32),
            pltpu.VMEM((384, CH), F32),
            pltpu.VMEM((192, CH), F32),
            pltpu.VMEM((96, CH), F32),
            pltpu.VMEM((PIX + 2 * WID, 6 * CH), BF16),
            pltpu.VMEM((PIX + 2 * WID, 6 * CH), BF16),
            pltpu.VMEM((PIX, CH), F32),
            pltpu.SemaphoreType.DMA((7,)),
        ],
        compiler_params=pltpu.CompilerParams(vmem_limit_bytes=60 * 1024 * 1024),
        cost_estimate=pl.CostEstimate(flops=7_000_000_000, bytes_accessed=6_500_000, transcendentals=2_000_000),
        name="edge_update",
    )(
        source, target, context, w_gates.reshape(3, 6 * CH, 2 * CH), w_cand.reshape(3, 6 * CH, CH), w_corr, w_head.T
    )


def sigmoid(x):
    return 1.0 / (1.0 + jnp.exp(-x))


def edge_terms(rel, depth, flow_u, flow_v, weight_u, weight_v, col, row):
    center_x = (WID - 1) / 2.0
    center_y = (HGT - 1) / 2.0
    ray_x = (col - center_x) / FOCAL
    ray_y = (row - center_y) / FOCAL
    move_x, move_y, move_z, turn_x, turn_y, turn_z = rel
    point_x = ray_x + turn_y - turn_z * ray_y + depth * move_x
    point_y = ray_y + turn_z * ray_x - turn_x + depth * move_y
    point_z = 1.0 + turn_x * ray_y - turn_y * ray_x + depth * move_z
    inverse_z = 1.0 / point_z
    slope = FOCAL * inverse_z
    bend_u = -FOCAL * point_x * inverse_z * inverse_z
    bend_v = -FOCAL * point_y * inverse_z * inverse_z
    resid_u = col + flow_u - (FOCAL * point_x * inverse_z + center_x)
    resid_v = row + flow_v - (FOCAL * point_y * inverse_z + center_y)
    blank = jnp.zeros_like(slope)
    jac_u = [depth * slope, blank, depth * bend_u, bend_u * ray_y, slope - bend_u * ray_x, -slope * ray_y]
    jac_v = [blank, depth * slope, depth * bend_v, bend_v * ray_y - slope, -bend_v * ray_x, slope * ray_x]
    depth_u = slope * move_x + bend_u * move_z
    depth_v = slope * move_y + bend_v * move_z
    scaled_u = [j * weight_u for j in jac_u]
    scaled_v = [j * weight_v for j in jac_v]
    cross = [scaled_u[c] * depth_u + scaled_v[c] * depth_v for c in range(6)]
    curve = weight_u * depth_u * depth_u + weight_v * depth_v * depth_v
    depth_grad = weight_u * depth_u * resid_u + weight_v * depth_v * resid_v
    return jac_u, jac_v, scaled_u, scaled_v, resid_u, resid_v, cross, curve, depth_grad


def reciprocal(x):
    r = pl.reciprocal(x, approx=True)
    r = r * (2.0 - x * r)
    return r * (2.0 - x * r)


def pivot_rows(panel, lead, first):
    tiles = len(panel)
    s = [
        [jnp.broadcast_to(lead[i : i + 1, first + j : first + j + 1], (8, 128)) for j in range(i + 1)]
        for i in range(8)
    ]
    x = [[jnp.broadcast_to(v[i : i + 1, :], (8, 128)) for v in panel] for i in range(8)]
    low = [[None] * 8 for _ in range(8)]
    inv = []
    for j in range(0, 8, 2):
        k = j + 1
        r = reciprocal(s[j][j] * s[k][k] - s[k][j] * s[k][j])
        a, b, c = s[k][k] * r, -s[k][j] * r, s[j][j] * r
        inv.append((a, b, c))
        for i in range(k + 1, 8):
            low[i][j] = s[i][j] * a + s[i][k] * b
            low[i][k] = s[i][j] * b + s[i][k] * c
        for i in range(k + 1, 8):
            for m in range(k + 1, i + 1):
                s[i][m] = s[i][m] - (low[i][j] * s[m][j] + low[i][k] * s[m][k])
    for i in range(2, 8):
        for j in range(i - i % 2):
            x[i] = [x[i][t] - low[i][j] * x[j][t] for t in range(tiles)]
    for j in range(0, 8, 2):
        a, b, c = inv[j // 2]
        u, v = x[j], x[j + 1]
        x[j] = [a * u[t] + b * v[t] for t in range(tiles)]
        x[j + 1] = [b * u[t] + c * v[t] for t in range(tiles)]
    for i in range(5, -1, -1):
        for j in range(7, i + 1 - i % 2, -1):
            x[i] = [x[i][t] - low[j][i] * x[j][t] for t in range(tiles)]
    return x


def stack_rows(x):
    sub = lax.broadcasted_iota(jnp.int32, (8, 128), 0)
    out = []
    for t in range(len(x[0])):
        v = x[0][t]
        for i in range(1, 8):
            v = jnp.where(sub == i, x[i][t], v)
        out.append(v)
    return tuple(out)


def shift_lanes(vals):
    lane = lax.broadcasted_iota(jnp.int32, (1, 128), 1)
    rolled = [pltpu.roll(v, 120, 1) for v in vals]
    return [
        v if t == len(vals) - 1 else jnp.where(lane < 120, v, rolled[t + 1]) for t, v in enumerate(rolled)
    ]


def eliminate(mat, first, last, rows):
    tiles = len(rows)
    cols = [slice(128 * t, 128 * t + 128) for t in range(tiles)]

    def step(p, own):
        base = pl.multiple_of(p * 8, 8)
        after = pl.multiple_of(jnp.minimum(p + 1, UNK // 8 - 1) * 8, 8)
        panel = [mat[pl.ds(after, 8), c] for c in cols]
        factors = [jnp.broadcast_to(panel[0][:, i : i + 1], (8, 128)) for i in range(8)]
        ahead = []
        for t in range(tiles):
            q = [factors[i] * jnp.broadcast_to(own[t][i : i + 1], (8, 128)) for i in range(8)]
            ahead.append(panel[t] - (((q[0] + q[1]) + (q[2] + q[3])) + ((q[4] + q[5]) + (q[6] + q[7]))))
        fresh = stack_rows(pivot_rows(shift_lanes(ahead), ahead[0], 8))
        wide = jnp.concatenate([jnp.concatenate(own, axis=1), jnp.zeros((120, 128 * tiles), F32)], axis=0)
        change = jnp.dot(mat[:, 0:128], wide, precision=HIGHEST, preferred_element_type=F32)
        vals = shift_lanes([mat[:, c] - change[:, c] for c in cols])
        mine = shift_lanes(list(own))
        for t in range(tiles):
            mat[:, cols[t]] = vals[t]
        for t in range(tiles):
            mat[pl.ds(base, 8), cols[t]] = mine[t]
        return fresh

    return lax.fori_loop(first, last, step, tuple(rows))


def gn_kernel(
    heads_s, table_ref, depth_ref,
    pose_out, depth_out,
    heads_r, k_s, k_r, f_s, f_r, row_s, row_r, d_s, rep_s, sgnt_s, mat,
    h_send, h_recv, k_send, k_recv, f_send, f_recv, r_send, r_recv, d_send, d_recv, own_sem,
):
    me_f = lax.axis_index("frames")
    me_e = lax.axis_index("edges")

    barrier = pltpu.get_barrier_semaphore()
    for dx, dz in FAR_FRAMES:
        peer = lax.rem(me_f // ZS + dx, XS) * ZS + lax.rem(me_f + dz, ZS)
        pl.semaphore_signal(barrier, inc=1, device_id={"frames": peer}, device_id_type=MESH)
    for dy, dc in FAR_EDGES:
        peer = lax.rem(me_e // 2 + dy, EDGES // 2) * 2 + lax.rem(me_e + dc, 2)
        pl.semaphore_signal(barrier, inc=1, device_id={"edges": peer}, device_id_type=MESH)

    lane256 = lax.broadcasted_iota(jnp.int32, (256, 128), 1)
    frame256 = lax.broadcasted_iota(jnp.int32, (256, 128), 0) // 8
    own = (frame256 == lane256 % NF).astype(F32)
    table = jnp.concatenate([table_ref[:, c] for c in range(XS)], axis=0)
    goal = jnp.broadcast_to(table[:, :, 6:7], (NF, EDGES, 128))
    for k in range(EDGES):
        same = jnp.broadcast_to(goal[:, k : k + 1, :], (NF, EDGES, 128)).reshape(256, 128)
        rep_s[k] = (same == (lane256 % NF).astype(F32)).astype(F32) - own
    signs = (goal.reshape(256, 128) == lane256.astype(F32)).astype(F32) - (frame256 == lane256).astype(F32)
    sgnt_s[...] = jnp.transpose(signs)[:NF]
    pl.semaphore_wait(barrier, EDGES - 1 + NF - 1)

    def exchange(src_of, dst_ref, send_sem, recv_sem):
        copies = []
        for d, (dy, dc) in enumerate(FAR_EDGES):
            peer = lax.rem(me_e // 2 + dy, EDGES // 2) * 2 + lax.rem(me_e + dc, 2)
            copy = pltpu.make_async_remote_copy(
                src_ref=src_of(peer),
                dst_ref=dst_ref,
                send_sem=send_sem.at[d],
                recv_sem=recv_sem.at[d],
                device_id={"edges": peer},
                device_id_type=MESH,
            )
            copy.start()
            copies.append(copy)
        return copies

    copies = exchange(lambda peer: heads_s.at[peer], heads_r.at[me_e], h_send, h_recv)
    own_heads = pltpu.make_async_copy(heads_s.at[me_e], heads_r.at[me_e], own_sem)
    own_heads.start()
    for copy in copies:
        copy.wait_recv()
    own_heads.wait()
    for copy in copies:
        copy.wait_send()

    def component(c):
        return jnp.concatenate([heads_r[k, c : c + 1, :] for k in range(EDGES)], axis=0)

    flow_u, flow_v = component(0), component(1)
    weight_u, weight_v = sigmoid(component(2)), sigmoid(component(3))
    pix = lax.broadcasted_iota(jnp.int32, (8, SLICE), 1)
    col = (pix % WID).astype(F32)
    row = (pix // WID + me_e * ROWS).astype(F32)
    depth = depth_ref[:, pl.ds(pl.multiple_of(me_e * SLICE, SLICE), SLICE)]

    k_lane = lax.broadcasted_iota(jnp.int32, (48, 128), 1)
    k_row = lax.broadcasted_iota(jnp.int32, (48, 128), 0)
    same_edge = (k_lane < 56) & (k_lane % 8 == k_row % 8)
    lane32 = lax.broadcasted_iota(jnp.int32, (NF, 128), 1)
    sub32 = lax.broadcasted_iota(jnp.int32, (NF, 128), 0)
    lane8 = lax.broadcasted_iota(jnp.int32, (8, 128), 1)
    sub8 = lax.broadcasted_iota(jnp.int32, (8, 128), 0)

    goal = jnp.broadcast_to(table_ref[lax.rem(me_f, ZS), me_f // ZS][:, 6:7], (8, 128))
    sgn = (goal == lane8.astype(F32)).astype(F32) - (lane8 == me_f).astype(F32)
    first = table[:, 0, :]
    poses = [
        jnp.sum(jnp.where(lane32 == sub32, jnp.broadcast_to(first[:, c : c + 1], (NF, 128)), 0.0), axis=0, keepdims=True)
        for c in range(6)
    ]
    poses = jnp.concatenate(poses + [jnp.zeros((2, 128), F32)], axis=0)

    def along_edges(vector):
        return jnp.sum(sgn * vector, axis=1, keepdims=True)

    for it in range(ITERS):
        rel = [along_edges(poses[c : c + 1, :]) for c in range(6)]
        jac_u, jac_v, scaled_u, scaled_v, resid_u, resid_v, cross, curve, depth_grad = edge_terms(
            rel, depth, flow_u, flow_v, weight_u, weight_v, col, row
        )
        frame_curve = jnp.sum(curve, axis=0, keepdims=True)
        frame_grad = jnp.sum(depth_grad, axis=0, keepdims=True)
        inv_damped = 1.0 / ((1.0 + DEPTH_DAMPING) * frame_curve + DEPTH_FLOOR)
        lead = jnp.concatenate([jnp.concatenate(scaled_u, axis=0), jnp.concatenate(scaled_v, axis=0)], axis=1)
        pad = jnp.zeros((72, 2 * SLICE), F32)
        trail = jnp.concatenate(
            [
                jnp.concatenate([jnp.concatenate(jac_u, axis=0), jnp.concatenate(jac_v, axis=0)], axis=1),
                jnp.concatenate([resid_u, resid_v], axis=1),
                pad,
            ],
            axis=0,
        )
        hess = dot_nt(lead, trail, HIGHEST)
        stack = jnp.concatenate(cross, axis=0)
        right = jnp.concatenate(
            [stack, jnp.broadcast_to(frame_grad, (8, SLICE)) * (sub_row(8, SLICE) == 0).astype(F32), pad[:, :SLICE]],
            axis=0,
        )
        schur = dot_nt(stack * inv_damped, right, HIGHEST)
        small = jnp.where(same_edge, hess, 0.0) - schur
        for c in range(6):
            k_s[it, c] = small[8 * c : 8 * c + 8]
        for c in range(6, 8):
            k_s[it, c] = jnp.zeros((8, 128), F32)
        copies = exchange(lambda peer: k_s.at[it, peer], k_r.at[it, me_e], k_send.at[it], k_recv.at[it])
        k_r[it, me_e] = k_s[it, me_e]
        for copy in copies:
            copy.wait()
        total = k_r[it, 0]
        for e in range(1, EDGES):
            total = total + k_r[it, e]
        f_s[it] = total
        f_r[it, me_f] = total

        copies = []
        for d, (dx, dz) in enumerate(FAR_FRAMES):
            peer = lax.rem(me_f // ZS + dx, XS) * ZS + lax.rem(me_f + dz, ZS)
            copy = pltpu.make_async_remote_copy(
                src_ref=f_s.at[it],
                dst_ref=f_r.at[it, me_f],
                send_sem=f_send.at[it, d],
                recv_sem=f_recv.at[it, d],
                device_id={"frames": peer},
                device_id_type=MESH,
            )
            copy.start()
            copies.append(copy)
        for copy in copies:
            copy.wait_recv()
        for copy in copies:
            copy.wait_send()

        blocks = f_r[it].reshape(256, 128)
        left_sum = jnp.zeros((256, 128), F32)
        right_sum = jnp.zeros((256, 128), F32)
        for k in range(EDGES):
            rep = rep_s[k]
            left_sum = left_sum + jnp.take_along_axis(blocks, (lane256 // 32) * 8 + k, axis=1) * rep
            right_sum = right_sum + jnp.take_along_axis(blocks, (lane256 // 32) % 2 * 8 + 32 + k, axis=1) * rep
        rhs = jnp.sum(jnp.where((lane256 >= 48) & (lane256 < 56), blocks, 0.0), axis=1, keepdims=True)
        right_sum = jnp.where(lane256 < 64, right_sum, jnp.where(lane256 == 64, rhs, 0.0))
        row_s[it] = jnp.concatenate(
            [
                jnp.dot(sgnt_s[...], left_sum, precision=HIGHEST, preferred_element_type=F32),
                jnp.dot(sgnt_s[...], right_sum, precision=HIGHEST, preferred_element_type=F32),
            ],
            axis=1,
        )
        copies = exchange(lambda peer: row_s.at[it], row_r.at[it, me_e], r_send.at[it], r_recv.at[it])
        row_r[it, me_e] = row_s[it]
        for copy in copies:
            copy.wait()

        for c in range(6):
            for t in range(2):
                v = row_r[it, c, :, 128 * t : 128 * t + 128]
                diag = lane32 + 128 * t == sub32 + 32 * c
                mat[32 * c : 32 * c + 32, 128 * t : 128 * t + 128] = v + jnp.where(
                    diag, POSE_DAMPING * v + POSE_FLOOR, 0.0
                )

        rows = stack_rows(pivot_rows([mat[0:8, 0:128], mat[0:8, 128:256]], mat[0:8, 0:128], 0))
        rows = eliminate(mat, 0, 9, rows)
        eliminate(mat, 9, UNK // 8, rows[:1])

        steps = []
        for c in range(6):
            v = jnp.broadcast_to(mat[32 * c : 32 * c + 32, 0:1], (NF, 128))
            steps.append(jnp.sum(jnp.where(lane32 == sub32, v, 0.0), axis=0, keepdims=True))
        along = jnp.zeros((8, SLICE), F32)
        for c in range(6):
            along = along + along_edges(steps[c]) * cross[c]
        along = jnp.sum(along, axis=0, keepdims=True)
        poses = poses + jnp.concatenate(steps + [jnp.zeros((2, 128), F32)], axis=0)
        depth = depth + (frame_grad - along) * inv_damped

    mine = jnp.sum(jnp.where(lane8 == me_f, poses, 0.0), axis=1, keepdims=True)
    pose_out[...] = jnp.sum(jnp.where(lane8 == sub_row(8, 128), mine, 0.0), axis=0, keepdims=True)[:, :6]
    d_s[...] = depth
    place = depth_out.at[:, pl.ds(pl.multiple_of(me_e * SLICE, SLICE), SLICE)]
    copies = exchange(lambda peer: d_s, place, d_send, d_recv)
    place[...] = depth
    for copy in copies:
        copy.wait()


def sub_row(rows, cols):
    return lax.broadcasted_iota(jnp.int32, (rows, cols), 0)


def gauss_newton(heads, inv_depth, table):
    vmem = pl.BlockSpec(memory_space=pltpu.VMEM)
    dma = pltpu.SemaphoreType.DMA
    pose_out, depth_out = pl.pallas_call(
        gn_kernel,
        out_shape=(
            jax.ShapeDtypeStruct((1, 6), F32),
            jax.ShapeDtypeStruct((1, PIX), F32),
        ),
        in_specs=[pl.BlockSpec(memory_space=pl.ANY), vmem, vmem],
        out_specs=(vmem, vmem),
        scratch_shapes=[
            pltpu.VMEM((EDGES, 8, SLICE), F32),
            pltpu.VMEM((ITERS, 8, 8, 128), F32),
            pltpu.VMEM((ITERS, 8, 8, 128), F32),
            pltpu.VMEM((ITERS, 8, 128), F32),
            pltpu.VMEM((ITERS, NF, 8, 128), F32),
            pltpu.VMEM((ITERS, NF, 256), F32),
            pltpu.VMEM((ITERS, EDGES, NF, 256), F32),
            pltpu.VMEM((1, SLICE), F32),
            pltpu.VMEM((EDGES, 256, 128), F32),
            pltpu.VMEM((NF, 256), F32),
            pltpu.VMEM((UNK, 256), F32),
            dma((EDGES,)),
            dma((EDGES,)),
            dma((ITERS, EDGES)),
            dma((ITERS, EDGES)),
            dma((ITERS, NF)),
            dma((ITERS, NF)),
            dma((ITERS, EDGES)),
            dma((ITERS, EDGES)),
            dma((EDGES,)),
            dma((EDGES,)),
            dma(()),
        ],
        compiler_params=pltpu.CompilerParams(
            vmem_limit_bytes=60 * 1024 * 1024, collective_id=1, has_side_effects=True
        ),
        name="gauss_newton",
    )(heads, table, inv_depth)
    return pose_out.T, depth_out


def per_device(fmap, context, poses, inv_depth, targets, w_corr, w_gates, w_cand, w_head):
    target, table = gather(fmap[0], poses, targets)
    hidden, heads = update(fmap[0], target, context[0], w_corr, w_gates, w_cand, w_head)
    new_poses, new_depth = gauss_newton(heads, inv_depth, table)
    return new_poses, new_depth, hidden[None]


def solution(mesh):
    return jax.shard_map(
        per_device,
        mesh=mesh,
        in_specs=(
            P("frames", None, None),
            P("frames", None, None),
            P(None, "frames"),
            P("frames", None),
            P(("frames", "edges")),
            P(),
            P(),
            P(),
            P(),
        ),
        out_specs=(P(None, "frames"), P("frames", None), P(("frames", "edges"), None, None)),
        check_vma=False,
    )
```

```python
import functools
import math

import jax
import jax.numpy as jnp
from jax import lax
from jax.experimental import pallas as pl
from jax.experimental.pallas import tpu as pltpu
from jax.sharding import PartitionSpec as P

HGT = 48
WID = 64
CH = 128
LEVELS = 4
RADIUS = 3
ITERS = 2
PIX = HGT * WID
NF = 32
EDGES = 8
SLICE = PIX // EDGES
ROWS = SLICE // WID
TILE = PIX // 3
UNK = 6 * NF

FOCAL = 50.0
POSE_DAMPING = 0.1
POSE_FLOOR = 1.0
DEPTH_DAMPING = 0.1
DEPTH_FLOOR = 1.0
HIGHEST = lax.Precision.HIGHEST
F32 = jnp.float32
BF16 = jnp.bfloat16
MESH = pl.DeviceIdType.MESH


def dot_nt(a, b, precision=None):
    return lax.dot_general(a, b, (((1,), (1,)), ((), ())), precision=precision, preferred_element_type=F32)


PART_A = 224
PART_B = SLICE - PART_A
XS = 4
ZS = NF // XS
FAR_EDGES = sorted(
    [(dy, dc) for dy in range(4) for dc in range(2) if dy + dc > 0], key=lambda d: -(2 * min(d[0], 4 - d[0]) + d[1])
)
FAR_FRAMES = sorted(
    [(dx, dz) for dx in range(XS) for dz in range(ZS) if dx + dz > 0],
    key=lambda d: -(min(d[0], XS - d[0]) + min(d[1], ZS - d[1])),
)


def gather_kernel(
    fmap_ref, pose_ref, goal_ref, out_ref, table_ref,
    maps_a, maps_b, chosen_a, chosen_b, goals_s, goals_r, goals_v, goals_m,
    own_sem, g_send, g_recv, tx_send, tx_recv, tz_send, tz_recv, za_send, za_recv,
    xa_send, xa_recv, xb_send, xb_recv, wr_send, wr_recv, wl_send, wl_recv,
    ca_send, ca_recv, cb_send, cb_recv, m_sem,
):
    me_f = lax.axis_index("frames")
    me_e = lax.axis_index("edges")
    x, z = me_f // ZS, lax.rem(me_f, ZS)

    def frame(dx, dz):
        return {"frames": lax.rem(x + dx, XS) * ZS + lax.rem(z + dz, ZS)}

    edge_peers = [lax.rem(me_e // 2 + dy, EDGES // 2) * 2 + lax.rem(me_e + dc, 2) for dy, dc in FAR_EDGES]

    def rows_of(h):
        return pl.ds(pl.multiple_of(me_e * SLICE + h * PART_A, 32), PART_B if h else PART_A)

    own = []
    for h, maps in enumerate((maps_a, maps_b)):
        copy = pltpu.make_async_copy(fmap_ref.at[rows_of(h)], maps.at[x, z], own_sem.at[h])
        copy.start()
        own.append(copy)

    barrier = pltpu.get_barrier_semaphore()
    for dz in (4, 3, 5, 2, 6, 1, 7):
        pl.semaphore_signal(barrier, inc=1, device_id=frame(0, dz), device_id_type=MESH)
    for dx in (2, 1, 3):
        pl.semaphore_signal(barrier, inc=1, device_id=frame(dx, 0), device_id_type=MESH)
    for peer in edge_peers:
        pl.semaphore_signal(barrier, inc=1, device_id={"edges": peer}, device_id_type=MESH)
    goals_s[...] = jnp.full((8, 128), goal_ref[0], jnp.int32)
    goals_r[me_e] = goals_s[...]
    for copy in own:
        copy.wait()
    pl.semaphore_wait(barrier, ZS - 1 + XS - 1 + EDGES - 1)

    def send(src, dst, send_sem, recv_sem, peer):
        copy = pltpu.make_async_remote_copy(
            src_ref=src, dst_ref=dst, send_sem=send_sem, recv_sem=recv_sem, device_id=peer, device_id_type=MESH
        )
        copy.start()
        return copy

    def across(dz, order):
        ref = maps_a.at[x, lax.rem(z + dz, ZS)]
        return [
            send(ref, ref, xa_send.at[d - 1, order], xa_recv.at[d - 1, order], frame(d, 0)) for d in (2, 1, 3)
        ]

    def ring_wide(s, way, c):
        zz = lax.rem(z + (ZS - s if way else s), ZS)
        ref = maps_b.at[pl.ds(2 * c, 2), zz]
        if s == 3:
            ref = maps_b.at[pl.ds(2 * c, 2), zz, pl.ds(0 if way else PART_B // 2, PART_B // 2)]
        if way:
            return send(ref, ref, wr_send.at[s, c], wr_recv.at[s, c], frame(0, 1))
        return send(ref, ref, wl_send.at[s, c], wl_recv.at[s, c], frame(0, ZS - 1))

    def pass_wide(s):
        for c in range(2):
            wr[s - 1][c].wait_recv()
            wr[s][c] = ring_wide(s, True, c)
            wl[s - 1][c].wait_recv()
            wl[s][c] = ring_wide(s, False, c)

    def jump(slot, block, dz, part=None):
        ref = maps_a.at[x, lax.rem(z + block, ZS)]
        if part is not None:
            ref = ref.at[pl.ds(part * (PART_A // 2), PART_A // 2)]
        return send(ref, ref, za_send.at[slot], za_recv.at[slot], frame(0, dz))

    xb = {}
    for d in (2, 1, 3):
        ref = maps_b.at[x, z]
        xb[d] = send(ref, ref, xb_send.at[d - 1], xb_recv.at[d - 1], frame(d, 0))
    za = [jump(0, 0, 2), jump(1, 0, 6), jump(2, 0, 1), jump(3, 0, 7)]
    goal_copies = [
        send(goals_s, goals_r.at[me_e], g_send.at[d], g_recv.at[d], {"edges": peer})
        for d, peer in enumerate(edge_peers)
    ]
    wr = [[None] * 2 for _ in range(4)]
    wl = [[None] * 2 for _ in range(4)]
    xa = across(0, 0)
    for d in (1, 3, 2):
        xb[d].wait_recv()
    for c in range(2):
        wr[0][c], wl[0][c] = ring_wide(0, True, c), ring_wide(0, False, c)

    za[2].wait_recv()
    za.append(jump(4, 7, 2))
    xa += across(7, 1)
    za[3].wait_recv()
    za.append(jump(5, 1, 6))
    xa += across(1, 2)
    za[0].wait_recv()
    za.append(jump(6, 6, 2, 0))
    za[1].wait_recv()
    za.append(jump(7, 2, 6, 1))
    xa += across(6, 3)
    xa += across(2, 4)

    for copy in goal_copies:
        copy.wait_recv()
    goals = jnp.concatenate([goals_r[k, 0:1, :] for k in range(EDGES)], axis=0)
    goals_v[...] = goals
    to_scalar = pltpu.make_async_copy(goals_v, goals_m, m_sem)
    to_scalar.start()
    lane = lax.broadcasted_iota(jnp.int32, (8, 128), 1)
    tile = jnp.where(lane == 6, goals.astype(F32), 0.0)
    for c in range(6):
        tile = jnp.where(lane == c, pose_ref[0, c], tile)
    table_ref[z, x] = tile
    ref = table_ref.at[z, x]
    tx = [send(ref, ref, tx_send.at[d], tx_recv.at[d], frame(d, 0)) for d in (2, 1, 3)]

    pass_wide(1)
    za[4].wait_recv()
    xa += across(5, 5)
    za[5].wait_recv()
    xa += across(3, 6)
    za[6].wait_recv()
    za[7].wait_recv()
    xa += across(4, 7)
    for copy in tx:
        copy.wait_recv()
    ref = table_ref.at[z]
    tz = [send(ref, ref, tz_send.at[d], tz_recv.at[d], frame(0, d)) for d in (4, 3, 5, 2, 6, 1, 7)]
    pass_wide(2)
    pass_wide(3)
    to_scalar.wait()
    for copy in xa:
        copy.wait_recv()

    def swap(maps, chosen, h, send_sem, recv_sem):
        mine = rows_of(h)
        for k in range(EDGES):
            goal = goals_m[k, 0]
            chosen[k] = maps[goal // ZS, lax.rem(goal, ZS)]
        copies = [
            send(chosen.at[peer], out_ref.at[mine], send_sem.at[d], recv_sem.at[d], {"edges": peer})
            for d, peer in enumerate(edge_peers)
        ]
        out_ref[mine, :] = chosen[me_e]
        return copies

    swaps = swap(maps_a, chosen_a, 0, ca_send, ca_recv)
    for c in range(2):
        wr[3][c].wait_recv()
        wl[3][c].wait_recv()
    swaps += swap(maps_b, chosen_b, 1, cb_send, cb_recv)
    for copy in tz:
        copy.wait_recv()
    for copy in swaps:
        copy.wait_recv()
    for copy in za + xa + list(xb.values()) + sum(wr, []) + sum(wl, []) + goal_copies + tx + tz + swaps:
        copy.wait_send()


def gather(fmap, poses, targets):
    vmem = pl.BlockSpec(memory_space=pltpu.VMEM)
    dma = pltpu.SemaphoreType.DMA
    return pl.pallas_call(
        gather_kernel,
        out_shape=(
            jax.ShapeDtypeStruct((PIX, CH), BF16),
            jax.ShapeDtypeStruct((ZS, XS, 8, 128), F32),
        ),
        in_specs=[
            pl.BlockSpec(memory_space=pl.ANY),
            pl.BlockSpec(memory_space=pltpu.SMEM),
            pl.BlockSpec(memory_space=pltpu.SMEM),
        ],
        out_specs=(vmem, vmem),
        scratch_shapes=[
            pltpu.VMEM((XS, ZS, PART_A, CH), BF16),
            pltpu.VMEM((XS, ZS, PART_B, CH), BF16),
            pltpu.VMEM((EDGES, PART_A, CH), BF16),
            pltpu.VMEM((EDGES, PART_B, CH), BF16),
            pltpu.VMEM((8, 128), jnp.int32),
            pltpu.VMEM((EDGES, 8, 128), jnp.int32),
            pltpu.VMEM((8, 128), jnp.int32),
            pltpu.SMEM((8, 128), jnp.int32),
            dma((2,)),
            dma((EDGES,)),
            dma((EDGES,)),
            dma((XS,)),
            dma((XS,)),
            dma((ZS,)),
            dma((ZS,)),
            dma((8,)),
            dma((8,)),
            dma((3, 8)),
            dma((3, 8)),
            dma((3,)),
            dma((3,)),
            dma((4, 2)),
            dma((4, 2)),
            dma((4, 2)),
            dma((4, 2)),
            dma((EDGES,)),
            dma((EDGES,)),
            dma((EDGES,)),
            dma((EDGES,)),
            dma(()),
        ],
        compiler_params=pltpu.CompilerParams(
            vmem_limit_bytes=60 * 1024 * 1024, collective_id=2, has_side_effects=True
        ),
        name="gather_maps",
    )(fmap, poses.T, targets)


def update_kernel(
    src_hbm, tgt_hbm, ctx_hbm, wg_hbm, wc_hbm, w_ref, wh_ref, hid_ref, heads_ref,
    src_ref, ctx_ref, wg_ref, wc_ref, wd_ref, w_slot, p0, p1, p2, p3, t1, f1, t2, f2, t3, sm, rm, upd, sems,
):
    loads = [
        pltpu.make_async_copy(a, b, sems.at[i])
        for i, (a, b) in enumerate(
            (
                (tgt_hbm, p0.at[pl.ds(192, PIX)]),
                (src_hbm, src_ref),
                (ctx_hbm, ctx_ref),
                (wg_hbm, wg_ref),
                (wc_hbm.at[0], wc_ref.at[:, pl.ds(0, CH)]),
                (wc_hbm.at[1], wc_ref.at[:, pl.ds(CH, CH)]),
                (wc_hbm.at[2], wd_ref),
            )
        )
    ]
    for load in loads:
        load.start()
    for g in range(4 * 7):
        w_slot[8 * g : 8 * g + 8] = jnp.concatenate(
            [w_ref[7 * g : 7 * g + 7].astype(F32), jnp.zeros((1, CH), F32)], axis=0
        )
    w_slots = w_slot[...].astype(BF16)
    w_head = jnp.concatenate([wh_ref[...].astype(F32), jnp.zeros((4, CH), F32)], axis=0).astype(BF16)
    zero = jnp.zeros((3 * WID, CH), BF16)
    p0[pl.ds(0, 192), :] = zero
    p0[pl.ds(51 * 64, 192), :] = zero
    p1[pl.ds(0, 96), :] = zero[:96]
    p1[pl.ds(27 * 32, 96), :] = zero[:96]
    p2[pl.ds(0, 48), :] = zero[:48]
    p2[pl.ds(15 * 16, 48), :] = zero[:48]
    p3[pl.ds(0, 24), :] = jnp.zeros((24, CH), F32)
    p3[pl.ds(9 * 8, 24), :] = jnp.zeros((24, CH), F32)
    edge = jnp.zeros((WID, 6 * CH), BF16)
    for ref in (sm, rm):
        ref[pl.ds(0, WID), :] = edge
        ref[pl.ds(PIX + WID, WID), :] = edge

    loads[0].wait()

    def fold_rows(r, carry):
        a = p0[pl.ds(r * 128 + 192, 64), :].astype(F32)
        b = p0[pl.ds(r * 128 + 256, 64), :].astype(F32)
        t1[pl.ds(r * 64, 64), :] = a + b
        return carry

    lax.fori_loop(0, HGT // 2, fold_rows, 0)
    f1[...] = 0.25 * (t1[pl.ds(0, 768, stride=2), :] + t1[pl.ds(1, 768, stride=2), :])
    p1[pl.ds(96, 768), :] = f1[...].astype(BF16)
    half = f1[...].reshape(12, 2, 32, CH)
    t2[...] = (half[:, 0] + half[:, 1]).reshape(384, CH)
    f2[...] = 0.25 * (t2[pl.ds(0, 192, stride=2), :] + t2[pl.ds(1, 192, stride=2), :])
    p2[pl.ds(48, 192), :] = f2[...].astype(BF16)
    half = f2[...].reshape(6, 2, 16, CH)
    t3[...] = (half[:, 0] + half[:, 1]).reshape(96, CH)
    f3 = 0.25 * (t3[pl.ds(0, 48, stride=2), :] + t3[pl.ds(1, 48, stride=2), :])
    p3[pl.ds(24, 48), :] = f3.astype(BF16).astype(F32)

    lane = lax.broadcasted_iota(jnp.int32, (8, 128), 1)
    sub = lax.broadcasted_iota(jnp.int32, (8, 128), 0)
    col = lane % WID
    scale = 1.0 / math.sqrt(CH)

    def rotate(x, level):
        amount = ((col >> level) + 5) % 8
        for bit in (1, 2, 4):
            x = jnp.where((amount // bit) % 2 == 1, pltpu.roll(x, 8 - bit, 0), x)
        return x

    def pick(vol, groups, level):
        acc = jnp.zeros((8, 128), F32)
        for g in range(groups):
            acc = jnp.where(jnp.abs(8 * g + sub - (col >> level)) <= RADIUS, vol[8 * g : 8 * g + 8], acc)
        return acc

    def spread(refs, start, lead, value):
        rows = value.shape[0]
        column = lax.broadcasted_iota(jnp.int32, value.shape, 0) % WID
        before = jnp.where(column == 0, 0.0, pltpu.roll(value, 1, 0))
        after = jnp.where(column == WID - 1, 0.0, pltpu.roll(value, rows - 1, 0))
        for dx, v in enumerate((before, value, after)):
            v = v.astype(BF16)
            for ref in refs:
                ref[pl.ds(start + WID, rows), 2 * CH * dx + lead : 2 * CH * dx + lead + CH] = v

    def block(q, carry):
        src = src_ref[pl.ds(q * 128, 128), :]
        parts = []
        vol = dot_nt(p0[pl.ds(q * 128, 512), :], src)
        rows = [pick(vol[64 * a : 64 * a + 64], 8, 0) for a in range(8)]
        for a in range(7):
            parts.append(rotate(jnp.where(lane < WID, rows[a], rows[a + 1]), 0))
        vol = dot_nt(p1[pl.ds(q * 32, 224), :], src)
        for a in range(7):
            parts.append(rotate(pick(vol[32 * a : 32 * a + 32], 4, 1), 1))
        vol = dot_nt(p2[pl.ds((q // 2) * 16, 112), :], src)
        for a in range(7):
            parts.append(rotate(pick(vol[16 * a : 16 * a + 16], 2, 2), 2))
        vol = dot_nt(p3[pl.ds((q // 4) * 8, 56), :].astype(BF16), src)
        for a in range(7):
            parts.append(rotate(pick(vol[8 * a : 8 * a + 8], 1, 3), 3))
        corr = (jnp.concatenate(parts, axis=0) * scale).astype(BF16)
        enc = lax.dot_general(corr, w_slots, (((0,), (0,)), ((), ())), preferred_element_type=F32)
        start = pl.multiple_of(q * 128, 128)
        ctx = ctx_ref[pl.ds(start, 128), :].astype(F32)
        motion = jnp.maximum(enc, 0.0) + jnp.maximum(ctx[:, CH:], 0.0)
        spread((sm, rm), start, CH, motion.astype(BF16).astype(F32))
        state = jnp.tanh(ctx[:, :CH]).astype(BF16).astype(F32)
        spread((sm,), start, 0, state)
        return carry

    loads[1].wait()
    loads[2].wait()
    lax.fori_loop(0, PIX // 128, block, 0, unroll=8)
    for load in loads[3:]:
        load.wait()

    def gates(t, carry):
        start = pl.multiple_of(t * TILE, TILE)
        acc = jnp.zeros((TILE, 2 * CH), F32)
        for dy in range(3):
            acc = acc + jnp.dot(sm[pl.ds(start + WID * dy, TILE), :], wg_ref[dy], preferred_element_type=F32)
        gate = 0.5 * jnp.tanh(0.5 * acc) + 0.5
        upd[pl.ds(start, TILE), :] = gate[:, :CH]
        state = sm[pl.ds(start + WID, TILE), 2 * CH : 3 * CH].astype(F32)
        spread((rm,), start, 0, (gate[:, CH:] * state).astype(BF16).astype(F32))
        return carry

    lax.fori_loop(0, PIX // TILE, gates, 0)

    def blend(t, carry):
        start = pl.multiple_of(t * TILE, TILE)
        both = jnp.dot(rm[pl.ds(start, TILE + WID), :], wc_ref[...], preferred_element_type=F32)
        last = jnp.dot(rm[pl.ds(start + 2 * WID, TILE), :], wd_ref[...], preferred_element_type=F32)
        acc = both[:TILE, :CH] + both[WID:, CH:] + last
        update = upd[pl.ds(start, TILE), :]
        state = sm[pl.ds(start + WID, TILE), 2 * CH : 3 * CH].astype(F32)
        hidden = ((1.0 - update) * state + update * jnp.tanh(acc)).astype(BF16)
        hid_ref[pl.ds(start, TILE), :] = hidden
        return carry

    lax.fori_loop(0, PIX // TILE, blend, 0)
    for t in range(EDGES):
        heads_ref[t] = dot_nt(w_head, hid_ref[pl.ds(t * SLICE, SLICE), :])


def update(source, target, context, w_corr, w_gates, w_cand, w_head):
    vmem = pl.BlockSpec(memory_space=pltpu.VMEM)
    return pl.pallas_call(
        update_kernel,
        out_shape=(jax.ShapeDtypeStruct((PIX, CH), BF16), jax.ShapeDtypeStruct((EDGES, 8, SLICE), F32)),
        in_specs=[pl.BlockSpec(memory_space=pl.ANY)] * 5 + [vmem] * 2,
        out_specs=(vmem, vmem),
        scratch_shapes=[
            pltpu.VMEM((PIX, CH), BF16),
            pltpu.VMEM((PIX, 2 * CH), BF16),
            pltpu.VMEM((3, 6 * CH, 2 * CH), BF16),
            pltpu.VMEM((6 * CH, 2 * CH), BF16),
            pltpu.VMEM((6 * CH, CH), BF16),
            pltpu.VMEM((224, CH), F32),
            pltpu.VMEM((54 * 64, CH), BF16),
            pltpu.VMEM((30 * 32, CH), BF16),
            pltpu.VMEM((18 * 16, CH), BF16),
            pltpu.VMEM((12 * 8, CH), F32),
            pltpu.VMEM((1536, CH), F32),
            pltpu.VMEM((768, CH), F32),
            pltpu.VMEM((384, CH), F32),
            pltpu.VMEM((192, CH), F32),
            pltpu.VMEM((96, CH), F32),
            pltpu.VMEM((PIX + 2 * WID, 6 * CH), BF16),
            pltpu.VMEM((PIX + 2 * WID, 6 * CH), BF16),
            pltpu.VMEM((PIX, CH), F32),
            pltpu.SemaphoreType.DMA((7,)),
        ],
        compiler_params=pltpu.CompilerParams(vmem_limit_bytes=60 * 1024 * 1024),
        cost_estimate=pl.CostEstimate(flops=7_000_000_000, bytes_accessed=6_500_000, transcendentals=2_000_000),
        name="edge_update",
    )(
        source, target, context, w_gates.reshape(3, 6 * CH, 2 * CH), w_cand.reshape(3, 6 * CH, CH), w_corr, w_head.T
    )


def sigmoid(x):
    return 1.0 / (1.0 + jnp.exp(-x))


def edge_terms(rel, depth, flow_u, flow_v, weight_u, weight_v, col, row):
    center_x = (WID - 1) / 2.0
    center_y = (HGT - 1) / 2.0
    ray_x = (col - center_x) / FOCAL
    ray_y = (row - center_y) / FOCAL
    move_x, move_y, move_z, turn_x, turn_y, turn_z = rel
    point_x = ray_x + turn_y - turn_z * ray_y + depth * move_x
    point_y = ray_y + turn_z * ray_x - turn_x + depth * move_y
    point_z = 1.0 + turn_x * ray_y - turn_y * ray_x + depth * move_z
    inverse_z = 1.0 / point_z
    slope = FOCAL * inverse_z
    bend_u = -FOCAL * point_x * inverse_z * inverse_z
    bend_v = -FOCAL * point_y * inverse_z * inverse_z
    resid_u = col + flow_u - (FOCAL * point_x * inverse_z + center_x)
    resid_v = row + flow_v - (FOCAL * point_y * inverse_z + center_y)
    blank = jnp.zeros_like(slope)
    jac_u = [depth * slope, blank, depth * bend_u, bend_u * ray_y, slope - bend_u * ray_x, -slope * ray_y]
    jac_v = [blank, depth * slope, depth * bend_v, bend_v * ray_y - slope, -bend_v * ray_x, slope * ray_x]
    depth_u = slope * move_x + bend_u * move_z
    depth_v = slope * move_y + bend_v * move_z
    scaled_u = [j * weight_u for j in jac_u]
    scaled_v = [j * weight_v for j in jac_v]
    cross = [scaled_u[c] * depth_u + scaled_v[c] * depth_v for c in range(6)]
    curve = weight_u * depth_u * depth_u + weight_v * depth_v * depth_v
    depth_grad = weight_u * depth_u * resid_u + weight_v * depth_v * resid_v
    return jac_u, jac_v, scaled_u, scaled_v, resid_u, resid_v, cross, curve, depth_grad


def reciprocal(x):
    r = pl.reciprocal(x, approx=True)
    r = r * (2.0 - x * r)
    return r * (2.0 - x * r)


def pivot_rows(panel, lead, first):
    tiles = len(panel)
    s = [
        [jnp.broadcast_to(lead[i : i + 1, first + j : first + j + 1], (8, 128)) for j in range(i + 1)]
        for i in range(8)
    ]
    x = [[jnp.broadcast_to(v[i : i + 1, :], (8, 128)) for v in panel] for i in range(8)]
    low = [[None] * 8 for _ in range(8)]
    inv = []
    for j in range(0, 8, 2):
        k = j + 1
        r = reciprocal(s[j][j] * s[k][k] - s[k][j] * s[k][j])
        a, b, c = s[k][k] * r, -s[k][j] * r, s[j][j] * r
        inv.append((a, b, c))
        for i in range(k + 1, 8):
            low[i][j] = s[i][j] * a + s[i][k] * b
            low[i][k] = s[i][j] * b + s[i][k] * c
        for i in range(k + 1, 8):
            for m in range(k + 1, i + 1):
                s[i][m] = s[i][m] - (low[i][j] * s[m][j] + low[i][k] * s[m][k])
    for i in range(2, 8):
        for j in range(i - i % 2):
            x[i] = [x[i][t] - low[i][j] * x[j][t] for t in range(tiles)]
    for j in range(0, 8, 2):
        a, b, c = inv[j // 2]
        u, v = x[j], x[j + 1]
        x[j] = [a * u[t] + b * v[t] for t in range(tiles)]
        x[j + 1] = [b * u[t] + c * v[t] for t in range(tiles)]
    for i in range(5, -1, -1):
        for j in range(7, i + 1 - i % 2, -1):
            x[i] = [x[i][t] - low[j][i] * x[j][t] for t in range(tiles)]
    return x


def thirds(a):
    first = a.astype(BF16)
    rest = a - first.astype(F32)
    second = rest.astype(BF16)
    return first, second, (rest - second.astype(F32)).astype(BF16)


def stack_rows(x):
    sub = lax.broadcasted_iota(jnp.int32, (8, 128), 0)
    out = []
    for t in range(len(x[0])):
        v = x[0][t]
        for i in range(1, 8):
            v = jnp.where(sub == i, x[i][t], v)
        out.append(v)
    return tuple(out)


def shift_lanes(vals):
    lane = lax.broadcasted_iota(jnp.int32, (1, 128), 1)
    rolled = [pltpu.roll(v, 120, 1) for v in vals]
    return [
        v if t == len(vals) - 1 else jnp.where(lane < 120, v, rolled[t + 1]) for t, v in enumerate(rolled)
    ]


def eliminate(mat, first, last, rows):
    tiles = len(rows)
    cols = [slice(128 * t, 128 * t + 128) for t in range(tiles)]

    def step(p, own):
        base = pl.multiple_of(p * 8, 8)
        after = pl.multiple_of(jnp.minimum(p + 1, UNK // 8 - 1) * 8, 8)
        panel = [mat[pl.ds(after, 8), c] for c in cols]
        factors = [jnp.broadcast_to(panel[0][:, i : i + 1], (8, 128)) for i in range(8)]
        ahead = []
        for t in range(tiles):
            q = [factors[i] * jnp.broadcast_to(own[t][i : i + 1], (8, 128)) for i in range(8)]
            ahead.append(panel[t] - (((q[0] + q[1]) + (q[2] + q[3])) + ((q[4] + q[5]) + (q[6] + q[7]))))
        fresh = stack_rows(pivot_rows(shift_lanes(ahead), ahead[0], 8))
        wide = jnp.concatenate([jnp.concatenate(own, axis=1), jnp.zeros((120, 128 * tiles), F32)], axis=0)
        c1, c2, c3 = thirds(mat[:, 0:128])
        x1, x2, x3 = thirds(wide)
        two = jnp.concatenate([c1, c2], axis=1)
        change = (
            jnp.dot(two, jnp.concatenate([x1, x1], axis=0), preferred_element_type=F32)
            + jnp.dot(two, jnp.concatenate([x2, x2], axis=0), preferred_element_type=F32)
            + jnp.dot(
                jnp.concatenate([c1, c3], axis=1), jnp.concatenate([x3, x1], axis=0), preferred_element_type=F32
            )
        )
        vals = shift_lanes([mat[:, c] - change[:, c] for c in cols])
        mine = shift_lanes(list(own))
        for t in range(tiles):
            mat[:, cols[t]] = vals[t]
        for t in range(tiles):
            mat[pl.ds(base, 8), cols[t]] = mine[t]
        return fresh

    return lax.fori_loop(first, last, step, tuple(rows))


def gn_kernel(
    heads_s, table_ref, depth_ref,
    pose_out, depth_out,
    heads_r, k_s, k_r, f_s, f_r, row_s, row_r, d_s, rep_s, sgnt_s, mat,
    h_send, h_recv, k_send, k_recv, f_send, f_recv, r_send, r_recv, d_send, d_recv, own_sem,
):
    me_f = lax.axis_index("frames")
    me_e = lax.axis_index("edges")

    barrier = pltpu.get_barrier_semaphore()
    for dx, dz in FAR_FRAMES:
        peer = lax.rem(me_f // ZS + dx, XS) * ZS + lax.rem(me_f + dz, ZS)
        pl.semaphore_signal(barrier, inc=1, device_id={"frames": peer}, device_id_type=MESH)
    for dy, dc in FAR_EDGES:
        peer = lax.rem(me_e // 2 + dy, EDGES // 2) * 2 + lax.rem(me_e + dc, 2)
        pl.semaphore_signal(barrier, inc=1, device_id={"edges": peer}, device_id_type=MESH)

    pl.semaphore_wait(barrier, EDGES - 1 + NF - 1)

    def exchange(src_of, dst_ref, send_sem, recv_sem):
        copies = []
        for d, (dy, dc) in enumerate(FAR_EDGES):
            peer = lax.rem(me_e // 2 + dy, EDGES // 2) * 2 + lax.rem(me_e + dc, 2)
            copy = pltpu.make_async_remote_copy(
                src_ref=src_of(peer),
                dst_ref=dst_ref,
                send_sem=send_sem.at[d],
                recv_sem=recv_sem.at[d],
                device_id={"edges": peer},
                device_id_type=MESH,
            )
            copy.start()
            copies.append(copy)
        return copies

    copies = exchange(lambda peer: heads_s.at[peer], heads_r.at[me_e], h_send, h_recv)
    own_heads = pltpu.make_async_copy(heads_s.at[me_e], heads_r.at[me_e], own_sem)
    own_heads.start()

    lane256 = lax.broadcasted_iota(jnp.int32, (256, 128), 1)
    frame256 = lax.broadcasted_iota(jnp.int32, (256, 128), 0) // 8
    own = (frame256 == lane256 % NF).astype(F32)
    table = jnp.concatenate([table_ref[:, c] for c in range(XS)], axis=0)
    goal = jnp.broadcast_to(table[:, :, 6:7], (NF, EDGES, 128))
    for k in range(EDGES):
        same = jnp.broadcast_to(goal[:, k : k + 1, :], (NF, EDGES, 128)).reshape(256, 128)
        rep_s[k] = (same == (lane256 % NF).astype(F32)).astype(F32) - own
    signs = (goal.reshape(256, 128) == lane256.astype(F32)).astype(F32) - (frame256 == lane256).astype(F32)
    sgnt_s[...] = jnp.transpose(signs)[:NF]

    for copy in copies:
        copy.wait_recv()
    own_heads.wait()
    for copy in copies:
        copy.wait_send()

    def component(c):
        return jnp.concatenate([heads_r[k, c : c + 1, :] for k in range(EDGES)], axis=0)

    flow_u, flow_v = component(0), component(1)
    weight_u, weight_v = sigmoid(component(2)), sigmoid(component(3))
    pix = lax.broadcasted_iota(jnp.int32, (8, SLICE), 1)
    col = (pix % WID).astype(F32)
    row = (pix // WID + me_e * ROWS).astype(F32)
    depth = depth_ref[:, pl.ds(pl.multiple_of(me_e * SLICE, SLICE), SLICE)]

    k_lane = lax.broadcasted_iota(jnp.int32, (48, 128), 1)
    k_row = lax.broadcasted_iota(jnp.int32, (48, 128), 0)
    same_edge = (k_lane < 56) & (k_lane % 8 == k_row % 8)
    lane32 = lax.broadcasted_iota(jnp.int32, (NF, 128), 1)
    sub32 = lax.broadcasted_iota(jnp.int32, (NF, 128), 0)
    lane8 = lax.broadcasted_iota(jnp.int32, (8, 128), 1)
    sub8 = lax.broadcasted_iota(jnp.int32, (8, 128), 0)

    goal = jnp.broadcast_to(table_ref[lax.rem(me_f, ZS), me_f // ZS][:, 6:7], (8, 128))
    sgn = (goal == lane8.astype(F32)).astype(F32) - (lane8 == me_f).astype(F32)
    first = table[:, 0, :]
    poses = [
        jnp.sum(jnp.where(lane32 == sub32, jnp.broadcast_to(first[:, c : c + 1], (NF, 128)), 0.0), axis=0, keepdims=True)
        for c in range(6)
    ]
    poses = jnp.concatenate(poses + [jnp.zeros((2, 128), F32)], axis=0)

    def along_edges(vector):
        return jnp.sum(sgn * vector, axis=1, keepdims=True)

    for it in range(ITERS):
        rel = [along_edges(poses[c : c + 1, :]) for c in range(6)]
        jac_u, jac_v, scaled_u, scaled_v, resid_u, resid_v, cross, curve, depth_grad = edge_terms(
            rel, depth, flow_u, flow_v, weight_u, weight_v, col, row
        )
        frame_curve = jnp.sum(curve, axis=0, keepdims=True)
        frame_grad = jnp.sum(depth_grad, axis=0, keepdims=True)
        inv_damped = 1.0 / ((1.0 + DEPTH_DAMPING) * frame_curve + DEPTH_FLOOR)
        lead = jnp.concatenate([jnp.concatenate(scaled_u, axis=0), jnp.concatenate(scaled_v, axis=0)], axis=1)
        pad = jnp.zeros((72, 2 * SLICE), F32)
        trail = jnp.concatenate(
            [
                jnp.concatenate([jnp.concatenate(jac_u, axis=0), jnp.concatenate(jac_v, axis=0)], axis=1),
                jnp.concatenate([resid_u, resid_v], axis=1),
                pad,
            ],
            axis=0,
        )
        hess = dot_nt(lead, trail, HIGHEST)
        stack = jnp.concatenate(cross, axis=0)
        right = jnp.concatenate(
            [stack, jnp.broadcast_to(frame_grad, (8, SLICE)) * (sub_row(8, SLICE) == 0).astype(F32), pad[:, :SLICE]],
            axis=0,
        )
        schur = dot_nt(stack * inv_damped, right, HIGHEST)
        small = jnp.where(same_edge, hess, 0.0) - schur
        for c in range(6):
            k_s[it, c] = small[8 * c : 8 * c + 8]
        for c in range(6, 8):
            k_s[it, c] = jnp.zeros((8, 128), F32)
        copies = exchange(lambda peer: k_s.at[it, peer], k_r.at[it, me_e], k_send.at[it], k_recv.at[it])
        k_r[it, me_e] = k_s[it, me_e]
        for copy in copies:
            copy.wait()
        total = k_r[it, 0]
        for e in range(1, EDGES):
            total = total + k_r[it, e]
        f_s[it] = total
        f_r[it, me_f] = total

        copies = []
        for d, (dx, dz) in enumerate(FAR_FRAMES):
            peer = lax.rem(me_f // ZS + dx, XS) * ZS + lax.rem(me_f + dz, ZS)
            copy = pltpu.make_async_remote_copy(
                src_ref=f_s.at[it],
                dst_ref=f_r.at[it, me_f],
                send_sem=f_send.at[it, d],
                recv_sem=f_recv.at[it, d],
                device_id={"frames": peer},
                device_id_type=MESH,
            )
            copy.start()
            copies.append(copy)
        for copy in copies:
            copy.wait_recv()
        for copy in copies:
            copy.wait_send()

        blocks = f_r[it].reshape(256, 128)
        left_sum = jnp.zeros((256, 128), F32)
        right_sum = jnp.zeros((256, 128), F32)
        for k in range(EDGES):
            rep = rep_s[k]
            left_sum = left_sum + jnp.take_along_axis(blocks, (lane256 // 32) * 8 + k, axis=1) * rep
            right_sum = right_sum + jnp.take_along_axis(blocks, (lane256 // 32) % 2 * 8 + 32 + k, axis=1) * rep
        rhs = jnp.sum(jnp.where((lane256 >= 48) & (lane256 < 56), blocks, 0.0), axis=1, keepdims=True)
        right_sum = jnp.where(lane256 < 64, right_sum, jnp.where(lane256 == 64, rhs, 0.0))
        row_s[it] = jnp.concatenate(
            [
                jnp.dot(sgnt_s[...], left_sum, precision=HIGHEST, preferred_element_type=F32),
                jnp.dot(sgnt_s[...], right_sum, precision=HIGHEST, preferred_element_type=F32),
            ],
            axis=1,
        )
        copies = exchange(lambda peer: row_s.at[it], row_r.at[it, me_e], r_send.at[it], r_recv.at[it])
        row_r[it, me_e] = row_s[it]
        for copy in copies:
            copy.wait()

        for c in range(6):
            for t in range(2):
                v = row_r[it, c, :, 128 * t : 128 * t + 128]
                diag = lane32 + 128 * t == sub32 + 32 * c
                mat[32 * c : 32 * c + 32, 128 * t : 128 * t + 128] = v + jnp.where(
                    diag, POSE_DAMPING * v + POSE_FLOOR, 0.0
                )

        rows = stack_rows(pivot_rows([mat[0:8, 0:128], mat[0:8, 128:256]], mat[0:8, 0:128], 0))
        rows = eliminate(mat, 0, 9, rows)
        eliminate(mat, 9, UNK // 8, rows[:1])

        steps = []
        for c in range(6):
            v = jnp.broadcast_to(mat[32 * c : 32 * c + 32, 0:1], (NF, 128))
            steps.append(jnp.sum(jnp.where(lane32 == sub32, v, 0.0), axis=0, keepdims=True))
        along = jnp.zeros((8, SLICE), F32)
        for c in range(6):
            along = along + along_edges(steps[c]) * cross[c]
        along = jnp.sum(along, axis=0, keepdims=True)
        poses = poses + jnp.concatenate(steps + [jnp.zeros((2, 128), F32)], axis=0)
        depth = depth + (frame_grad - along) * inv_damped

    mine = jnp.sum(jnp.where(lane8 == me_f, poses, 0.0), axis=1, keepdims=True)
    pose_out[...] = jnp.sum(jnp.where(lane8 == sub_row(8, 128), mine, 0.0), axis=0, keepdims=True)[:, :6]
    d_s[...] = depth
    place = depth_out.at[:, pl.ds(pl.multiple_of(me_e * SLICE, SLICE), SLICE)]
    copies = exchange(lambda peer: d_s, place, d_send, d_recv)
    place[...] = depth
    for copy in copies:
        copy.wait()


def sub_row(rows, cols):
    return lax.broadcasted_iota(jnp.int32, (rows, cols), 0)


def gauss_newton(heads, inv_depth, table):
    vmem = pl.BlockSpec(memory_space=pltpu.VMEM)
    dma = pltpu.SemaphoreType.DMA
    pose_out, depth_out = pl.pallas_call(
        gn_kernel,
        out_shape=(
            jax.ShapeDtypeStruct((1, 6), F32),
            jax.ShapeDtypeStruct((1, PIX), F32),
        ),
        in_specs=[pl.BlockSpec(memory_space=pl.ANY), vmem, vmem],
        out_specs=(vmem, vmem),
        scratch_shapes=[
            pltpu.VMEM((EDGES, 8, SLICE), F32),
            pltpu.VMEM((ITERS, 8, 8, 128), F32),
            pltpu.VMEM((ITERS, 8, 8, 128), F32),
            pltpu.VMEM((ITERS, 8, 128), F32),
            pltpu.VMEM((ITERS, NF, 8, 128), F32),
            pltpu.VMEM((ITERS, NF, 256), F32),
            pltpu.VMEM((ITERS, EDGES, NF, 256), F32),
            pltpu.VMEM((1, SLICE), F32),
            pltpu.VMEM((EDGES, 256, 128), F32),
            pltpu.VMEM((NF, 256), F32),
            pltpu.VMEM((UNK, 256), F32),
            dma((EDGES,)),
            dma((EDGES,)),
            dma((ITERS, EDGES)),
            dma((ITERS, EDGES)),
            dma((ITERS, NF)),
            dma((ITERS, NF)),
            dma((ITERS, EDGES)),
            dma((ITERS, EDGES)),
            dma((EDGES,)),
            dma((EDGES,)),
            dma(()),
        ],
        compiler_params=pltpu.CompilerParams(
            vmem_limit_bytes=60 * 1024 * 1024, collective_id=1, has_side_effects=True
        ),
        name="gauss_newton",
    )(heads, table, inv_depth)
    return pose_out.T, depth_out


def per_device(fmap, context, poses, inv_depth, targets, w_corr, w_gates, w_cand, w_head):
    target, table = gather(fmap[0], poses, targets)
    hidden, heads = update(fmap[0], target, context[0], w_corr, w_gates, w_cand, w_head)
    new_poses, new_depth = gauss_newton(heads, inv_depth, table)
    return new_poses, new_depth, hidden[None]


def solution(mesh):
    return jax.shard_map(
        per_device,
        mesh=mesh,
        in_specs=(
            P("frames", None, None),
            P("frames", None, None),
            P(None, "frames"),
            P("frames", None),
            P(("frames", "edges")),
            P(),
            P(),
            P(),
            P(),
        ),
        out_specs=(P(None, "frames"), P("frames", None), P(("frames", "edges"), None, None)),
        check_vma=False,
    )
```

```python
import functools
import math

import jax
import jax.numpy as jnp
from jax import lax
from jax.experimental import pallas as pl
from jax.experimental.pallas import tpu as pltpu
from jax.sharding import PartitionSpec as P

HGT = 48
WID = 64
CH = 128
LEVELS = 4
RADIUS = 3
ITERS = 2
PIX = HGT * WID
NF = 32
EDGES = 8
SLICE = PIX // EDGES
ROWS = SLICE // WID
TILE = PIX // 3
UNK = 6 * NF

FOCAL = 50.0
POSE_DAMPING = 0.1
POSE_FLOOR = 1.0
DEPTH_DAMPING = 0.1
DEPTH_FLOOR = 1.0
HIGHEST = lax.Precision.HIGHEST
F32 = jnp.float32
BF16 = jnp.bfloat16
MESH = pl.DeviceIdType.MESH


def dot_nt(a, b, precision=None):
    return lax.dot_general(a, b, (((1,), (1,)), ((), ())), precision=precision, preferred_element_type=F32)


PART_A = 224
PART_B = SLICE - PART_A
XS = 4
ZS = NF // XS
FAR_EDGES = sorted(
    [(dy, dc) for dy in range(4) for dc in range(2) if dy + dc > 0], key=lambda d: -(2 * min(d[0], 4 - d[0]) + d[1])
)
FAR_FRAMES = sorted(
    [(dx, dz) for dx in range(XS) for dz in range(ZS) if dx + dz > 0],
    key=lambda d: -(min(d[0], XS - d[0]) + min(d[1], ZS - d[1])),
)


def gather_kernel(
    fmap_ref, pose_ref, goal_ref, out_ref, table_ref,
    maps_a, maps_b, chosen_a, chosen_b, goals_s, goals_r, goals_v, goals_m,
    own_sem, g_send, g_recv, tx_send, tx_recv, tz_send, tz_recv, za_send, za_recv,
    xa_send, xa_recv, xb_send, xb_recv, wr_send, wr_recv, wl_send, wl_recv,
    ca_send, ca_recv, cb_send, cb_recv, m_sem, stay_sem,
):
    me_f = lax.axis_index("frames")
    me_e = lax.axis_index("edges")
    x, z = me_f // ZS, lax.rem(me_f, ZS)

    def frame(dx, dz):
        return {"frames": lax.rem(x + dx, XS) * ZS + lax.rem(z + dz, ZS)}

    edge_peers = [lax.rem(me_e // 2 + dy, EDGES // 2) * 2 + lax.rem(me_e + dc, 2) for dy, dc in FAR_EDGES]

    def rows_of(h):
        return pl.ds(pl.multiple_of(me_e * SLICE + h * PART_A, 32), PART_B if h else PART_A)

    own = []
    for h, maps in enumerate((maps_a, maps_b)):
        copy = pltpu.make_async_copy(fmap_ref.at[rows_of(h)], maps.at[x, z], own_sem.at[h])
        copy.start()
        own.append(copy)

    barrier = pltpu.get_barrier_semaphore()
    for dz in (4, 3, 5, 2, 6, 1, 7):
        pl.semaphore_signal(barrier, inc=1, device_id=frame(0, dz), device_id_type=MESH)
    for dx in (2, 1, 3):
        pl.semaphore_signal(barrier, inc=1, device_id=frame(dx, 0), device_id_type=MESH)
    for peer in edge_peers:
        pl.semaphore_signal(barrier, inc=1, device_id={"edges": peer}, device_id_type=MESH)
    goals_s[...] = jnp.full((8, 128), goal_ref[0], jnp.int32)
    goals_r[me_e] = goals_s[...]
    for copy in own:
        copy.wait()
    pl.semaphore_wait(barrier, ZS - 1 + XS - 1 + EDGES - 1)

    def send(src, dst, send_sem, recv_sem, peer):
        copy = pltpu.make_async_remote_copy(
            src_ref=src, dst_ref=dst, send_sem=send_sem, recv_sem=recv_sem, device_id=peer, device_id_type=MESH
        )
        copy.start()
        return copy

    def across(dz, order):
        ref = maps_a.at[x, lax.rem(z + dz, ZS)]
        return [
            send(ref, ref, xa_send.at[d - 1, order], xa_recv.at[d - 1, order], frame(d, 0)) for d in (2, 1, 3)
        ]

    def ring_wide(s, way, c):
        zz = lax.rem(z + (ZS - s if way else s), ZS)
        ref = maps_b.at[pl.ds(2 * c, 2), zz]
        if s == 3:
            ref = maps_b.at[pl.ds(2 * c, 2), zz, pl.ds(0 if way else PART_B // 2, PART_B // 2)]
        if way:
            return send(ref, ref, wr_send.at[s, c], wr_recv.at[s, c], frame(0, 1))
        return send(ref, ref, wl_send.at[s, c], wl_recv.at[s, c], frame(0, ZS - 1))

    def pass_wide(s):
        for c in range(2):
            wr[s - 1][c].wait_recv()
            wr[s][c] = ring_wide(s, True, c)
            wl[s - 1][c].wait_recv()
            wl[s][c] = ring_wide(s, False, c)

    def jump(slot, block, dz, part=None):
        ref = maps_a.at[x, lax.rem(z + block, ZS)]
        if part is not None:
            ref = ref.at[pl.ds(part * (PART_A // 2), PART_A // 2)]
        return send(ref, ref, za_send.at[slot], za_recv.at[slot], frame(0, dz))

    xb = {}
    for d in (2, 1, 3):
        ref = maps_b.at[x, z]
        xb[d] = send(ref, ref, xb_send.at[d - 1], xb_recv.at[d - 1], frame(d, 0))
    za = [jump(0, 0, 2), jump(1, 0, 6), jump(2, 0, 1), jump(3, 0, 7)]
    goal_copies = [
        send(goals_s, goals_r.at[me_e], g_send.at[d], g_recv.at[d], {"edges": peer})
        for d, peer in enumerate(edge_peers)
    ]
    wr = [[None] * 2 for _ in range(4)]
    wl = [[None] * 2 for _ in range(4)]
    xa = across(0, 0)
    for d in (1, 3, 2):
        xb[d].wait_recv()
    for c in range(2):
        wr[0][c], wl[0][c] = ring_wide(0, True, c), ring_wide(0, False, c)

    za[2].wait_recv()
    za.append(jump(4, 7, 2))
    xa += across(7, 1)
    za[3].wait_recv()
    za.append(jump(5, 1, 6))
    xa += across(1, 2)
    za[0].wait_recv()
    za.append(jump(6, 6, 2, 0))
    za[1].wait_recv()
    za.append(jump(7, 2, 6, 1))
    xa += across(6, 3)
    xa += across(2, 4)

    for copy in goal_copies:
        copy.wait_recv()
    goals = jnp.concatenate([goals_r[k, 0:1, :] for k in range(EDGES)], axis=0)
    goals_v[...] = goals
    to_scalar = pltpu.make_async_copy(goals_v, goals_m, m_sem)
    to_scalar.start()
    lane = lax.broadcasted_iota(jnp.int32, (8, 128), 1)
    tile = jnp.where(lane == 6, goals.astype(F32), 0.0)
    for c in range(6):
        tile = jnp.where(lane == c, pose_ref[0, c], tile)
    table_ref[z, x] = tile
    ref = table_ref.at[z, x]
    tx = [send(ref, ref, tx_send.at[d], tx_recv.at[d], frame(d, 0)) for d in (2, 1, 3)]

    pass_wide(1)
    za[4].wait_recv()
    xa += across(5, 5)
    za[5].wait_recv()
    xa += across(3, 6)
    za[6].wait_recv()
    za[7].wait_recv()
    xa += across(4, 7)
    for copy in tx:
        copy.wait_recv()
    ref = table_ref.at[z]
    tz = [send(ref, ref, tz_send.at[d], tz_recv.at[d], frame(0, d)) for d in (4, 3, 5, 2, 6, 1, 7)]
    pass_wide(2)
    pass_wide(3)
    to_scalar.wait()
    for copy in xa:
        copy.wait_recv()

    def swap(maps, chosen, h, send_sem, recv_sem):
        mine = rows_of(h)
        for k in range(EDGES):
            goal = goals_m[k, 0]
            chosen[k] = maps[goal // ZS, lax.rem(goal, ZS)]
        copies = [
            send(chosen.at[peer], out_ref.at[mine], send_sem.at[d], recv_sem.at[d], {"edges": peer})
            for d, peer in enumerate(edge_peers)
        ]
        stay = pltpu.make_async_copy(chosen.at[me_e], out_ref.at[mine], stay_sem.at[h])
        stay.start()
        return copies, stay

    swaps, stay_a = swap(maps_a, chosen_a, 0, ca_send, ca_recv)
    for c in range(2):
        wr[3][c].wait_recv()
        wl[3][c].wait_recv()
    more, stay_b = swap(maps_b, chosen_b, 1, cb_send, cb_recv)
    swaps += more
    stay_a.wait()
    stay_b.wait()
    for copy in tz:
        copy.wait_recv()
    for copy in swaps:
        copy.wait_recv()
    for copy in za + xa + list(xb.values()) + sum(wr, []) + sum(wl, []) + goal_copies + tx + tz + swaps:
        copy.wait_send()


def gather(fmap, poses, targets):
    vmem = pl.BlockSpec(memory_space=pltpu.VMEM)
    dma = pltpu.SemaphoreType.DMA
    return pl.pallas_call(
        gather_kernel,
        out_shape=(
            jax.ShapeDtypeStruct((PIX, CH), BF16),
            jax.ShapeDtypeStruct((ZS, XS, 8, 128), F32),
        ),
        in_specs=[
            pl.BlockSpec(memory_space=pl.ANY),
            pl.BlockSpec(memory_space=pltpu.SMEM),
            pl.BlockSpec(memory_space=pltpu.SMEM),
        ],
        out_specs=(pl.BlockSpec(memory_space=pl.ANY), vmem),
        scratch_shapes=[
            pltpu.VMEM((XS, ZS, PART_A, CH), BF16),
            pltpu.VMEM((XS, ZS, PART_B, CH), BF16),
            pltpu.VMEM((EDGES, PART_A, CH), BF16),
            pltpu.VMEM((EDGES, PART_B, CH), BF16),
            pltpu.VMEM((8, 128), jnp.int32),
            pltpu.VMEM((EDGES, 8, 128), jnp.int32),
            pltpu.VMEM((8, 128), jnp.int32),
            pltpu.SMEM((8, 128), jnp.int32),
            dma((2,)),
            dma((EDGES,)),
            dma((EDGES,)),
            dma((XS,)),
            dma((XS,)),
            dma((ZS,)),
            dma((ZS,)),
            dma((8,)),
            dma((8,)),
            dma((3, 8)),
            dma((3, 8)),
            dma((3,)),
            dma((3,)),
            dma((4, 2)),
            dma((4, 2)),
            dma((4, 2)),
            dma((4, 2)),
            dma((EDGES,)),
            dma((EDGES,)),
            dma((EDGES,)),
            dma((EDGES,)),
            dma(()),
            dma((2,)),
        ],
        compiler_params=pltpu.CompilerParams(
            vmem_limit_bytes=60 * 1024 * 1024, collective_id=2, has_side_effects=True
        ),
        name="gather_maps",
    )(fmap, poses.T, targets)


def update_kernel(
    src_hbm, tgt_hbm, ctx_hbm, wg_hbm, wc_hbm, w_ref, wh_ref, hid_hbm, heads_ref,
    src_ref, ctx_ref, wg_ref, wc_ref, wd_ref, w_slot, p0, p1, p2, p3, t1, f1, t2, f2, t3, sm, rm, upd, hid_ref, sems, out_sems,
):
    loads = [
        pltpu.make_async_copy(a, b, sems.at[i])
        for i, (a, b) in enumerate(
            (
                (tgt_hbm, p0.at[pl.ds(192, PIX)]),
                (src_hbm, src_ref),
                (ctx_hbm, ctx_ref),
                (wg_hbm, wg_ref),
                (wc_hbm.at[0], wc_ref.at[:, pl.ds(0, CH)]),
                (wc_hbm.at[1], wc_ref.at[:, pl.ds(CH, CH)]),
                (wc_hbm.at[2], wd_ref),
            )
        )
    ]
    for load in loads:
        load.start()
    for g in range(4 * 7):
        w_slot[8 * g : 8 * g + 8] = jnp.concatenate(
            [w_ref[7 * g : 7 * g + 7].astype(F32), jnp.zeros((1, CH), F32)], axis=0
        )
    w_slots = w_slot[...].astype(BF16)
    w_head = jnp.concatenate([wh_ref[...].astype(F32), jnp.zeros((4, CH), F32)], axis=0).astype(BF16)
    zero = jnp.zeros((3 * WID, CH), BF16)
    p0[pl.ds(0, 192), :] = zero
    p0[pl.ds(51 * 64, 192), :] = zero
    p1[pl.ds(0, 96), :] = zero[:96]
    p1[pl.ds(27 * 32, 96), :] = zero[:96]
    p2[pl.ds(0, 48), :] = zero[:48]
    p2[pl.ds(15 * 16, 48), :] = zero[:48]
    p3[pl.ds(0, 24), :] = jnp.zeros((24, CH), F32)
    p3[pl.ds(9 * 8, 24), :] = jnp.zeros((24, CH), F32)
    edge = jnp.zeros((WID, 6 * CH), BF16)
    for ref in (sm, rm):
        ref[pl.ds(0, WID), :] = edge
        ref[pl.ds(PIX + WID, WID), :] = edge

    loads[0].wait()

    def fold_rows(r, carry):
        a = p0[pl.ds(r * 128 + 192, 64), :].astype(F32)
        b = p0[pl.ds(r * 128 + 256, 64), :].astype(F32)
        t1[pl.ds(r * 64, 64), :] = a + b
        return carry

    lax.fori_loop(0, HGT // 2, fold_rows, 0)
    f1[...] = 0.25 * (t1[pl.ds(0, 768, stride=2), :] + t1[pl.ds(1, 768, stride=2), :])
    p1[pl.ds(96, 768), :] = f1[...].astype(BF16)
    half = f1[...].reshape(12, 2, 32, CH)
    t2[...] = (half[:, 0] + half[:, 1]).reshape(384, CH)
    f2[...] = 0.25 * (t2[pl.ds(0, 192, stride=2), :] + t2[pl.ds(1, 192, stride=2), :])
    p2[pl.ds(48, 192), :] = f2[...].astype(BF16)
    half = f2[...].reshape(6, 2, 16, CH)
    t3[...] = (half[:, 0] + half[:, 1]).reshape(96, CH)
    f3 = 0.25 * (t3[pl.ds(0, 48, stride=2), :] + t3[pl.ds(1, 48, stride=2), :])
    p3[pl.ds(24, 48), :] = f3.astype(BF16).astype(F32)

    lane = lax.broadcasted_iota(jnp.int32, (8, 128), 1)
    sub = lax.broadcasted_iota(jnp.int32, (8, 128), 0)
    col = lane % WID
    scale = 1.0 / math.sqrt(CH)

    def rotate(x, level):
        amount = ((col >> level) + 5) % 8
        for bit in (1, 2, 4):
            x = jnp.where((amount // bit) % 2 == 1, pltpu.roll(x, 8 - bit, 0), x)
        return x

    def pick(vol, groups, level):
        acc = jnp.zeros((8, 128), F32)
        for g in range(groups):
            acc = jnp.where(jnp.abs(8 * g + sub - (col >> level)) <= RADIUS, vol[8 * g : 8 * g + 8], acc)
        return acc

    def spread(refs, start, lead, value):
        rows = value.shape[0]
        column = lax.broadcasted_iota(jnp.int32, value.shape, 0) % WID
        before = jnp.where(column == 0, 0.0, pltpu.roll(value, 1, 0))
        after = jnp.where(column == WID - 1, 0.0, pltpu.roll(value, rows - 1, 0))
        for dx, v in enumerate((before, value, after)):
            v = v.astype(BF16)
            for ref in refs:
                ref[pl.ds(start + WID, rows), 2 * CH * dx + lead : 2 * CH * dx + lead + CH] = v

    def block(q, carry):
        src = src_ref[pl.ds(q * 128, 128), :]
        parts = []
        vol = dot_nt(p0[pl.ds(q * 128, 512), :], src)
        rows = [pick(vol[64 * a : 64 * a + 64], 8, 0) for a in range(8)]
        for a in range(7):
            parts.append(rotate(jnp.where(lane < WID, rows[a], rows[a + 1]), 0))
        vol = dot_nt(p1[pl.ds(q * 32, 224), :], src)
        for a in range(7):
            parts.append(rotate(pick(vol[32 * a : 32 * a + 32], 4, 1), 1))
        vol = dot_nt(p2[pl.ds((q // 2) * 16, 112), :], src)
        for a in range(7):
            parts.append(rotate(pick(vol[16 * a : 16 * a + 16], 2, 2), 2))
        vol = dot_nt(p3[pl.ds((q // 4) * 8, 56), :].astype(BF16), src)
        for a in range(7):
            parts.append(rotate(pick(vol[8 * a : 8 * a + 8], 1, 3), 3))
        corr = (jnp.concatenate(parts, axis=0) * scale).astype(BF16)
        enc = lax.dot_general(corr, w_slots, (((0,), (0,)), ((), ())), preferred_element_type=F32)
        start = pl.multiple_of(q * 128, 128)
        ctx = ctx_ref[pl.ds(start, 128), :].astype(F32)
        motion = jnp.maximum(enc, 0.0) + jnp.maximum(ctx[:, CH:], 0.0)
        spread((sm, rm), start, CH, motion.astype(BF16).astype(F32))
        state = jnp.tanh(ctx[:, :CH]).astype(BF16).astype(F32)
        spread((sm,), start, 0, state)
        return carry

    loads[1].wait()
    loads[2].wait()
    lax.fori_loop(0, PIX // 128, block, 0, unroll=8)
    for load in loads[3:]:
        load.wait()

    def gates(t, carry):
        start = pl.multiple_of(t * TILE, TILE)
        acc = jnp.zeros((TILE, 2 * CH), F32)
        for dy in range(3):
            acc = acc + jnp.dot(sm[pl.ds(start + WID * dy, TILE), :], wg_ref[dy], preferred_element_type=F32)
        gate = 0.5 * jnp.tanh(0.5 * acc) + 0.5
        upd[pl.ds(start, TILE), :] = gate[:, :CH]
        state = sm[pl.ds(start + WID, TILE), 2 * CH : 3 * CH].astype(F32)
        spread((rm,), start, 0, (gate[:, CH:] * state).astype(BF16).astype(F32))
        return carry

    lax.fori_loop(0, PIX // TILE, gates, 0)

    def leave(t):
        rows = pl.ds(pl.multiple_of(t * TILE, TILE), TILE)
        return pltpu.make_async_copy(hid_ref.at[rows], hid_hbm.at[rows], out_sems.at[t])

    def blend(t, carry):
        start = pl.multiple_of(t * TILE, TILE)
        both = jnp.dot(rm[pl.ds(start, TILE + WID), :], wc_ref[...], preferred_element_type=F32)
        last = jnp.dot(rm[pl.ds(start + 2 * WID, TILE), :], wd_ref[...], preferred_element_type=F32)
        acc = both[:TILE, :CH] + both[WID:, CH:] + last
        update = upd[pl.ds(start, TILE), :]
        state = sm[pl.ds(start + WID, TILE), 2 * CH : 3 * CH].astype(F32)
        hidden = ((1.0 - update) * state + update * jnp.tanh(acc)).astype(BF16)
        hid_ref[pl.ds(start, TILE), :] = hidden
        leave(t).start()
        return carry

    lax.fori_loop(0, PIX // TILE, blend, 0)
    for t in range(EDGES):
        heads_ref[t] = dot_nt(w_head, hid_ref[pl.ds(t * SLICE, SLICE), :])
    for t in range(PIX // TILE):
        leave(t).wait()


def update(source, target, context, w_corr, w_gates, w_cand, w_head):
    vmem = pl.BlockSpec(memory_space=pltpu.VMEM)
    return pl.pallas_call(
        update_kernel,
        out_shape=(jax.ShapeDtypeStruct((PIX, CH), BF16), jax.ShapeDtypeStruct((EDGES, 8, SLICE), F32)),
        in_specs=[pl.BlockSpec(memory_space=pl.ANY)] * 5 + [vmem] * 2,
        out_specs=(pl.BlockSpec(memory_space=pl.ANY), vmem),
        scratch_shapes=[
            pltpu.VMEM((PIX, CH), BF16),
            pltpu.VMEM((PIX, 2 * CH), BF16),
            pltpu.VMEM((3, 6 * CH, 2 * CH), BF16),
            pltpu.VMEM((6 * CH, 2 * CH), BF16),
            pltpu.VMEM((6 * CH, CH), BF16),
            pltpu.VMEM((224, CH), F32),
            pltpu.VMEM((54 * 64, CH), BF16),
            pltpu.VMEM((30 * 32, CH), BF16),
            pltpu.VMEM((18 * 16, CH), BF16),
            pltpu.VMEM((12 * 8, CH), F32),
            pltpu.VMEM((1536, CH), F32),
            pltpu.VMEM((768, CH), F32),
            pltpu.VMEM((384, CH), F32),
            pltpu.VMEM((192, CH), F32),
            pltpu.VMEM((96, CH), F32),
            pltpu.VMEM((PIX + 2 * WID, 6 * CH), BF16),
            pltpu.VMEM((PIX + 2 * WID, 6 * CH), BF16),
            pltpu.VMEM((PIX, CH), F32),
            pltpu.VMEM((PIX, CH), BF16),
            pltpu.SemaphoreType.DMA((7,)),
            pltpu.SemaphoreType.DMA((PIX // TILE,)),
        ],
        compiler_params=pltpu.CompilerParams(vmem_limit_bytes=60 * 1024 * 1024),
        cost_estimate=pl.CostEstimate(flops=7_000_000_000, bytes_accessed=6_500_000, transcendentals=2_000_000),
        name="edge_update",
    )(
        source, target, context, w_gates.reshape(3, 6 * CH, 2 * CH), w_cand.reshape(3, 6 * CH, CH), w_corr, w_head.T
    )


def sigmoid(x):
    return 1.0 / (1.0 + jnp.exp(-x))


def edge_terms(rel, depth, flow_u, flow_v, weight_u, weight_v, col, row):
    center_x = (WID - 1) / 2.0
    center_y = (HGT - 1) / 2.0
    ray_x = (col - center_x) / FOCAL
    ray_y = (row - center_y) / FOCAL
    move_x, move_y, move_z, turn_x, turn_y, turn_z = rel
    point_x = ray_x + turn_y - turn_z * ray_y + depth * move_x
    point_y = ray_y + turn_z * ray_x - turn_x + depth * move_y
    point_z = 1.0 + turn_x * ray_y - turn_y * ray_x + depth * move_z
    inverse_z = 1.0 / point_z
    slope = FOCAL * inverse_z
    bend_u = -FOCAL * point_x * inverse_z * inverse_z
    bend_v = -FOCAL * point_y * inverse_z * inverse_z
    resid_u = col + flow_u - (FOCAL * point_x * inverse_z + center_x)
    resid_v = row + flow_v - (FOCAL * point_y * inverse_z + center_y)
    blank = jnp.zeros_like(slope)
    jac_u = [depth * slope, blank, depth * bend_u, bend_u * ray_y, slope - bend_u * ray_x, -slope * ray_y]
    jac_v = [blank, depth * slope, depth * bend_v, bend_v * ray_y - slope, -bend_v * ray_x, slope * ray_x]
    depth_u = slope * move_x + bend_u * move_z
    depth_v = slope * move_y + bend_v * move_z
    scaled_u = [j * weight_u for j in jac_u]
    scaled_v = [j * weight_v for j in jac_v]
    cross = [scaled_u[c] * depth_u + scaled_v[c] * depth_v for c in range(6)]
    curve = weight_u * depth_u * depth_u + weight_v * depth_v * depth_v
    depth_grad = weight_u * depth_u * resid_u + weight_v * depth_v * resid_v
    return jac_u, jac_v, scaled_u, scaled_v, resid_u, resid_v, cross, curve, depth_grad


def reciprocal(x):
    r = pl.reciprocal(x, approx=True)
    r = r * (2.0 - x * r)
    return r * (2.0 - x * r)


def pivot_rows(panel, lead, first):
    tiles = len(panel)
    s = [
        [jnp.broadcast_to(lead[i : i + 1, first + j : first + j + 1], (8, 128)) for j in range(i + 1)]
        for i in range(8)
    ]
    x = [[jnp.broadcast_to(v[i : i + 1, :], (8, 128)) for v in panel] for i in range(8)]
    low = [[None] * 8 for _ in range(8)]
    inv = []
    for j in range(0, 8, 2):
        k = j + 1
        r = reciprocal(s[j][j] * s[k][k] - s[k][j] * s[k][j])
        a, b, c = s[k][k] * r, -s[k][j] * r, s[j][j] * r
        inv.append((a, b, c))
        for i in range(k + 1, 8):
            low[i][j] = s[i][j] * a + s[i][k] * b
            low[i][k] = s[i][j] * b + s[i][k] * c
        for i in range(k + 1, 8):
            for m in range(k + 1, i + 1):
                s[i][m] = s[i][m] - (low[i][j] * s[m][j] + low[i][k] * s[m][k])
    for i in range(2, 8):
        for j in range(i - i % 2):
            x[i] = [x[i][t] - low[i][j] * x[j][t] for t in range(tiles)]
    for j in range(0, 8, 2):
        a, b, c = inv[j // 2]
        u, v = x[j], x[j + 1]
        x[j] = [a * u[t] + b * v[t] for t in range(tiles)]
        x[j + 1] = [b * u[t] + c * v[t] for t in range(tiles)]
    for i in range(5, -1, -1):
        for j in range(7, i + 1 - i % 2, -1):
            x[i] = [x[i][t] - low[j][i] * x[j][t] for t in range(tiles)]
    return x


def thirds(a):
    first = a.astype(BF16)
    rest = a - first.astype(F32)
    second = rest.astype(BF16)
    return first, second, (rest - second.astype(F32)).astype(BF16)


def stack_rows(x):
    sub = lax.broadcasted_iota(jnp.int32, (8, 128), 0)
    out = []
    for t in range(len(x[0])):
        v = x[0][t]
        for i in range(1, 8):
            v = jnp.where(sub == i, x[i][t], v)
        out.append(v)
    return tuple(out)


def shift_lanes(vals):
    lane = lax.broadcasted_iota(jnp.int32, (1, 128), 1)
    rolled = [pltpu.roll(v, 120, 1) for v in vals]
    return [
        v if t == len(vals) - 1 else jnp.where(lane < 120, v, rolled[t + 1]) for t, v in enumerate(rolled)
    ]


def eliminate(mat, first, last, rows):
    tiles = len(rows)
    cols = [slice(128 * t, 128 * t + 128) for t in range(tiles)]

    def step(p, own):
        base = pl.multiple_of(p * 8, 8)
        after = pl.multiple_of(jnp.minimum(p + 1, UNK // 8 - 1) * 8, 8)
        panel = [mat[pl.ds(after, 8), c] for c in cols]
        factors = [jnp.broadcast_to(panel[0][:, i : i + 1], (8, 128)) for i in range(8)]
        ahead = []
        for t in range(tiles):
            q = [factors[i] * jnp.broadcast_to(own[t][i : i + 1], (8, 128)) for i in range(8)]
            ahead.append(panel[t] - (((q[0] + q[1]) + (q[2] + q[3])) + ((q[4] + q[5]) + (q[6] + q[7]))))
        fresh = stack_rows(pivot_rows(shift_lanes(ahead), ahead[0], 8))
        wide = jnp.concatenate([jnp.concatenate(own, axis=1), jnp.zeros((120, 128 * tiles), F32)], axis=0)
        c1, c2, c3 = thirds(mat[:, 0:128])
        x1, x2, x3 = thirds(wide)
        two = jnp.concatenate([c1, c2], axis=1)
        change = (
            jnp.dot(two, jnp.concatenate([x1, x1], axis=0), preferred_element_type=F32)
            + jnp.dot(two, jnp.concatenate([x2, x2], axis=0), preferred_element_type=F32)
            + jnp.dot(
                jnp.concatenate([c1, c3], axis=1), jnp.concatenate([x3, x1], axis=0), preferred_element_type=F32
            )
        )
        vals = shift_lanes([mat[:, c] - change[:, c] for c in cols])
        mine = shift_lanes(list(own))
        for t in range(tiles):
            mat[:, cols[t]] = vals[t]
        for t in range(tiles):
            mat[pl.ds(base, 8), cols[t]] = mine[t]
        return fresh

    return lax.fori_loop(first, last, step, tuple(rows))


def gn_kernel(
    heads_s, table_ref, depth_ref,
    pose_out, depth_out,
    heads_r, k_s, k_r, f_s, f_r, row_s, row_r, d_s, rep_s, sgnt_s, mat,
    h_send, h_recv, k_send, k_recv, f_send, f_recv, r_send, r_recv, d_send, d_recv, own_sem,
):
    me_f = lax.axis_index("frames")
    me_e = lax.axis_index("edges")

    barrier = pltpu.get_barrier_semaphore()
    for dx, dz in FAR_FRAMES:
        peer = lax.rem(me_f // ZS + dx, XS) * ZS + lax.rem(me_f + dz, ZS)
        pl.semaphore_signal(barrier, inc=1, device_id={"frames": peer}, device_id_type=MESH)
    for dy, dc in FAR_EDGES:
        peer = lax.rem(me_e // 2 + dy, EDGES // 2) * 2 + lax.rem(me_e + dc, 2)
        pl.semaphore_signal(barrier, inc=1, device_id={"edges": peer}, device_id_type=MESH)

    pl.semaphore_wait(barrier, EDGES - 1 + NF - 1)

    def exchange(src_of, dst_ref, send_sem, recv_sem):
        copies = []
        for d, (dy, dc) in enumerate(FAR_EDGES):
            peer = lax.rem(me_e // 2 + dy, EDGES // 2) * 2 + lax.rem(me_e + dc, 2)
            copy = pltpu.make_async_remote_copy(
                src_ref=src_of(peer),
                dst_ref=dst_ref,
                send_sem=send_sem.at[d],
                recv_sem=recv_sem.at[d],
                device_id={"edges": peer},
                device_id_type=MESH,
            )
            copy.start()
            copies.append(copy)
        return copies

    copies = exchange(lambda peer: heads_s.at[peer], heads_r.at[me_e], h_send, h_recv)
    own_heads = pltpu.make_async_copy(heads_s.at[me_e], heads_r.at[me_e], own_sem)
    own_heads.start()

    lane256 = lax.broadcasted_iota(jnp.int32, (256, 128), 1)
    frame256 = lax.broadcasted_iota(jnp.int32, (256, 128), 0) // 8
    own = (frame256 == lane256 % NF).astype(F32)
    table = jnp.concatenate([table_ref[:, c] for c in range(XS)], axis=0)
    goal = jnp.broadcast_to(table[:, :, 6:7], (NF, EDGES, 128))
    for k in range(EDGES):
        same = jnp.broadcast_to(goal[:, k : k + 1, :], (NF, EDGES, 128)).reshape(256, 128)
        rep_s[k] = (same == (lane256 % NF).astype(F32)).astype(F32) - own
    signs = (goal.reshape(256, 128) == lane256.astype(F32)).astype(F32) - (frame256 == lane256).astype(F32)
    sgnt_s[...] = jnp.transpose(signs)[:NF]

    for copy in copies:
        copy.wait_recv()
    own_heads.wait()
    for copy in copies:
        copy.wait_send()

    def component(c):
        return jnp.concatenate([heads_r[k, c : c + 1, :] for k in range(EDGES)], axis=0)

    flow_u, flow_v = component(0), component(1)
    weight_u, weight_v = sigmoid(component(2)), sigmoid(component(3))
    pix = lax.broadcasted_iota(jnp.int32, (8, SLICE), 1)
    col = (pix % WID).astype(F32)
    row = (pix // WID + me_e * ROWS).astype(F32)
    depth = depth_ref[:, pl.ds(pl.multiple_of(me_e * SLICE, SLICE), SLICE)]

    k_lane = lax.broadcasted_iota(jnp.int32, (48, 128), 1)
    k_row = lax.broadcasted_iota(jnp.int32, (48, 128), 0)
    same_edge = (k_lane < 56) & (k_lane % 8 == k_row % 8)
    lane32 = lax.broadcasted_iota(jnp.int32, (NF, 128), 1)
    sub32 = lax.broadcasted_iota(jnp.int32, (NF, 128), 0)
    lane8 = lax.broadcasted_iota(jnp.int32, (8, 128), 1)
    sub8 = lax.broadcasted_iota(jnp.int32, (8, 128), 0)

    goal = jnp.broadcast_to(table_ref[lax.rem(me_f, ZS), me_f // ZS][:, 6:7], (8, 128))
    sgn = (goal == lane8.astype(F32)).astype(F32) - (lane8 == me_f).astype(F32)
    first = table[:, 0, :]
    poses = [
        jnp.sum(jnp.where(lane32 == sub32, jnp.broadcast_to(first[:, c : c + 1], (NF, 128)), 0.0), axis=0, keepdims=True)
        for c in range(6)
    ]
    poses = jnp.concatenate(poses + [jnp.zeros((2, 128), F32)], axis=0)

    def along_edges(vector):
        return jnp.sum(sgn * vector, axis=1, keepdims=True)

    for it in range(ITERS):
        rel = [along_edges(poses[c : c + 1, :]) for c in range(6)]
        jac_u, jac_v, scaled_u, scaled_v, resid_u, resid_v, cross, curve, depth_grad = edge_terms(
            rel, depth, flow_u, flow_v, weight_u, weight_v, col, row
        )
        frame_curve = jnp.sum(curve, axis=0, keepdims=True)
        frame_grad = jnp.sum(depth_grad, axis=0, keepdims=True)
        inv_damped = 1.0 / ((1.0 + DEPTH_DAMPING) * frame_curve + DEPTH_FLOOR)
        lead = jnp.concatenate([jnp.concatenate(scaled_u, axis=0), jnp.concatenate(scaled_v, axis=0)], axis=1)
        pad = jnp.zeros((72, 2 * SLICE), F32)
        trail = jnp.concatenate(
            [
                jnp.concatenate([jnp.concatenate(jac_u, axis=0), jnp.concatenate(jac_v, axis=0)], axis=1),
                jnp.concatenate([resid_u, resid_v], axis=1),
                pad,
            ],
            axis=0,
        )
        hess = dot_nt(lead, trail, HIGHEST)
        stack = jnp.concatenate(cross, axis=0)
        right = jnp.concatenate(
            [stack, jnp.broadcast_to(frame_grad, (8, SLICE)) * (sub_row(8, SLICE) == 0).astype(F32), pad[:, :SLICE]],
            axis=0,
        )
        schur = dot_nt(stack * inv_damped, right, HIGHEST)
        small = jnp.where(same_edge, hess, 0.0) - schur
        for c in range(6):
            k_s[it, c] = small[8 * c : 8 * c + 8]
        for c in range(6, 8):
            k_s[it, c] = jnp.zeros((8, 128), F32)
        copies = exchange(lambda peer: k_s.at[it, peer], k_r.at[it, me_e], k_send.at[it], k_recv.at[it])
        k_r[it, me_e] = k_s[it, me_e]
        for copy in copies:
            copy.wait()
        total = k_r[it, 0]
        for e in range(1, EDGES):
            total = total + k_r[it, e]
        f_s[it] = total
        f_r[it, me_f] = total

        copies = []
        for d, (dx, dz) in enumerate(FAR_FRAMES):
            peer = lax.rem(me_f // ZS + dx, XS) * ZS + lax.rem(me_f + dz, ZS)
            copy = pltpu.make_async_remote_copy(
                src_ref=f_s.at[it],
                dst_ref=f_r.at[it, me_f],
                send_sem=f_send.at[it, d],
                recv_sem=f_recv.at[it, d],
                device_id={"frames": peer},
                device_id_type=MESH,
            )
            copy.start()
            copies.append(copy)
        for copy in copies:
            copy.wait_recv()
        for copy in copies:
            copy.wait_send()

        blocks = f_r[it].reshape(256, 128)
        left_sum = jnp.zeros((256, 128), F32)
        right_sum = jnp.zeros((256, 128), F32)
        for k in range(EDGES):
            rep = rep_s[k]
            left_sum = left_sum + jnp.take_along_axis(blocks, (lane256 // 32) * 8 + k, axis=1) * rep
            right_sum = right_sum + jnp.take_along_axis(blocks, (lane256 // 32) % 2 * 8 + 32 + k, axis=1) * rep
        rhs = jnp.sum(jnp.where((lane256 >= 48) & (lane256 < 56), blocks, 0.0), axis=1, keepdims=True)
        right_sum = jnp.where(lane256 < 64, right_sum, jnp.where(lane256 == 64, rhs, 0.0))
        row_s[it] = jnp.concatenate(
            [
                jnp.dot(sgnt_s[...], left_sum, precision=HIGHEST, preferred_element_type=F32),
                jnp.dot(sgnt_s[...], right_sum, precision=HIGHEST, preferred_element_type=F32),
            ],
            axis=1,
        )
        copies = exchange(lambda peer: row_s.at[it], row_r.at[it, me_e], r_send.at[it], r_recv.at[it])
        row_r[it, me_e] = row_s[it]
        for copy in copies:
            copy.wait()

        for c in range(6):
            for t in range(2):
                v = row_r[it, c, :, 128 * t : 128 * t + 128]
                diag = lane32 + 128 * t == sub32 + 32 * c
                mat[32 * c : 32 * c + 32, 128 * t : 128 * t + 128] = v + jnp.where(
                    diag, POSE_DAMPING * v + POSE_FLOOR, 0.0
                )

        rows = stack_rows(pivot_rows([mat[0:8, 0:128], mat[0:8, 128:256]], mat[0:8, 0:128], 0))
        rows = eliminate(mat, 0, 9, rows)
        eliminate(mat, 9, UNK // 8, rows[:1])

        steps = []
        for c in range(6):
            v = jnp.broadcast_to(mat[32 * c : 32 * c + 32, 0:1], (NF, 128))
            steps.append(jnp.sum(jnp.where(lane32 == sub32, v, 0.0), axis=0, keepdims=True))
        along = jnp.zeros((8, SLICE), F32)
        for c in range(6):
            along = along + along_edges(steps[c]) * cross[c]
        along = jnp.sum(along, axis=0, keepdims=True)
        poses = poses + jnp.concatenate(steps + [jnp.zeros((2, 128), F32)], axis=0)
        depth = depth + (frame_grad - along) * inv_damped

    mine = jnp.sum(jnp.where(lane8 == me_f, poses, 0.0), axis=1, keepdims=True)
    pose_out[...] = jnp.sum(jnp.where(lane8 == sub_row(8, 128), mine, 0.0), axis=0, keepdims=True)[:, :6]
    d_s[...] = depth
    place = depth_out.at[:, pl.ds(pl.multiple_of(me_e * SLICE, SLICE), SLICE)]
    copies = exchange(lambda peer: d_s, place, d_send, d_recv)
    place[...] = depth
    for copy in copies:
        copy.wait()


def sub_row(rows, cols):
    return lax.broadcasted_iota(jnp.int32, (rows, cols), 0)


def gauss_newton(heads, inv_depth, table):
    vmem = pl.BlockSpec(memory_space=pltpu.VMEM)
    dma = pltpu.SemaphoreType.DMA
    pose_out, depth_out = pl.pallas_call(
        gn_kernel,
        out_shape=(
            jax.ShapeDtypeStruct((1, 6), F32),
            jax.ShapeDtypeStruct((1, PIX), F32),
        ),
        in_specs=[pl.BlockSpec(memory_space=pl.ANY), vmem, vmem],
        out_specs=(vmem, vmem),
        scratch_shapes=[
            pltpu.VMEM((EDGES, 8, SLICE), F32),
            pltpu.VMEM((ITERS, 8, 8, 128), F32),
            pltpu.VMEM((ITERS, 8, 8, 128), F32),
            pltpu.VMEM((ITERS, 8, 128), F32),
            pltpu.VMEM((ITERS, NF, 8, 128), F32),
            pltpu.VMEM((ITERS, NF, 256), F32),
            pltpu.VMEM((ITERS, EDGES, NF, 256), F32),
            pltpu.VMEM((1, SLICE), F32),
            pltpu.VMEM((EDGES, 256, 128), F32),
            pltpu.VMEM((NF, 256), F32),
            pltpu.VMEM((UNK, 256), F32),
            dma((EDGES,)),
            dma((EDGES,)),
            dma((ITERS, EDGES)),
            dma((ITERS, EDGES)),
            dma((ITERS, NF)),
            dma((ITERS, NF)),
            dma((ITERS, EDGES)),
            dma((ITERS, EDGES)),
            dma((EDGES,)),
            dma((EDGES,)),
            dma(()),
        ],
        compiler_params=pltpu.CompilerParams(
            vmem_limit_bytes=60 * 1024 * 1024, collective_id=1, has_side_effects=True
        ),
        name="gauss_newton",
    )(heads, table, inv_depth)
    return pose_out.T, depth_out


def per_device(fmap, context, poses, inv_depth, targets, w_corr, w_gates, w_cand, w_head):
    target, table = gather(fmap[0], poses, targets)
    hidden, heads = update(fmap[0], target, context[0], w_corr, w_gates, w_cand, w_head)
    new_poses, new_depth = gauss_newton(heads, inv_depth, table)
    return new_poses, new_depth, hidden[None]


def solution(mesh):
    return jax.shard_map(
        per_device,
        mesh=mesh,
        in_specs=(
            P("frames", None, None),
            P("frames", None, None),
            P(None, "frames"),
            P("frames", None),
            P(("frames", "edges")),
            P(),
            P(),
            P(),
            P(),
        ),
        out_specs=(P(None, "frames"), P("frames", None), P(("frames", "edges"), None, None)),
        check_vma=False,
    )
```
